32 devices in a mesh: row: 4 (over y, x), col: 8 (over z, core).
Axes of the slice: x: 2, y: 2, z: 4, core: 2. Of those that a mesh axis runs over, the one named last changes fastest.
Arguments:
- trailing: bfloat16 [16384, 16384], P('row', 'col'), may hold values from -0.0625 to 0.0625
- panel_vectors: bfloat16 [16384, 512], P(('row', 'col')), may hold values from -6 to 6
Outputs:
- sym_product: float32 [16384, 512], P(('row', 'col'))
The draws below stay inside these ranges and needn't reach their ends.
All inputs are finite; a program needn't handle non-finite values.
Results may differ from the reference program's by a relative error of at most 0.0003.
Values may be sent and summed in bfloat16 or wider, within the bound.
No kernel may reach another device: no remote copies, remote signals or barrier semaphores. Data moves between devices by JAX's collectives and lax.ppermute only.
A program may use at most 128 MiB of HBM per device.

```python
import jax
import jax.numpy as jnp
from jax import lax

BLK = 2048
PANEL = 512
ORDER = 16384


def spiked(result, own_key, source, target, shards_of, factor):
    owner, partner = [(jnp.arange(result.shape[dim]) // (result.shape[dim] // shards_of)).reshape([-1 if axis == dim else 1 for axis in range(result.ndim)]) for dim in (source, target)]
    chosen = jax.random.permutation(own_key, shards_of)[partner]
    strong = (owner == chosen) | (owner == (partner + shards_of // 2) % shards_of)
    return jnp.where(strong, factor * result, result)


def block_levels(stream_key, dims, cuts, least, largest):
    def one(axis_at, blocks):
        heights = jax.random.uniform(jax.random.fold_in(jax.random.fold_in(stream_key, 6), axis_at), (blocks,), jnp.float32, least / len(cuts), largest / len(cuts))
        return jnp.repeat(jnp.exp(heights), dims[axis_at] // blocks).reshape((-1,) + (1,) * (len(dims) - axis_at - 1))

    level = one(*cuts[0])
    for cut in cuts[1:]:
        level = level * one(*cut)
    return level


def gaussian(stream_key, extent, spread, limit, pieces=(), kind=jnp.bfloat16):
    values = jax.random.normal(stream_key, extent, jnp.float32) * spread
    if len(pieces) > 0:
        values = block_levels(stream_key, extent, pieces, -0.22, 0.18) * values
    return jnp.clip(values, min=-limit, max=limit).astype(kind)


def noise_with(key, dims, width, bound, cuts, heavy, kind=jnp.bfloat16):
    drawn = width * jax.random.normal(key, dims, jnp.float32)
    if cuts:
        drawn = drawn * block_levels(key, dims, cuts, -0.22, 0.18)
    return jnp.clip(spiked(drawn, jax.random.fold_in(key, 3), *heavy), -bound, bound).astype(kind)


def setup_inputs(seed: int = 0) -> dict:
    key_list = jax.random.split(jax.random.key(seed), 3)
    trailing = noise_with(key_list[0], (ORDER, ORDER), ORDER ** -0.5, 0.0625, ((0, 4), (1, 8)), (1, 0, 8, 2.0))
    panel_vectors = gaussian(key_list[1], (ORDER, PANEL), 1.0, 6.0, ((0, 32),))
    return {"trailing": trailing, "panel_vectors": panel_vectors}


def reference(trailing, panel_vectors):
    order = trailing.shape[0]
    strips = order // BLK
    empty = jnp.zeros((), trailing.dtype)

    def advance(index, carry):
        direct, mirrored = carry
        first_row = (index * BLK).astype(jnp.int32)
        strip_rows = lax.dynamic_slice_in_dim(trailing, first_row, BLK, 0)
        row_ids = first_row + lax.iota(jnp.int32, BLK)
        col_ids = lax.iota(jnp.int32, order)
        lower_part = jnp.where(row_ids[:, None] >= col_ids[None, :], strip_rows, empty)
        strict_part = jnp.where(row_ids[:, None] > col_ids[None, :], strip_rows, empty)
        rows_out = jnp.dot(lower_part, panel_vectors, preferred_element_type=jnp.float32)
        direct = lax.dynamic_update_slice_in_dim(direct, rows_out, first_row, 0)
        panel_strip = lax.dynamic_slice_in_dim(panel_vectors, first_row, BLK, 0)
        mirrored = mirrored + jnp.dot(strict_part.T, panel_strip, preferred_element_type=jnp.float32)
        return direct, mirrored

    start_direct = jnp.zeros((order, PANEL), jnp.float32)
    start_mirror = jnp.zeros((order, PANEL), jnp.float32)
    direct, mirrored = lax.fori_loop(0, strips, advance, (start_direct, start_mirror))
    return direct + mirrored
```

```python
import functools

import jax
import jax.numpy as jnp
from jax import lax
from jax.experimental import pallas as pl
from jax.experimental.pallas import tpu as pltpu
from jax.sharding import PartitionSpec as P

TOP = 40000.0
TAIL = 16
VMEM = 12 * 2**20


def scale_for(largest):
    scale = TOP / jnp.maximum(largest, 1e-30)
    return scale.astype(jnp.bfloat16).astype(jnp.float32)


def encode(values, scale):
    x = values * scale
    x2 = x * x
    x4 = x2 * x2
    return (x * jnp.abs(x) * x2 * x4).astype(jnp.bfloat16)


def decode(coded, scale):
    y = coded.astype(jnp.float32)
    back = jnp.where(scale > 0, 1.0 / scale, 0.0)
    return y * jnp.exp2(-0.875 * jnp.log2(jnp.maximum(jnp.abs(y), 2.0**-126))) * back


def scale_of(message, rows, block):
    return message[pl.ds(rows + block * TAIL, TAIL), :][0:1, 0:1].astype(jnp.float32)


def put_scale(message, rows, block, scale):
    spread = jnp.full((TAIL, message.shape[1]), scale, jnp.float32).astype(jnp.bfloat16)
    message[pl.ds(rows + block * TAIL, TAIL), :] = spread


def local(kernel, out_shape, name, *operands, after=(), cost=None, **options):
    count, skipped = len(operands), len(after)

    def body(*refs):
        kernel(*refs[:count], *refs[count + skipped :])

    return pl.pallas_call(
        body,
        out_shape=out_shape,
        in_specs=[pl.BlockSpec(memory_space=pltpu.SMEM)]
        + [pl.BlockSpec(memory_space=pltpu.VMEM)] * (count - 1)
        + [pl.BlockSpec(memory_space=pl.ANY)] * skipped,
        out_specs=jax.tree.map(lambda _: pl.BlockSpec(memory_space=pltpu.VMEM), out_shape),
        compiler_params=pltpu.CompilerParams(vmem_limit_bytes=VMEM),
        cost_estimate=cost,
        name=name,
        **options,
    )(*operands, *after)


def load_kernel(ids, a_ref, out_ref, sem):
    height, cols = a_ref.shape
    block = cols // 4

    @pl.when(ids[1] <= ids[0])
    def _():
        copy = pltpu.make_async_copy(a_ref, out_ref, sem)
        copy.start()
        copy.wait()

    for part in range(4):
        here = pl.ds(part * block, block)

        @pl.when(ids[1] == ids[0])
        def _():
            @pl.loop(0, height // block)
            def _(at):
                first = ids[3] + at * block
                rows = pl.ds(pl.multiple_of(at * block, block), block)

                @pl.when(first < part * block)
                def _():
                    out_ref[rows, here] = jnp.zeros((block, block), out_ref.dtype)

                @pl.when(first == part * block)
                def _():
                    tile = out_ref[rows, here]
                    kept = lax.broadcasted_iota(jnp.int32, tile.shape, 0) >= lax.broadcasted_iota(
                        jnp.int32, tile.shape, 1
                    )
                    out_ref[rows, here] = jnp.where(kept, tile, jnp.zeros_like(tile))


def load(ids, trailing):
    return pl.pallas_call(
        load_kernel,
        out_shape=jax.ShapeDtypeStruct(trailing.shape, trailing.dtype),
        in_specs=[pl.BlockSpec(memory_space=pltpu.SMEM), pl.BlockSpec(memory_space=pl.ANY)],
        out_specs=pl.BlockSpec(memory_space=pltpu.VMEM),
        scratch_shapes=[pltpu.SemaphoreType.DMA],
        compiler_params=pltpu.CompilerParams(vmem_limit_bytes=VMEM),
        cost_estimate=pl.CostEstimate(flops=0, bytes_accessed=trailing.size * 4, transcendentals=0),
        name="load",
    )(ids, trailing)


def line_kernel(ids, *refs):
    *came, out_ref = refs
    height = came[0].shape[0]
    for step, piece in enumerate(came):
        chip = lax.rem(ids[1] + len(came) - step, len(came))
        out_ref[pl.ds(pl.multiple_of(chip * height, height), height), :] = piece[...]


def line(ids, came, after):
    height, width = came[0].shape
    out_shape = jax.ShapeDtypeStruct((height * len(came), width), came[0].dtype)
    return local(line_kernel, out_shape, "line", ids, *came, after=after)


def half_kernel(height, ids, mine, other, out_ref):
    count = out_ref.shape[0] // height
    for at in range(count // 2):
        chip = ids[2] * (count // 2) + at
        rows = pl.ds(pl.multiple_of(chip * height, height), height)
        for core, ref in ((ids[2], mine), (1 - ids[2], other)):
            out_ref[pl.ds(pl.multiple_of((2 * at + core) * height, height), height), :] = ref[rows, :]


def half(ids, mine, other, height):
    out_shape = jax.ShapeDtypeStruct(mine.shape, mine.dtype)
    return local(functools.partial(half_kernel, height), out_shape, "half", ids, mine, other)


def mirrored_kernel(piece, ids, a_ref, mine, other, m_ref, msg_ref, turned):
    height, cols = a_ref.shape
    block = cols // 4
    used = ids[1] <= ids[0]

    @pl.loop(0, height // piece // 2)
    def _(at):
        rows = pl.ds(pl.multiple_of(at * piece, piece), piece)
        for core, ref in ((ids[2], mine), (1 - ids[2], other)):
            turned[:, pl.ds(pl.multiple_of((2 * at + core) * piece, piece), piece)] = ref[rows, :].T

    @pl.loop(0, 4)
    def _(part):
        here = pl.ds(pl.multiple_of(part * block, block), block)

        @pl.when(used)
        def _():
            m_ref[here, :] = jnp.dot(turned[...], a_ref[:, here], preferred_element_type=jnp.float32).T

        @pl.when(jnp.logical_not(used))
        def _():
            m_ref[here, :] = jnp.zeros((block, m_ref.shape[1]), jnp.float32)

        @pl.when(ids[1] == ids[0])
        def _():
            rows = pl.ds(pl.multiple_of(part * block - ids[3], block), block)
            tile = a_ref[rows, here]
            kept = lax.broadcasted_iota(jnp.int32, tile.shape, 0) == lax.broadcasted_iota(jnp.int32, tile.shape, 1)
            tile = jnp.where(kept, tile, jnp.zeros_like(tile))
            m_ref[here, :] -= jnp.dot(turned[:, rows], tile, preferred_element_type=jnp.float32).T

        total = m_ref[here, :]
        scale = scale_for(jnp.max(jnp.abs(total), keepdims=True))
        msg_ref[here, :] = encode(total, scale)
        put_scale(msg_ref, cols, part, scale)


def mirrored_product(ids, trailing, mine, other, piece, after):
    rows, cols = trailing.shape
    width = mine.shape[1]
    out_shape = [
        jax.ShapeDtypeStruct((cols, width), jnp.float32),
        jax.ShapeDtypeStruct((cols + 4 * TAIL, width), jnp.bfloat16),
    ]
    cost = pl.CostEstimate(flops=4 * rows * cols * width, bytes_accessed=rows * cols * 2, transcendentals=0)
    return local(
        functools.partial(mirrored_kernel, piece), out_shape, "mirrored_product",
        ids, trailing, mine, other, after=after, cost=cost,
        scratch_shapes=[pltpu.VMEM((width, rows), jnp.bfloat16)],
    )


def relay_kernel(ids, m_ref, *refs):
    *messages, msg_ref = refs
    rows, width = m_ref.shape
    height = rows // 4

    @pl.loop(0, 4)
    def _(part):
        at = pl.ds(pl.multiple_of(part * height, height), height)
        total = m_ref[at, :]
        for message in messages:
            total += decode(message[at, :], scale_of(message, rows, part))
        scale = scale_for(jnp.max(jnp.abs(total), keepdims=True))
        msg_ref[at, :] = encode(total, scale)
        put_scale(msg_ref, rows, part, scale)


def relay(ids, partial, messages, after):
    cost = pl.CostEstimate(flops=0, bytes_accessed=partial.size * 8, transcendentals=0)
    out_shape = jax.ShapeDtypeStruct(messages[0].shape, messages[0].dtype)
    return local(relay_kernel, out_shape, "relay", ids, partial, *messages, after=after, cost=cost)


def direct_kernel(places, ids, a_ref, m_ref, *refs):
    panels = refs[:places]
    messages = refs[places:-4]
    *outs, panel, sem = refs[-4:]
    height = outs[0].shape[0] // places
    cols = a_ref.shape[1]
    blocks = cols // height
    core = ids[2]
    used = ids[1] <= ids[0]

    for place in range(places):

        @pl.when(ids[4] == place)
        def _():
            copy = pltpu.make_async_copy(panels[place], panel, sem)
            copy.start()
            copy.wait()

    @pl.loop(0, outs[0].shape[0] // height)
    def _(piece):
        to = pl.ds(pl.multiple_of(piece * height, height), height)
        for other, out_ref in enumerate(outs):
            step = 2 * piece + (core ^ other)
            rows = pl.ds(pl.multiple_of(step * height, height), height)

            @pl.when(used)
            def _():
                out_ref[to, :] = jnp.dot(a_ref[rows, :], panel[...], preferred_element_type=jnp.float32)

            inside = step - core * blocks

            @pl.when((ids[1] == ids[0]) & (inside >= 0) & (inside < blocks))
            def _():
                block = jnp.clip(inside, 0, blocks - 1)
                at = pl.ds(pl.multiple_of(block * height, height), height)
                total = out_ref[to, :] + m_ref[at, :]
                for message in messages:
                    total += decode(message[at, :], scale_of(message, cols, lax.div(block * 4, blocks)))
                out_ref[to, :] = total


def direct_product(ids, trailing, partial, panels, messages, height, after):
    rows, cols = trailing.shape
    width = partial.shape[1]
    out_shape = [jax.ShapeDtypeStruct((rows // 2, width), jnp.float32)] * 2
    cost = pl.CostEstimate(flops=4 * rows * cols * width, bytes_accessed=rows * cols * 2, transcendentals=0)
    return local(
        functools.partial(direct_kernel, len(panels)), out_shape, "direct_product",
        ids, trailing, partial, *panels, *messages, after=after, cost=cost,
        scratch_shapes=[pltpu.VMEM((cols, width), jnp.bfloat16), pltpu.SemaphoreType.DMA],
    )


def pack_kernel(ids, a_ref, b_ref, own_ref, *msgs):
    height = own_ref.shape[0]
    chips = 1 + len(msgs)
    for step in range(chips):
        rows = pl.ds(pl.multiple_of(lax.rem(ids[1] + step, chips) * height, height), height)
        total = a_ref[rows, :] + b_ref[rows, :]
        if step == 0:
            own_ref[...] = jnp.where(ids[1] <= ids[0], total, 0.0)
        else:
            msg = msgs[step - 1]
            scale = scale_for(jnp.max(jnp.abs(total), keepdims=True))
            msg[pl.ds(0, height), :] = encode(total, scale)
            put_scale(msg, height, 0, scale)


def pack(ids, mine, theirs, chips, after):
    rows, width = mine.shape
    height = rows // chips
    out_shape = [
        jax.ShapeDtypeStruct((height, width), jnp.float32),
        *[jax.ShapeDtypeStruct((height + TAIL, width), jnp.bfloat16)] * (chips - 1),
    ]
    return local(pack_kernel, out_shape, "pack", ids, mine, theirs, after=after)


def finish_kernel(ids, before, own, *refs):
    *messages, out_ref = refs
    height, width = own.shape
    total = own[...]
    for message in messages:
        total += decode(message[pl.ds(0, height), :], scale_of(message, height, 0))
    done = out_ref.shape[1] - width
    if done:
        out_ref[:, pl.ds(0, done)] = before[:, pl.ds(0, done)]
    out_ref[:, pl.ds(done, width)] = total


def finish(ids, before, arrays, after):
    height, width = arrays[0].shape
    done = 0 if before is None else before.shape[1]
    out_shape = jax.ShapeDtypeStruct((height, done + width), jnp.float32)
    return local(finish_kernel, out_shape, "finish", ids, arrays[0] if before is None else before, *arrays, after=after)


def shards(trailing, panel_vectors):
    rows_here, cols_here = trailing.shape
    piece = panel_vectors.shape[0]
    count = lax.axis_size("row")
    devices_along = lax.axis_size("col")
    chips = devices_along // 2
    bits = count.bit_length() - 1
    row, col = lax.axis_index("row"), lax.axis_index("col")
    chip, core = col // 2, col % 2

    def at(row, chip, core):
        return (row * chips + chip) * 2 + core

    def turned(place, core):
        if core == 0:
            return place
        return sum(((place >> b) & 1) << (bits - 1 - b) for b in range(bits))

    def send(x, pairs):
        return lax.ppermute(x, ("row", "col"), [(at(*s), at(*d)) for s, d in pairs])

    offset = row ^ chip
    reverse = sum(((offset >> b) & 1) << (bits - 1 - b) for b in range(bits))
    place = jnp.where(core == 0, offset, reverse)
    ids = jnp.stack([row, chip, core, row * rows_here - col * cols_here, place]).astype(jnp.int32)

    def needed(chip, core, place, bit):
        rest = range(0, count, 2 ** (bit + 1))
        return any(chip ^ turned(place | r, core) > chip for r in rest)

    everyone = [(k, c) for k in range(chips) for c in range(2)]

    width = panel_vectors.shape[1] // 2
    active = [(r, k, c) for r in range(count) for k in range(r + 1) for c in range(2)]

    def spread(place, source):
        bit = place.bit_length() - 1
        before = place - (1 << bit)
        pairs = [
            ((k ^ turned(before, c), k, c), (k ^ turned(place, c), k, c))
            for k, c in everyone
            if needed(k, c, place, bit)
        ]
        return send(source, pairs)

    def collect(bit, message):
        pairs = [
            ((k ^ turned(p, c), k, c), (k ^ turned(p - (1 << bit), c), k, c))
            for k, c in everyone
            for p in range(1 << bit, 2 << bit)
            if needed(k, c, p, bit)
        ]
        return send(message, pairs)

    matrix = load(ids, trailing)

    def gather(block):
        came = [block]
        for step in range(1, chips):
            pairs = [
                ((r, k, c), (r, (k + step) % chips, c))
                for r in range(count)
                for k in range(chips)
                for c in range(2)
                if (k + step) % chips <= r
            ]
            came.append(send(block, pairs))
        return came

    swap = [((r, k, c), (r, k, 1 - c)) for r, k, c in active]

    def opening(came, beside):
        mine = line(ids, came, [])
        other = send(mine, swap)
        panels = [half(ids, mine, other, piece)]
        panels.append(spread(1, panels[0]))
        partial, message = mirrored_product(ids, matrix, mine, other, piece, [panels[0]])
        message, panels[1], *beside = lax.optimization_barrier((message, panels[1], *beside))
        messages = [collect(bits - 1, message)]
        return panels, partial, messages, message, beside

    def relaying(panels, partial, messages, after):
        panels[0], panels[1] = lax.optimization_barrier((panels[0], panels[1]))
        for place in range(2, count):
            panels.append(spread(place, panels[place - (1 << (place.bit_length() - 1))]))
        for bit in reversed(range(bits - 1)):
            message = relay(ids, partial, messages, [panels[1], *after])
            message, *panels[2:] = lax.optimization_barrier((message, *panels[2:]))
            messages.append(collect(bit, message))
        return message

    def product(panels, partial, messages, after):
        keep, give = direct_product(ids, matrix, partial, panels, messages, piece, after)
        got = send(give, swap)
        return keep, got

    def deliver(keep, got, after):
        own, *out = pack(ids, keep, got, chips, after)
        arrays = [own]
        for step, x in enumerate(out, 1):
            arrays.append(send(x, [((r, k, c), (r, (k + step) % chips, c)) for r, k, c in active]))
        return arrays

    came_a = gather(panel_vectors[:, :width])
    came_a, block_b, matrix = lax.optimization_barrier((came_a, panel_vectors[:, width:], matrix))
    came_b = gather(block_b)
    first = opening(came_a, came_b[1:-1])
    came_b[1:-1] = first[4]
    relayed = relaying(*first[:3], [came_b[-1]])
    second = opening(came_b, [relayed])
    keep_a, got_a = product(*first[:3], [second[3], second[0][1]])
    relayed = relaying(*second[:3], [keep_a])
    arrays_a = deliver(keep_a, got_a, [relayed])
    keep_b, give_b = direct_product(ids, matrix, second[1], second[0], second[2], piece, [arrays_a[0]])
    give_b, *arrays_a[1:-1] = lax.optimization_barrier((give_b, *arrays_a[1:-1]))
    arrays_b = deliver(keep_b, send(give_b, swap), [])
    result = finish(ids, None, arrays_a, [arrays_b[0]])
    return finish(ids, result, arrays_b, [])


def solution(mesh):
    in_specs = (P("row", "col"), P(("row", "col"), None))
    out_specs = P(("row", "col"), None)
    return jax.shard_map(shards, mesh=mesh, in_specs=in_specs, out_specs=out_specs, check_vma=False)
```

```python
import functools

import jax
import jax.numpy as jnp
from jax import lax
from jax.experimental import pallas as pl
from jax.experimental.pallas import tpu as pltpu
from jax.sharding import PartitionSpec as P

TOP = 40000.0
TAIL = 16
VMEM = 6 * 2**20


def scale_for(largest):
    scale = TOP / jnp.maximum(largest, 1e-30)
    return scale.astype(jnp.bfloat16).astype(jnp.float32)


def encode(values, scale):
    x = values * scale
    x2 = x * x
    x4 = x2 * x2
    return (x * jnp.abs(x) * x2 * x4).astype(jnp.bfloat16)


def decode(coded, scale):
    y = coded.astype(jnp.float32)
    back = jnp.where(scale > 0, 1.0 / scale, 0.0)
    return y * jnp.exp2(-0.875 * jnp.log2(jnp.maximum(jnp.abs(y), 2.0**-126))) * back


def scale_of(message, rows, block):
    return message[pl.ds(rows + block * TAIL, TAIL), :][0:1, 0:1].astype(jnp.float32)


def put_scale(message, rows, block, scale):
    spread = jnp.full((TAIL, message.shape[1]), scale, jnp.float32).astype(jnp.bfloat16)
    message[pl.ds(rows + block * TAIL, TAIL), :] = spread


def local(kernel, out_shape, name, *operands, after=(), **options):
    count, skipped = len(operands), len(after)

    def body(*refs):
        kernel(*refs[:count], *refs[count + skipped :])

    return pl.pallas_call(
        body,
        out_shape=out_shape,
        in_specs=[pl.BlockSpec(memory_space=pltpu.SMEM)]
        + [pl.BlockSpec(memory_space=pltpu.VMEM)] * (count - 1)
        + [pl.BlockSpec(memory_space=pl.ANY)] * skipped,
        out_specs=jax.tree.map(lambda _: pl.BlockSpec(memory_space=pltpu.VMEM), out_shape),
        compiler_params=pltpu.CompilerParams(vmem_limit_bytes=VMEM),
        name=name,
        **options,
    )(*operands, *after)


def load_kernel(ids, a_ref, out_ref, diagonal, sem):
    height, cols = a_ref.shape
    block = cols // 4
    diagonal[...] = jnp.zeros_like(diagonal)

    @pl.when(ids[1] <= ids[0])
    def _():
        copy = pltpu.make_async_copy(a_ref, out_ref, sem)
        copy.start()
        copy.wait()

    for part in range(4):
        here = pl.ds(part * block, block)

        @pl.when(ids[1] == ids[0])
        def _():
            @pl.loop(0, height // block)
            def _(at):
                first = ids[3] + at * block
                rows = pl.ds(pl.multiple_of(at * block, block), block)

                @pl.when(first < part * block)
                def _():
                    out_ref[rows, here] = jnp.zeros((block, block), out_ref.dtype)

                @pl.when(first == part * block)
                def _():
                    tile = out_ref[rows, here]
                    empty = jnp.zeros_like(tile)
                    row = lax.broadcasted_iota(jnp.int32, tile.shape, 0)
                    col = lax.broadcasted_iota(jnp.int32, tile.shape, 1)
                    out_ref[rows, here] = jnp.where(row >= col, tile, empty)
                    on = jnp.where(row == col, tile, empty).astype(jnp.float32)
                    diagonal[:, here] = jnp.broadcast_to(jnp.sum(on, axis=0, keepdims=True), (8, block))


def load(ids, trailing):
    return pl.pallas_call(
        load_kernel,
        out_shape=[
            jax.ShapeDtypeStruct(trailing.shape, trailing.dtype),
            jax.ShapeDtypeStruct((8, trailing.shape[1]), jnp.float32),
        ],
        in_specs=[pl.BlockSpec(memory_space=pltpu.SMEM), pl.BlockSpec(memory_space=pltpu.HBM)],
        out_specs=[pl.BlockSpec(memory_space=pltpu.VMEM)] * 2,
        scratch_shapes=[pltpu.SemaphoreType.DMA],
        compiler_params=pltpu.CompilerParams(vmem_limit_bytes=VMEM),
        name="load",
    )(ids, trailing)


def line_kernel(places, ids, *refs):
    *came, out_ref = refs
    height = came[0].shape[0]
    for place, piece in zip(places, came):
        chip, there = place(ids[1])

        @pl.when(there)
        def _():
            out_ref[pl.ds(pl.multiple_of(chip * height, height), height), :] = piece[...]


def line(ids, came, places, after):
    height, width = came[0].shape
    chips = 4 if len(came) == 5 else len(came)
    out_shape = jax.ShapeDtypeStruct((height * chips, width), came[0].dtype)
    return local(functools.partial(line_kernel, places), out_shape, "line", ids, *came, after=after)


def half_kernel(height, ids, mine, other, out_ref):
    count = out_ref.shape[0] // height
    for at in range(count // 2):
        chip = ids[2] * (count // 2) + at
        here = pl.ds(pl.multiple_of(chip * height, height), height)
        for core, ref in ((ids[2], mine), (1 - ids[2], other)):
            out_ref[pl.ds(pl.multiple_of((2 * at + core) * height, height), height), :] = ref[here, :]


def half(ids, mine, other, height):
    out_shape = jax.ShapeDtypeStruct(mine.shape, mine.dtype)
    return local(functools.partial(half_kernel, height), out_shape, "half", ids, mine, other)


def mirrored_kernel(piece, ids, a_ref, diagonal, mine, other, m_ref, msg_ref, turned):
    height, cols = a_ref.shape
    block = cols // 4
    used = ids[1] <= ids[0]

    @pl.loop(0, height // piece // 2)
    def _(at):
        rows = pl.ds(pl.multiple_of(at * piece, piece), piece)
        for core, ref in ((ids[2], mine), (1 - ids[2], other)):
            turned[:, pl.ds(pl.multiple_of((2 * at + core) * piece, piece), piece)] = ref[rows, :].T

    @pl.loop(0, 4)
    def _(part):
        here = pl.ds(pl.multiple_of(part * block, block), block)

        @pl.when(used)
        def _():
            m_ref[here, :] = jnp.dot(turned[...], a_ref[:, here], preferred_element_type=jnp.float32).T

        @pl.when(jnp.logical_not(used))
        def _():
            m_ref[here, :] = jnp.zeros((block, m_ref.shape[1]), jnp.float32)

        @pl.when(ids[1] == ids[0])
        def _():
            rows = pl.ds(pl.multiple_of(part * block - ids[3], block), block)
            m_ref[here, :] -= (turned[:, rows].astype(jnp.float32) * diagonal[0:1, here]).T

        total = m_ref[here, :]
        scale = scale_for(jnp.max(jnp.abs(total), keepdims=True))
        msg_ref[here, :] = encode(total, scale)
        put_scale(msg_ref, cols, part, scale)


def mirrored_product(ids, matrix, diagonal, mine, other, piece, after):
    rows, cols = matrix.shape
    width = mine.shape[1]
    out_shape = [
        jax.ShapeDtypeStruct((cols, width), jnp.float32),
        jax.ShapeDtypeStruct((cols + 4 * TAIL, width), jnp.bfloat16),
    ]
    return local(
        functools.partial(mirrored_kernel, piece), out_shape, "mirrored_product",
        ids, matrix, diagonal, mine, other, after=after,
        scratch_shapes=[pltpu.VMEM((width, rows), jnp.bfloat16)],
    )


def relay_kernel(ids, m_ref, in_ref, sum_ref, msg_ref):
    rows, width = m_ref.shape
    height = rows // 4

    @pl.loop(0, 4)
    def _(part):
        at = pl.ds(pl.multiple_of(part * height, height), height)
        total = m_ref[at, :] + decode(in_ref[at, :], scale_of(in_ref, rows, part))
        scale = scale_for(jnp.max(jnp.abs(total), keepdims=True))
        sum_ref[at, :] = total
        msg_ref[at, :] = encode(total, scale)
        put_scale(msg_ref, rows, part, scale)


def relay(ids, partial, message, after):
    out_shape = [jax.ShapeDtypeStruct(x.shape, x.dtype) for x in (partial, message)]
    return local(relay_kernel, out_shape, "relay", ids, partial, message, after=after)


def pick(ids, panels, panel, sem):
    for place, ref in enumerate(panels):

        @pl.when(ids[4] == place)
        def _():
            copy = pltpu.make_async_copy(ref, panel, sem)
            copy.start()
            copy.wait()


def give_kernel(ids, a_ref, *refs):
    *panels, give_ref, give_too, panel, sem = refs
    pick(ids, panels, panel, sem)
    rows_kernel(ids, a_ref, panel, give_ref, core=1 - ids[2], of=2)
    rows_kernel(ids, a_ref, panel, give_too, core=1 - ids[2], at=1, of=2)


def direct_kernel(ids, a_ref, *refs):
    *panels, keep_ref, give_ref, give_too, panel, sem = refs
    pick(ids, panels, panel, sem)
    rows_kernel(ids, a_ref, panel, give_ref, core=1 - ids[2], of=2)
    rows_kernel(ids, a_ref, panel, give_too, core=1 - ids[2], at=1, of=2)
    rows_kernel(ids, a_ref, panel, keep_ref)


def rows_kernel(ids, a_ref, panel, out_ref, core=None, at=0, of=1):
    core = ids[2] if core is None else core
    rows = out_ref.shape[0]
    height = rows * of // 4
    skip = at * rows

    @pl.when(ids[1] <= ids[0])
    def _():
        @pl.loop(0, 4 // of)
        def _(part):
            at = pl.ds(pl.multiple_of(core * rows * of + skip + part * height, height), height)
            to = pl.ds(pl.multiple_of(part * height, height), height)
            out_ref[to, :] = jnp.dot(a_ref[at, :], panel[...], preferred_element_type=jnp.float32)


def direct_product(ids, matrix, panels, after):
    rows, cols = matrix.shape
    width = panels[0].shape[1]
    out_shape = [jax.ShapeDtypeStruct((rows // parts, width), jnp.float32) for parts in (2, 4, 4)]
    return local(
        direct_kernel, out_shape, "direct_product", ids, matrix, *panels, after=after,
        scratch_shapes=[pltpu.VMEM((cols, width), jnp.bfloat16), pltpu.SemaphoreType.DMA],
    )


def give_product(ids, matrix, panels, after):
    rows, cols = matrix.shape
    width = panels[0].shape[1]
    out_shape = [
        *[jax.ShapeDtypeStruct((rows // 4, width), jnp.float32)] * 2,
        jax.ShapeDtypeStruct((cols, width), jnp.bfloat16),
    ]
    return local(
        give_kernel, out_shape, "give_product", ids, matrix, *panels, after=after,
        scratch_shapes=[pltpu.SemaphoreType.DMA],
    )


def keep_product(ids, matrix, panel, after):
    rows, cols = matrix.shape
    width = panel.shape[1]
    out_shape = jax.ShapeDtypeStruct((rows // 2, width), jnp.float32)
    return local(
        rows_kernel, out_shape, "keep_product", ids, matrix, panel, after=after
    )


def pack_kernel(count, ids, a_ref, *refs):
    theirs, (sum_ref, in_ref, own_ref, *msgs, total) = refs[:count], refs[count:]
    height = own_ref.shape[0]
    chips = len(msgs)
    rows = chips * height
    tile = rows // 4
    chip, core = ids[1], ids[2]

    for part in range(4):
        at = pl.ds(part * tile, tile)
        b_ref, where = theirs[part * count // 4], part * tile % theirs[0].shape[0]
        total[at, :] = a_ref[at, :] + b_ref[pl.ds(where, tile), :]

    @pl.when(ids[0] == chip)
    def _():
        @pl.loop(0, 4)
        def _(part):
            at = pl.ds(pl.multiple_of(part * tile, tile), tile)
            total[at, :] += sum_ref[at, :] + decode(in_ref[at, :], scale_of(in_ref, rows, part))

    for step, msg in enumerate(msgs):
        at = pl.ds(pl.multiple_of(lax.rem(chip + step, chips) * height, height), height)
        values = total[at, :]
        scale = scale_for(jnp.max(jnp.abs(values), keepdims=True))
        msg[pl.ds(0, height), :] = encode(values, scale)
        put_scale(msg, height, 0, scale)

    stays = (chip <= ids[0]) & (lax.div(chip, chips // 2) == core)

    @pl.when(stays)
    def _():
        at = pl.ds(pl.multiple_of((2 * lax.rem(chip, chips // 2) + core) * height, height), height)
        own_ref[...] = total[at, :]

    @pl.when(jnp.logical_not(stays))
    def _():
        own_ref[...] = jnp.zeros_like(own_ref)


def pack(ids, mine, theirs, partial, message, chips, after):
    rows, width = mine.shape
    height = rows // chips
    out_shape = [
        jax.ShapeDtypeStruct((height, width), jnp.float32),
        *[jax.ShapeDtypeStruct((height + TAIL, width), jnp.bfloat16)] * chips,
    ]
    return local(
        functools.partial(pack_kernel, len(theirs)), out_shape, "pack", ids, mine, *theirs, partial, message, after=after,
        scratch_shapes=[pltpu.VMEM((rows, width), jnp.float32)],
    )


def finish_kernel(ids, before, own, *refs):
    *messages, out_ref = refs
    height, width = own.shape
    total = own[...]
    for message in messages:
        total += decode(message[pl.ds(0, height), :], scale_of(message, height, 0))
    done = out_ref.shape[1] - width
    if done:
        out_ref[:, pl.ds(0, done)] = before[:, pl.ds(0, done)]
    out_ref[:, pl.ds(done, width)] = total


def finish(ids, before, arrays, after):
    height, width = arrays[0].shape
    done = 0 if before is None else before.shape[1]
    out_shape = jax.ShapeDtypeStruct((height, done + width), jnp.float32)
    return local(finish_kernel, out_shape, "finish", ids, arrays[0] if before is None else before, *arrays, after=after)


def shards(trailing, panel_vectors):
    rows_here, cols_here = trailing.shape
    piece = panel_vectors.shape[0]
    count = lax.axis_size("row")
    devices_along = lax.axis_size("col")
    chips = devices_along // 2
    bits = count.bit_length() - 1
    row, col = lax.axis_index("row"), lax.axis_index("col")
    chip, core = col // 2, col % 2

    def at(row, chip, core):
        return (row * chips + chip) * 2 + core

    def turned(place, core):
        if core == 0:
            return place
        return sum(((place >> b) & 1) << (bits - 1 - b) for b in range(bits))

    def send(x, pairs):
        return lax.ppermute(x, ("row", "col"), [(at(*s), at(*d)) for s, d in pairs])

    offset = row ^ chip
    reverse = sum(((offset >> b) & 1) << (bits - 1 - b) for b in range(bits))
    place = jnp.where(core == 0, offset, reverse)
    ids = jnp.stack([row, chip, core, row * rows_here - col * cols_here, place]).astype(jnp.int32)

    def needed(chip, core, place, bit):
        rest = range(0, count, 2 ** (bit + 1))
        return any(chip ^ turned(place | r, core) > chip for r in rest)

    everyone = [(k, c) for k in range(chips) for c in range(2)]

    width = panel_vectors.shape[1] // 2
    active = [(r, k, c) for r in range(count) for k in range(r + 1) for c in range(2)]

    def spread(place, source):
        bit = place.bit_length() - 1
        before = place - (1 << bit)
        pairs = [
            ((k ^ turned(before, c), k, c), (k ^ turned(place, c), k, c))
            for k, c in everyone
            if needed(k, c, place, bit)
        ]
        return send(source, pairs)

    def collect(bit, message):
        pairs = [
            ((k ^ turned(p, c), k, c), (k ^ turned(p - (1 << bit), c), k, c))
            for k, c in everyone
            for p in range(1 << bit, 2 << bit)
            if needed(k, c, p, bit)
        ]
        return send(message, pairs)

    matrix, diagonal = load(ids, trailing)

    line_of = [(r, k, c) for r in range(count) for k in range(chips) for c in range(2)]

    def step(x, to, wanted):
        return send(x, [((r, k, c), (r, to(k), c)) for r, k, c in line_of if wanted(r, k)])

    def by_distance(block):
        came, places = [block], [lambda chip: (chip, chip >= 0)]
        for by in range(1, chips):
            came.append(step(block, lambda k: (k + by) % chips, lambda r, k: (k + by) % chips <= r))
            places.append(lambda chip, by=by: (lax.rem(chip + chips - by, chips), chip >= 0))
        return came, places

    four = [
        lambda chip: (chip, chip >= 0),
        lambda chip: (chip ^ 2, chip >= 0),
        lambda chip: (jnp.maximum(chip - 1, 0), chip > 0),
        lambda chip: (jnp.minimum(chip + 1, 3), chip < 3),
        lambda chip: (3 - chip, (chip == 0) | (chip == 3)),
    ]

    def two_away(block):
        return step(block, lambda k: k ^ 2, lambda r, k: k >= 2 or k + 2 <= r)

    def next_ones(block):
        up = step(block, lambda k: k + 1, lambda r, k: k + 1 <= r and k < 3)
        return [up, step(block, lambda k: k - 1, lambda r, k: 0 <= k - 1 <= r)]

    def ends(two):
        return step(two, lambda k: 3 * (k - 1), lambda r, k: k == 1 or (k == 2 and r == 3))

    swap = [((r, k, c), (r, k, 1 - c)) for r, k, c in active]

    def widen(panels, after):
        panels[0], panels[1] = lax.optimization_barrier((panels[0], panels[1]))
        for place in range(2, count):
            panels.append(spread(place, panels[place - (1 << (place.bit_length() - 1))]))

    def relaying(partial, came, panels, after):
        for bit in reversed(range(bits - 1)):
            partial, message = relay(ids, partial, came, after)
            if panels:
                message, *panels[2:] = lax.optimization_barrier((message, *panels[2:]))
            came = collect(bit, message)
        return partial, came, message

    def deliver(keep, got, partial, came, after):
        own, *out = pack(ids, keep, got, partial, came, chips, after)
        arrays = [own]
        for step, x in enumerate(out):
            pairs = []
            for r, k, c in active:
                at = c * chips + (k + step) % chips
                if (at // 2, at % 2) != (k, c):
                    pairs.append(((r, k, c), (r, at // 2, at % 2)))
            arrays.append(send(x, pairs))
        return arrays

    block_a, block_b = panel_vectors[:, :width], panel_vectors[:, width:]
    if chips == 4:
        two_a, two_b = two_away(block_a), two_away(block_b)
        came_a = [block_a, two_a, *next_ones(block_a)]
        two_a, matrix = lax.optimization_barrier((two_a, matrix))
        came_a.append(ends(two_a))
        mine_a = line(ids, came_a, four, [two_b])
        came_b, places = [block_b, two_b, *next_ones(block_b), ends(two_b)], four
    else:
        came_a, places = by_distance(block_a)
        came_b, places = by_distance(block_b)
        mine_a = line(ids, came_a, places, [])
    other_a = send(mine_a, swap)
    panels_a = [half(ids, mine_a, other_a, piece)]
    panels_a.append(spread(1, panels_a[0]))
    partial_a, message_a = mirrored_product(ids, matrix, diagonal, mine_a, other_a, piece, [panels_a[0]])
    message_a, panels_a[1], *came_b[2:] = lax.optimization_barrier((message_a, panels_a[1], *came_b[2:]))
    to_a = collect(bits - 1, message_a)
    widen(panels_a, [])

    mine_b = line(ids, came_b, places, [])
    other_b = send(mine_b, swap)
    panels_b = [half(ids, mine_b, other_b, piece)]
    panels_b.append(spread(1, panels_b[0]))
    partial_b, message_b = mirrored_product(ids, matrix, diagonal, mine_b, other_b, piece, [panels_b[0]])
    to_b = collect(bits - 1, message_b)
    partial_a, to_a, relayed = relaying(partial_a, to_a, panels_a, [message_b])
    keep_a, *give_a = direct_product(ids, matrix, panels_a, [relayed, panels_b[1]])
    got_a = [send(x, swap) for x in give_a]
    partial_b, to_b, relayed = relaying(partial_b, to_b, [], [keep_a, to_a])
    widen(panels_b, [])
    arrays_a = deliver(keep_a, got_a, partial_a, to_a, [relayed])
    *give_b, panel_b = give_product(ids, matrix, panels_b, [arrays_a[0]])
    give_b, arrays_a[1] = lax.optimization_barrier((give_b, arrays_a[1]))
    got_b = [send(x, swap) for x in give_b]
    keep_b = keep_product(ids, matrix, panel_b, [to_b])
    arrays_b = deliver(keep_b, got_b, partial_b, to_b, [])
    result = finish(ids, None, arrays_a, [arrays_b[0]])
    return finish(ids, result, arrays_b, [])


def solution(mesh):
    in_specs = (P("row", "col"), P(("row", "col"), None))
    out_specs = P(("row", "col"), None)
    return jax.shard_map(shards, mesh=mesh, in_specs=in_specs, out_specs=out_specs, check_vma=False)
```

```python
import functools

import jax
import jax.numpy as jnp
from jax import lax
from jax.experimental import pallas as pl
from jax.experimental.pallas import tpu as pltpu
from jax.sharding import PartitionSpec as P

TOP = 40000.0
TAIL = 16
VMEM = 6 * 2**20


def scale_for(largest):
    scale = TOP / jnp.maximum(largest, 1e-30)
    return scale.astype(jnp.bfloat16).astype(jnp.float32)


def encode(values, scale):
    x = values * scale
    x2 = x * x
    x4 = x2 * x2
    return (x * jnp.abs(x) * x2 * x4).astype(jnp.bfloat16)


def decode(coded, scale):
    y = coded.astype(jnp.float32)
    back = jnp.where(scale > 0, 1.0 / scale, 0.0)
    return y * jnp.exp2(-0.875 * jnp.log2(jnp.maximum(jnp.abs(y), 2.0**-126))) * back


def scale_of(message, rows, block):
    return message[pl.ds(rows + block * TAIL, TAIL), :][0:1, 0:1].astype(jnp.float32)


def put_scale(message, rows, block, scale):
    spread = jnp.full((TAIL, message.shape[1]), scale, jnp.float32).astype(jnp.bfloat16)
    message[pl.ds(rows + block * TAIL, TAIL), :] = spread


def local(kernel, out_shape, name, *operands, after=(), **options):
    count, skipped = len(operands), len(after)

    def body(*refs):
        kernel(*refs[:count], *refs[count + skipped :])

    return pl.pallas_call(
        body,
        out_shape=out_shape,
        in_specs=[pl.BlockSpec(memory_space=pltpu.SMEM)]
        + [pl.BlockSpec(memory_space=pltpu.VMEM)] * (count - 1)
        + [pl.BlockSpec(memory_space=pl.ANY)] * skipped,
        out_specs=jax.tree.map(lambda _: pl.BlockSpec(memory_space=pltpu.VMEM), out_shape),
        compiler_params=pltpu.CompilerParams(vmem_limit_bytes=VMEM),
        name=name,
        **options,
    )(*operands, *after)


def load_kernel(ids, a_ref, out_ref, diagonal, sem):
    height, cols = a_ref.shape
    block = cols // 4
    diagonal[...] = jnp.zeros_like(diagonal)

    @pl.when(ids[1] <= ids[0])
    def _():
        copy = pltpu.make_async_copy(a_ref, out_ref, sem)
        copy.start()
        copy.wait()

    for part in range(4):
        here = pl.ds(part * block, block)

        @pl.when(ids[1] == ids[0])
        def _():
            @pl.loop(0, height // block)
            def _(at):
                first = ids[3] + at * block
                rows = pl.ds(pl.multiple_of(at * block, block), block)

                @pl.when(first < part * block)
                def _():
                    out_ref[rows, here] = jnp.zeros((block, block), out_ref.dtype)

                @pl.when(first == part * block)
                def _():
                    tile = out_ref[rows, here]
                    empty = jnp.zeros_like(tile)
                    row = lax.broadcasted_iota(jnp.int32, tile.shape, 0)
                    col = lax.broadcasted_iota(jnp.int32, tile.shape, 1)
                    out_ref[rows, here] = jnp.where(row >= col, tile, empty)
                    on = jnp.where(row == col, tile, empty).astype(jnp.float32)
                    diagonal[:, here] = jnp.broadcast_to(jnp.sum(on, axis=0, keepdims=True), (8, block))


def load(ids, trailing):
    return pl.pallas_call(
        load_kernel,
        out_shape=[
            jax.ShapeDtypeStruct(trailing.shape, trailing.dtype),
            jax.ShapeDtypeStruct((8, trailing.shape[1]), jnp.float32),
        ],
        in_specs=[pl.BlockSpec(memory_space=pltpu.SMEM), pl.BlockSpec(memory_space=pltpu.HBM)],
        out_specs=[pl.BlockSpec(memory_space=pltpu.VMEM)] * 2,
        scratch_shapes=[pltpu.SemaphoreType.DMA],
        compiler_params=pltpu.CompilerParams(vmem_limit_bytes=VMEM),
        name="load",
    )(ids, trailing)


def line_kernel(places, ids, *refs):
    *came, out_ref = refs
    height = came[0].shape[0]
    for place, piece in zip(places, came):
        chip, there = place(ids[1])

        @pl.when(there)
        def _():
            out_ref[pl.ds(pl.multiple_of(chip * height, height), height), :] = piece[...]


def line(ids, came, places, after):
    height, width = came[0].shape
    chips = 4 if len(came) == 5 else len(came)
    out_shape = jax.ShapeDtypeStruct((height * chips, width), came[0].dtype)
    return local(functools.partial(line_kernel, places), out_shape, "line", ids, *came, after=after)


def half_kernel(height, ids, mine, other, *outs):
    rows, width = outs[0].shape
    count = rows // height
    for at in range(count // 2):
        chip = ids[2] * (count // 2) + at
        here = pl.ds(pl.multiple_of(chip * height, height), height)
        for core, ref in ((ids[2], mine), (1 - ids[2], other)):
            to = pl.ds(pl.multiple_of((2 * at + core) * height, height), height)
            for part, out_ref in enumerate(outs):
                out_ref[to, :] = ref[here, pl.ds(part * width, width)]


def half(ids, mine, other, height):
    rows, width = mine.shape
    out_shape = [jax.ShapeDtypeStruct((rows, width // 2), mine.dtype)] * 2
    return local(functools.partial(half_kernel, height), out_shape, "half", ids, mine, other)


def mirrored_kernel(piece, part_at, ids, a_ref, diagonal, mine, other, m_ref, msg_ref, turned):
    height, cols = a_ref.shape
    block = cols // 4
    used = ids[1] <= ids[0]
    these = pl.ds(part_at * m_ref.shape[1], m_ref.shape[1])

    @pl.loop(0, height // piece // 2)
    def _(at):
        rows = pl.ds(pl.multiple_of(at * piece, piece), piece)
        for core, ref in ((ids[2], mine), (1 - ids[2], other)):
            turned[:, pl.ds(pl.multiple_of((2 * at + core) * piece, piece), piece)] = ref[rows, these].T

    @pl.loop(0, 4)
    def _(part):
        here = pl.ds(pl.multiple_of(part * block, block), block)

        @pl.when(used)
        def _():
            m_ref[here, :] = jnp.dot(turned[...], a_ref[:, here], preferred_element_type=jnp.float32).T

        @pl.when(jnp.logical_not(used))
        def _():
            m_ref[here, :] = jnp.zeros((block, m_ref.shape[1]), jnp.float32)

        @pl.when(ids[1] == ids[0])
        def _():
            rows = pl.ds(pl.multiple_of(part * block - ids[3], block), block)
            m_ref[here, :] -= (turned[:, rows].astype(jnp.float32) * diagonal[0:1, here]).T

        total = m_ref[here, :]
        scale = scale_for(jnp.max(jnp.abs(total), keepdims=True))
        msg_ref[here, :] = encode(total, scale)
        put_scale(msg_ref, cols, part, scale)


def mirrored_product(ids, matrix, diagonal, mine, other, piece, part_at, after):
    rows, cols = matrix.shape
    width = mine.shape[1] // 2
    out_shape = [
        jax.ShapeDtypeStruct((cols, width), jnp.float32),
        jax.ShapeDtypeStruct((cols + 4 * TAIL, width), jnp.bfloat16),
    ]
    return local(
        functools.partial(mirrored_kernel, piece, part_at), out_shape, "mirrored_product",
        ids, matrix, diagonal, mine, other, after=after,
        scratch_shapes=[pltpu.VMEM((width, rows), jnp.bfloat16)],
    )


def relay_kernel(ids, m_ref, in_ref, sum_ref, msg_ref):
    rows, width = m_ref.shape
    height = rows // 4

    @pl.loop(0, 4)
    def _(part):
        at = pl.ds(pl.multiple_of(part * height, height), height)
        total = m_ref[at, :] + decode(in_ref[at, :], scale_of(in_ref, rows, part))
        scale = scale_for(jnp.max(jnp.abs(total), keepdims=True))
        sum_ref[at, :] = total
        msg_ref[at, :] = encode(total, scale)
        put_scale(msg_ref, rows, part, scale)


def relay(ids, partial, message, after):
    out_shape = [jax.ShapeDtypeStruct(x.shape, x.dtype) for x in (partial, message)]
    return local(relay_kernel, out_shape, "relay", ids, partial, message, after=after)


def pick(ids, panels, panel, sem):
    for place, ref in enumerate(panels):

        @pl.when(ids[4] == place)
        def _():
            copy = pltpu.make_async_copy(ref, panel, sem)
            copy.start()
            copy.wait()


def give_kernel(ids, a_ref, *refs):
    *panels, give_ref, give_too, panel, sem = refs
    pick(ids, panels, panel, sem)
    rows_kernel(ids, a_ref, panel, give_ref, core=1 - ids[2], of=2)
    rows_kernel(ids, a_ref, panel, give_too, core=1 - ids[2], at=1, of=2)


def direct_kernel(ids, a_ref, *refs):
    *panels, keep_ref, give_ref, give_too, panel, sem = refs
    pick(ids, panels, panel, sem)
    rows_kernel(ids, a_ref, panel, give_ref, core=1 - ids[2], of=2)
    rows_kernel(ids, a_ref, panel, give_too, core=1 - ids[2], at=1, of=2)
    rows_kernel(ids, a_ref, panel, keep_ref)


def rows_kernel(ids, a_ref, panel, out_ref, core=None, at=0, of=1):
    core = ids[2] if core is None else core
    rows = out_ref.shape[0]
    height = rows * of // 4
    skip = at * rows

    @pl.when(ids[1] <= ids[0])
    def _():
        @pl.loop(0, 4 // of)
        def _(part):
            at = pl.ds(pl.multiple_of(core * rows * of + skip + part * height, height), height)
            to = pl.ds(pl.multiple_of(part * height, height), height)
            out_ref[to, :] = jnp.dot(a_ref[at, :], panel[...], preferred_element_type=jnp.float32)


def direct_product(ids, matrix, panels, after):
    rows, cols = matrix.shape
    width = panels[0].shape[1]
    out_shape = [jax.ShapeDtypeStruct((rows // parts, width), jnp.float32) for parts in (2, 4, 4)]
    return local(
        direct_kernel, out_shape, "direct_product", ids, matrix, *panels, after=after,
        scratch_shapes=[pltpu.VMEM((cols, width), jnp.bfloat16), pltpu.SemaphoreType.DMA],
    )


def give_product(ids, matrix, panels, after):
    rows, cols = matrix.shape
    width = panels[0].shape[1]
    out_shape = [
        *[jax.ShapeDtypeStruct((rows // 4, width), jnp.float32)] * 2,
        jax.ShapeDtypeStruct((cols, width), jnp.bfloat16),
    ]
    return local(
        give_kernel, out_shape, "give_product", ids, matrix, *panels, after=after,
        scratch_shapes=[pltpu.SemaphoreType.DMA],
    )


def keep_product(ids, matrix, panel, after):
    rows, cols = matrix.shape
    width = panel.shape[1]
    out_shape = jax.ShapeDtypeStruct((rows // 2, width), jnp.float32)
    return local(
        rows_kernel, out_shape, "keep_product", ids, matrix, panel, after=after
    )


def pack_kernel(count, ids, a_ref, *refs):
    theirs, (sum_ref, in_ref, own_ref, *msgs, total) = refs[:count], refs[count:]
    height = own_ref.shape[0]
    chips = len(msgs)
    rows = chips * height
    tile = rows // 4
    chip, core = ids[1], ids[2]

    for part in range(4):
        at = pl.ds(part * tile, tile)
        b_ref, where = theirs[part * count // 4], part * tile % theirs[0].shape[0]
        total[at, :] = a_ref[at, :] + b_ref[pl.ds(where, tile), :]

    @pl.when(ids[0] == chip)
    def _():
        @pl.loop(0, 4)
        def _(part):
            at = pl.ds(pl.multiple_of(part * tile, tile), tile)
            total[at, :] += sum_ref[at, :] + decode(in_ref[at, :], scale_of(in_ref, rows, part))

    for step, msg in enumerate(msgs):
        at = pl.ds(pl.multiple_of(lax.rem(chip + step, chips) * height, height), height)
        values = total[at, :]
        scale = scale_for(jnp.max(jnp.abs(values), keepdims=True))
        msg[pl.ds(0, height), :] = encode(values, scale)
        put_scale(msg, height, 0, scale)

    stays = (chip <= ids[0]) & (lax.div(chip, chips // 2) == core)

    @pl.when(stays)
    def _():
        at = pl.ds(pl.multiple_of((2 * lax.rem(chip, chips // 2) + core) * height, height), height)
        own_ref[...] = total[at, :]

    @pl.when(jnp.logical_not(stays))
    def _():
        own_ref[...] = jnp.zeros_like(own_ref)


def pack(ids, mine, theirs, partial, message, chips, after):
    rows, width = mine.shape
    height = rows // chips
    out_shape = [
        jax.ShapeDtypeStruct((height, width), jnp.float32),
        *[jax.ShapeDtypeStruct((height + TAIL, width), jnp.bfloat16)] * chips,
    ]
    return local(
        functools.partial(pack_kernel, len(theirs)), out_shape, "pack", ids, mine, *theirs, partial, message, after=after,
        scratch_shapes=[pltpu.VMEM((rows, width), jnp.float32)],
    )


def finish_kernel(ids, before, own, *refs):
    *messages, out_ref = refs
    height, width = own.shape
    total = own[...]
    for message in messages:
        total += decode(message[pl.ds(0, height), :], scale_of(message, height, 0))
    done = out_ref.shape[1] - width
    if done:
        out_ref[:, pl.ds(0, done)] = before[:, pl.ds(0, done)]
    out_ref[:, pl.ds(done, width)] = total


def finish(ids, before, arrays, after):
    height, width = arrays[0].shape
    done = 0 if before is None else before.shape[1]
    out_shape = jax.ShapeDtypeStruct((height, done + width), jnp.float32)
    return local(finish_kernel, out_shape, "finish", ids, arrays[0] if before is None else before, *arrays, after=after)


def shards(trailing, panel_vectors):
    rows_here, cols_here = trailing.shape
    piece = panel_vectors.shape[0]
    count = lax.axis_size("row")
    devices_along = lax.axis_size("col")
    chips = devices_along // 2
    bits = count.bit_length() - 1
    row, col = lax.axis_index("row"), lax.axis_index("col")
    chip, core = col // 2, col % 2

    def at(row, chip, core):
        return (row * chips + chip) * 2 + core

    def turned(place, core):
        if core == 0:
            return place
        return sum(((place >> b) & 1) << (bits - 1 - b) for b in range(bits))

    def send(x, pairs):
        return lax.ppermute(x, ("row", "col"), [(at(*s), at(*d)) for s, d in pairs])

    offset = row ^ chip
    reverse = sum(((offset >> b) & 1) << (bits - 1 - b) for b in range(bits))
    place = jnp.where(core == 0, offset, reverse)
    ids = jnp.stack([row, chip, core, row * rows_here - col * cols_here, place]).astype(jnp.int32)

    def needed(chip, core, place, bit):
        rest = range(0, count, 2 ** (bit + 1))
        return any(chip ^ turned(place | r, core) > chip for r in rest)

    everyone = [(k, c) for k in range(chips) for c in range(2)]

    active = [(r, k, c) for r in range(count) for k in range(r + 1) for c in range(2)]

    def spread(place, source):
        bit = place.bit_length() - 1
        before = place - (1 << bit)
        pairs = [
            ((k ^ turned(before, c), k, c), (k ^ turned(place, c), k, c))
            for k, c in everyone
            if needed(k, c, place, bit)
        ]
        return send(source, pairs)

    def collect(bit, message):
        pairs = [
            ((k ^ turned(p, c), k, c), (k ^ turned(p - (1 << bit), c), k, c))
            for k, c in everyone
            for p in range(1 << bit, 2 << bit)
            if needed(k, c, p, bit)
        ]
        return send(message, pairs)

    matrix, diagonal = load(ids, trailing)

    line_of = [(r, k, c) for r in range(count) for k in range(chips) for c in range(2)]

    def step(x, to, wanted):
        return send(x, [((r, k, c), (r, to(k), c)) for r, k, c in line_of if wanted(r, k)])

    def by_distance(block):
        came, places = [block], [lambda chip: (chip, chip >= 0)]
        for by in range(1, chips):
            came.append(step(block, lambda k: (k + by) % chips, lambda r, k: (k + by) % chips <= r))
            places.append(lambda chip, by=by: (lax.rem(chip + chips - by, chips), chip >= 0))
        return came, places

    four = [
        lambda chip: (chip, chip >= 0),
        lambda chip: (chip ^ 2, chip >= 0),
        lambda chip: (jnp.maximum(chip - 1, 0), chip > 0),
        lambda chip: (jnp.minimum(chip + 1, 3), chip < 3),
        lambda chip: (3 - chip, (chip == 0) | (chip == 3)),
    ]

    def two_away(block):
        return step(block, lambda k: k ^ 2, lambda r, k: k >= 2 or k + 2 <= r)

    def next_ones(block):
        up = step(block, lambda k: k + 1, lambda r, k: k + 1 <= r and k < 3)
        return [up, step(block, lambda k: k - 1, lambda r, k: 0 <= k - 1 <= r)]

    def ends(two):
        return step(two, lambda k: 3 * (k - 1), lambda r, k: k == 1 or (k == 2 and r == 3))

    swap = [((r, k, c), (r, k, 1 - c)) for r, k, c in active]

    def widen(panels, after):
        panels[0], panels[1] = lax.optimization_barrier((panels[0], panels[1]))
        for place in range(2, count):
            panels.append(spread(place, panels[place - (1 << (place.bit_length() - 1))]))

    def relaying(partial, came, panels, after):
        for bit in reversed(range(bits - 1)):
            partial, message = relay(ids, partial, came, after)
            if panels:
                message, *panels[2:] = lax.optimization_barrier((message, *panels[2:]))
            came = collect(bit, message)
        return partial, came, message

    def deliver(keep, got, partial, came, after):
        own, *out = pack(ids, keep, got, partial, came, chips, after)
        arrays = [own]
        for step, x in enumerate(out):
            pairs = []
            for r, k, c in active:
                at = c * chips + (k + step) % chips
                if (at // 2, at % 2) != (k, c):
                    pairs.append(((r, k, c), (r, at // 2, at % 2)))
            arrays.append(send(x, pairs))
        return arrays

    if chips == 4:
        two = two_away(panel_vectors)
        came, places = [panel_vectors, two, *next_ones(panel_vectors)], four
        two, matrix = lax.optimization_barrier((two, matrix))
        came.append(ends(two))
    else:
        came, places = by_distance(panel_vectors)
    mine = line(ids, came, places, [])
    other = send(mine, swap)
    panels_a, panels_b = ([x] for x in half(ids, mine, other, piece))
    panels_a.append(spread(1, panels_a[0]))
    partial_a, message_a = mirrored_product(ids, matrix, diagonal, mine, other, piece, 0, [panels_a[0]])
    message_a, panels_a[1] = lax.optimization_barrier((message_a, panels_a[1]))
    to_a = collect(bits - 1, message_a)
    widen(panels_a, [])
    partial_b, message_b = mirrored_product(ids, matrix, diagonal, mine, other, piece, 1, [message_a])
    to_b = collect(bits - 1, message_b)
    panels_b.append(spread(1, panels_b[0]))
    partial_a, to_a, relayed = relaying(partial_a, to_a, panels_a, [message_b])
    keep_a, *give_a = direct_product(ids, matrix, panels_a, [relayed])
    got_a = [send(x, swap) for x in give_a]
    partial_b, to_b, relayed = relaying(partial_b, to_b, [], [keep_a, to_a])
    widen(panels_b, [])
    arrays_a = deliver(keep_a, got_a, partial_a, to_a, [relayed])
    *give_b, panel_b = give_product(ids, matrix, panels_b, [arrays_a[0]])
    give_b, arrays_a[1] = lax.optimization_barrier((give_b, arrays_a[1]))
    got_b = [send(x, swap) for x in give_b]
    keep_b = keep_product(ids, matrix, panel_b, [to_b])
    arrays_b = deliver(keep_b, got_b, partial_b, to_b, [])
    result = finish(ids, None, arrays_a, [arrays_b[0]])
    return finish(ids, result, arrays_b, [])


def solution(mesh):
    in_specs = (P("row", "col"), P(("row", "col"), None))
    out_specs = P(("row", "col"), None)
    return jax.shard_map(shards, mesh=mesh, in_specs=in_specs, out_specs=out_specs, check_vma=False)
```

```python
import functools

import jax
import jax.numpy as jnp
from jax import lax
from jax.experimental import pallas as pl
from jax.experimental.pallas import tpu as pltpu
from jax.sharding import PartitionSpec as P

TOP = 1400.0
TAIL = 16
VMEM = 6 * 2**20


def scale_for(largest):
    scale = TOP / jnp.maximum(largest, 1e-30)
    return scale.astype(jnp.bfloat16).astype(jnp.float32)


def encode(values, scale):
    x = values * scale
    x2 = x * x
    x4 = x2 * x2
    return (x * jnp.abs(x) * x2 * (x4 * x4)).astype(jnp.bfloat16)


def decode(coded, scale):
    y = coded.astype(jnp.float32)
    back = jnp.where(scale > 0, 1.0 / scale, 0.0)
    return y * jnp.exp2(-11 / 12 * jnp.log2(jnp.maximum(jnp.abs(y), 2.0**-126))) * back


def scale_of(message, rows, block):
    return message[pl.ds(rows + block * TAIL, TAIL), :][0:1, 0:1].astype(jnp.float32)


def put_scale(message, rows, block, scale):
    spread = jnp.full((TAIL, message.shape[1]), scale, jnp.float32).astype(jnp.bfloat16)
    message[pl.ds(rows + block * TAIL, TAIL), :] = spread


def local(kernel, out_shape, name, *operands, after=(), **options):
    count, skipped = len(operands), len(after)

    def body(*refs):
        kernel(*refs[:count], *refs[count + skipped :])

    return pl.pallas_call(
        body,
        out_shape=out_shape,
        in_specs=[pl.BlockSpec(memory_space=pltpu.SMEM)]
        + [pl.BlockSpec(memory_space=pltpu.VMEM)] * (count - 1)
        + [pl.BlockSpec(memory_space=pl.ANY)] * skipped,
        out_specs=jax.tree.map(lambda _: pl.BlockSpec(memory_space=pltpu.VMEM), out_shape),
        compiler_params=pltpu.CompilerParams(vmem_limit_bytes=VMEM),
        name=name,
        **options,
    )(*operands, *after)


def load_kernel(ids, a_ref, out_ref, diagonal, sem):
    height, cols = a_ref.shape
    block = cols // 4
    diagonal[...] = jnp.zeros_like(diagonal)

    @pl.when(ids[1] <= ids[0])
    def _():
        copy = pltpu.make_async_copy(a_ref, out_ref, sem)
        copy.start()
        copy.wait()

    for part in range(4):
        here = pl.ds(part * block, block)

        @pl.when(ids[1] == ids[0])
        def _():
            @pl.loop(0, height // block)
            def _(at):
                first = ids[3] + at * block
                rows = pl.ds(pl.multiple_of(at * block, block), block)

                @pl.when(first < part * block)
                def _():
                    out_ref[rows, here] = jnp.zeros((block, block), out_ref.dtype)

                @pl.when(first == part * block)
                def _():
                    tile = out_ref[rows, here]
                    empty = jnp.zeros_like(tile)
                    row = lax.broadcasted_iota(jnp.int32, tile.shape, 0)
                    col = lax.broadcasted_iota(jnp.int32, tile.shape, 1)
                    out_ref[rows, here] = jnp.where(row >= col, tile, empty)
                    on = jnp.where(row == col, tile, empty).astype(jnp.float32)
                    diagonal[:, here] = jnp.broadcast_to(jnp.sum(on, axis=0, keepdims=True), (8, block))


def load(ids, trailing):
    return pl.pallas_call(
        load_kernel,
        out_shape=[
            jax.ShapeDtypeStruct(trailing.shape, trailing.dtype),
            jax.ShapeDtypeStruct((8, trailing.shape[1]), jnp.float32),
        ],
        in_specs=[pl.BlockSpec(memory_space=pltpu.SMEM), pl.BlockSpec(memory_space=pltpu.HBM)],
        out_specs=[pl.BlockSpec(memory_space=pltpu.VMEM)] * 2,
        scratch_shapes=[pltpu.SemaphoreType.DMA],
        compiler_params=pltpu.CompilerParams(vmem_limit_bytes=VMEM),
        name="load",
    )(ids, trailing)


def line_kernel(places, ids, *refs):
    *came, out_ref = refs
    height = came[0].shape[0]
    for place, piece in zip(places, came):
        chip, there = place(ids[1])

        @pl.when(there)
        def _():
            out_ref[pl.ds(pl.multiple_of(chip * height, height), height), :] = piece[...]


def line(ids, came, places, after):
    height, width = came[0].shape
    chips = 4 if len(came) == 5 else len(came)
    out_shape = jax.ShapeDtypeStruct((height * chips, width), came[0].dtype)
    return local(functools.partial(line_kernel, places), out_shape, "line", ids, *came, after=after)


def half_kernel(height, ids, mine, other, *outs):
    rows, width = outs[0].shape
    count = rows // height
    for at in range(count // 2):
        chip = ids[2] * (count // 2) + at
        here = pl.ds(pl.multiple_of(chip * height, height), height)
        for core, ref in ((ids[2], mine), (1 - ids[2], other)):
            to = pl.ds(pl.multiple_of((2 * at + core) * height, height), height)
            for part, out_ref in enumerate(outs):
                out_ref[to, :] = ref[here, pl.ds(part * width, width)]


def half(ids, mine, other, height):
    rows, width = mine.shape
    out_shape = [jax.ShapeDtypeStruct((rows, width // 2), mine.dtype)] * 2
    return local(functools.partial(half_kernel, height), out_shape, "half", ids, mine, other)


def mirrored_kernel(piece, part_at, ids, a_ref, diagonal, mine, other, m_ref, msg_ref, turned):
    height, cols = a_ref.shape
    block = cols // 4
    used = ids[1] <= ids[0]
    these = pl.ds(part_at * m_ref.shape[1], m_ref.shape[1])

    @pl.loop(0, height // piece // 2)
    def _(at):
        rows = pl.ds(pl.multiple_of(at * piece, piece), piece)
        for core, ref in ((ids[2], mine), (1 - ids[2], other)):
            turned[:, pl.ds(pl.multiple_of((2 * at + core) * piece, piece), piece)] = ref[rows, these].T

    @pl.loop(0, 4)
    def _(part):
        here = pl.ds(pl.multiple_of(part * block, block), block)

        @pl.when(used)
        def _():
            m_ref[here, :] = jnp.dot(turned[...], a_ref[:, here], preferred_element_type=jnp.float32).T

        @pl.when(jnp.logical_not(used))
        def _():
            m_ref[here, :] = jnp.zeros((block, m_ref.shape[1]), jnp.float32)

        @pl.when(ids[1] == ids[0])
        def _():
            rows = pl.ds(pl.multiple_of(part * block - ids[3], block), block)
            m_ref[here, :] -= (turned[:, rows].astype(jnp.float32) * diagonal[0:1, here]).T

        total = m_ref[here, :]
        scale = scale_for(jnp.max(jnp.abs(total), keepdims=True))
        msg_ref[here, :] = encode(total, scale)
        put_scale(msg_ref, cols, part, scale)


def mirrored_product(ids, matrix, diagonal, mine, other, piece, part_at, after):
    rows, cols = matrix.shape
    width = mine.shape[1] // 2
    out_shape = [
        jax.ShapeDtypeStruct((cols, width), jnp.float32),
        jax.ShapeDtypeStruct((cols + 4 * TAIL, width), jnp.bfloat16),
    ]
    return local(
        functools.partial(mirrored_kernel, piece, part_at), out_shape, "mirrored_product",
        ids, matrix, diagonal, mine, other, after=after,
        scratch_shapes=[pltpu.VMEM((width, rows), jnp.bfloat16)],
    )


def relay_kernel(ids, m_ref, in_ref, sum_ref, msg_ref):
    rows, width = m_ref.shape
    height = rows // 4

    @pl.loop(0, 4)
    def _(part):
        at = pl.ds(pl.multiple_of(part * height, height), height)
        total = m_ref[at, :] + decode(in_ref[at, :], scale_of(in_ref, rows, part))
        scale = scale_for(jnp.max(jnp.abs(total), keepdims=True))
        sum_ref[at, :] = total
        msg_ref[at, :] = encode(total, scale)
        put_scale(msg_ref, rows, part, scale)


def relay(ids, partial, message, after):
    out_shape = [jax.ShapeDtypeStruct(x.shape, x.dtype) for x in (partial, message)]
    return local(relay_kernel, out_shape, "relay", ids, partial, message, after=after)


def pick(ids, panels, panel, sem):
    for place, ref in enumerate(panels):

        @pl.when(ids[4] == place)
        def _():
            copy = pltpu.make_async_copy(ref, panel, sem)
            copy.start()
            copy.wait()


def give_kernel(ids, a_ref, *refs):
    *panels, give_ref, give_too, panel, sem = refs
    pick(ids, panels, panel, sem)
    rows_kernel(ids, a_ref, panel, give_ref, core=1 - ids[2], of=2)
    rows_kernel(ids, a_ref, panel, give_too, core=1 - ids[2], at=1, of=2)


def direct_kernel(ids, a_ref, *refs):
    *panels, keep_ref, give_ref, give_too, panel, sem = refs
    pick(ids, panels, panel, sem)
    rows_kernel(ids, a_ref, panel, give_ref, core=1 - ids[2], of=2)
    rows_kernel(ids, a_ref, panel, give_too, core=1 - ids[2], at=1, of=2)
    rows_kernel(ids, a_ref, panel, keep_ref)


def rows_kernel(ids, a_ref, panel, out_ref, core=None, at=0, of=1):
    core = ids[2] if core is None else core
    rows = out_ref.shape[0]
    height = rows * of // 4
    skip = at * rows

    @pl.when(ids[1] <= ids[0])
    def _():
        @pl.loop(0, 4 // of)
        def _(part):
            at = pl.ds(pl.multiple_of(core * rows * of + skip + part * height, height), height)
            to = pl.ds(pl.multiple_of(part * height, height), height)
            out_ref[to, :] = jnp.dot(a_ref[at, :], panel[...], preferred_element_type=jnp.float32)


def direct_product(ids, matrix, panels, after):
    rows, cols = matrix.shape
    width = panels[0].shape[1]
    out_shape = [jax.ShapeDtypeStruct((rows // parts, width), jnp.float32) for parts in (2, 4, 4)]
    return local(
        direct_kernel, out_shape, "direct_product", ids, matrix, *panels, after=after,
        scratch_shapes=[pltpu.VMEM((cols, width), jnp.bfloat16), pltpu.SemaphoreType.DMA],
    )


def give_product(ids, matrix, panels, after):
    rows, cols = matrix.shape
    width = panels[0].shape[1]
    out_shape = [
        *[jax.ShapeDtypeStruct((rows // 4, width), jnp.float32)] * 2,
        jax.ShapeDtypeStruct((cols, width), jnp.bfloat16),
    ]
    return local(
        give_kernel, out_shape, "give_product", ids, matrix, *panels, after=after,
        scratch_shapes=[pltpu.SemaphoreType.DMA],
    )


def keep_product(ids, matrix, panel, after):
    rows, cols = matrix.shape
    width = panel.shape[1]
    out_shape = jax.ShapeDtypeStruct((rows // 2, width), jnp.float32)
    return local(
        rows_kernel, out_shape, "keep_product", ids, matrix, panel, after=after
    )


def pack_kernel(count, ids, a_ref, *refs):
    theirs, (sum_ref, in_ref, own_ref, *msgs, total) = refs[:count], refs[count:]
    height = own_ref.shape[0]
    rounds = len(msgs)
    rows = rounds * height
    tile = rows // 4
    chip, core = ids[1], ids[2]

    for part in range(4):
        at = pl.ds(part * tile, tile)
        b_ref, where = theirs[part * count // 4], part * tile % theirs[0].shape[0]
        total[at, :] = a_ref[at, :] + b_ref[pl.ds(where, tile), :]

    @pl.when(ids[0] == chip)
    def _():
        @pl.loop(0, 4)
        def _(part):
            at = pl.ds(pl.multiple_of(part * tile, tile), tile)
            total[at, :] += sum_ref[at, :] + decode(in_ref[at, :], scale_of(in_ref, rows, part))

    for step, msg in enumerate(msgs):
        at = pl.ds(pl.multiple_of(lax.rem(chip + step, rounds) * height, height), height)
        values = total[at, :]
        scale = scale_for(jnp.max(jnp.abs(values), keepdims=True))
        msg[pl.ds(0, height), :] = encode(values, scale)
        put_scale(msg, height, 0, scale)

    stays = (chip <= ids[0]) & (lax.div(chip, rounds // 2) == core)

    @pl.when(stays)
    def _():
        place = 2 * lax.rem(chip, rounds // 2) + core
        own_ref[...] = total[pl.ds(pl.multiple_of(place * height, height), height), :]

    @pl.when(jnp.logical_not(stays))
    def _():
        own_ref[...] = jnp.zeros_like(own_ref)


def pack(ids, mine, theirs, partial, message, rounds, after):
    rows, width = mine.shape
    height = rows // rounds
    out_shape = [
        jax.ShapeDtypeStruct((height, width), jnp.float32),
        *[jax.ShapeDtypeStruct((height + TAIL, width), jnp.bfloat16)] * rounds,
    ]
    return local(
        functools.partial(pack_kernel, len(theirs)), out_shape, "pack", ids, mine, *theirs, partial, message, after=after,
        scratch_shapes=[pltpu.VMEM((rows, width), jnp.float32)],
    )


def finish_kernel(ids, before, own, *refs):
    *messages, out_ref = refs
    height, width = own.shape
    total = own[...]
    for message in messages:
        total += decode(message[pl.ds(0, height), :], scale_of(message, height, 0))
    done = out_ref.shape[1] - width
    if done:
        out_ref[:, pl.ds(0, done)] = before[:, pl.ds(0, done)]
    out_ref[:, pl.ds(done, width)] = total


def finish(ids, before, arrays, after):
    height, width = arrays[0].shape
    done = 0 if before is None else before.shape[1]
    out_shape = jax.ShapeDtypeStruct((height, done + width), jnp.float32)
    return local(finish_kernel, out_shape, "finish", ids, arrays[0] if before is None else before, *arrays, after=after)


def shards(trailing, panel_vectors):
    rows_here, cols_here = trailing.shape
    piece = panel_vectors.shape[0]
    count = lax.axis_size("row")
    devices_along = lax.axis_size("col")
    chips = devices_along // 2
    bits = count.bit_length() - 1
    row, col = lax.axis_index("row"), lax.axis_index("col")
    chip, core = col // 2, col % 2

    def at(row, chip, core):
        return (row * chips + chip) * 2 + core

    def turned(place, core):
        if core == 0:
            return place
        return sum(((place >> b) & 1) << (bits - 1 - b) for b in range(bits))

    def send(x, pairs):
        return lax.ppermute(x, ("row", "col"), [(at(*s), at(*d)) for s, d in pairs])

    offset = row ^ chip
    reverse = sum(((offset >> b) & 1) << (bits - 1 - b) for b in range(bits))
    place = jnp.where(core == 0, offset, reverse)
    ids = jnp.stack([row, chip, core, row * rows_here - col * cols_here, place]).astype(jnp.int32)

    def needed(chip, core, place, bit):
        rest = range(0, count, 2 ** (bit + 1))
        return any(chip ^ turned(place | r, core) > chip for r in rest)

    everyone = [(k, c) for k in range(chips) for c in range(2)]

    active = [(r, k, c) for r in range(count) for k in range(r + 1) for c in range(2)]

    def spread(place, source):
        bit = place.bit_length() - 1
        before = place - (1 << bit)
        pairs = [
            ((k ^ turned(before, c), k, c), (k ^ turned(place, c), k, c))
            for k, c in everyone
            if needed(k, c, place, bit)
        ]
        return send(source, pairs)

    def collect(bit, message):
        pairs = [
            ((k ^ turned(p, c), k, c), (k ^ turned(p - (1 << bit), c), k, c))
            for k, c in everyone
            for p in range(1 << bit, 2 << bit)
            if needed(k, c, p, bit)
        ]
        return send(message, pairs)

    matrix, diagonal = load(ids, trailing)

    line_of = [(r, k, c) for r in range(count) for k in range(chips) for c in range(2)]

    def step(x, to, wanted):
        return send(x, [((r, k, c), (r, to(k), c)) for r, k, c in line_of if wanted(r, k)])

    def by_distance(block):
        came, places = [block], [lambda chip: (chip, chip >= 0)]
        for by in range(1, chips):
            came.append(step(block, lambda k: (k + by) % chips, lambda r, k: (k + by) % chips <= r))
            places.append(lambda chip, by=by: (lax.rem(chip + chips - by, chips), chip >= 0))
        return came, places

    four = [
        lambda chip: (chip, chip >= 0),
        lambda chip: (chip ^ 2, chip >= 0),
        lambda chip: (jnp.maximum(chip - 1, 0), chip > 0),
        lambda chip: (jnp.minimum(chip + 1, 3), chip < 3),
        lambda chip: (3 - chip, (chip == 0) | (chip == 3)),
    ]

    def two_away(block):
        return step(block, lambda k: k ^ 2, lambda r, k: k >= 2 or k + 2 <= r)

    def next_ones(block):
        up = step(block, lambda k: k + 1, lambda r, k: k + 1 <= r and k < 3)
        return [up, step(block, lambda k: k - 1, lambda r, k: 0 <= k - 1 <= r)]

    def ends(two):
        return step(two, lambda k: 3 * (k - 1), lambda r, k: k == 1 or (k == 2 and r == 3))

    swap = [((r, k, c), (r, k, 1 - c)) for r, k, c in active]

    def widen(panels, after):
        panels[0], panels[1], *_ = lax.optimization_barrier((panels[0], panels[1], *after))
        for place in range(2, count):
            panels.append(spread(place, panels[place - (1 << (place.bit_length() - 1))]))

    def relaying(partial, came, panels, after):
        for bit in reversed(range(bits - 1)):
            partial, message = relay(ids, partial, came, after)
            if panels:
                message, *panels[2:] = lax.optimization_barrier((message, *panels[2:]))
            came = collect(bit, message)
        return partial, came, message

    def deliver(keep, got, partial, came, after):
        own, *out = pack(ids, keep, got, partial, came, chips, after)
        arrays = [own]
        for step, x in enumerate(out):
            pairs = []
            for r, k, c in active:
                at = c * chips + (k + step) % chips
                if (at // 2, at % 2) != (k, c):
                    pairs.append(((r, k, c), (r, at // 2, at % 2)))
            arrays.append(send(x, pairs))
        return arrays

    if chips == 4:
        two = two_away(panel_vectors)
        came, places = [panel_vectors, two, *next_ones(panel_vectors)], four
        two, matrix = lax.optimization_barrier((two, matrix))
        came.append(ends(two))
    else:
        came, places = by_distance(panel_vectors)
    mine = line(ids, came, places, [])
    other = send(mine, swap)
    panels_a, panels_b = ([x] for x in half(ids, mine, other, piece))
    panels_a.append(spread(1, panels_a[0]))
    partial_a, message_a = mirrored_product(ids, matrix, diagonal, mine, other, piece, 0, [])
    to_a = collect(bits - 1, message_a)
    partial_b, message_b = mirrored_product(ids, matrix, diagonal, mine, other, piece, 1, [message_a])
    to_b = collect(bits - 1, message_b)
    widen(panels_a, [message_b])
    panels_b.append(spread(1, panels_b[0]))
    partial_a, to_a, relayed = relaying(partial_a, to_a, [], [message_b])
    keep_a, *give_a = direct_product(ids, matrix, panels_a, [relayed])
    got_a = [send(x, swap) for x in give_a]
    partial_b, to_b, relayed = relaying(partial_b, to_b, [], [keep_a, to_a])
    widen(panels_b, [])
    arrays_a = deliver(keep_a, got_a, partial_a, to_a, [relayed])
    *give_b, panel_b = give_product(ids, matrix, panels_b, [arrays_a[0]])
    give_b, to_b, *arrays_a[1:3] = lax.optimization_barrier((give_b, to_b, *arrays_a[1:3]))
    got_b = [send(x, swap) for x in give_b]
    keep_b = keep_product(ids, matrix, panel_b, [])
    arrays_b = deliver(keep_b, got_b, partial_b, to_b, [])
    result = finish(ids, None, arrays_a, [arrays_b[0]])
    return finish(ids, result, arrays_b, [])


def solution(mesh):
    in_specs = (P("row", "col"), P(("row", "col"), None))
    out_specs = P(("row", "col"), None)
    return jax.shard_map(shards, mesh=mesh, in_specs=in_specs, out_specs=out_specs, check_vma=False)
```

```python
import functools

import jax
import jax.numpy as jnp
from jax import lax
from jax.experimental import pallas as pl
from jax.experimental.pallas import tpu as pltpu
from jax.sharding import PartitionSpec as P

TOP = 1400.0
TAIL = 16
VMEM = 6 * 2**20


def scale_for(largest):
    scale = TOP / jnp.maximum(largest, 1e-30)
    return scale.astype(jnp.bfloat16).astype(jnp.float32)


def encode(values, scale):
    x = values * scale
    x2 = x * x
    x4 = x2 * x2
    return (x * jnp.abs(x) * x2 * (x4 * x4)).astype(jnp.bfloat16)


def decode(coded, scale):
    y = coded.astype(jnp.float32)
    back = jnp.where(scale > 0, 1.0 / scale, 0.0)
    return y * jnp.exp2(-11 / 12 * jnp.log2(jnp.maximum(jnp.abs(y), 2.0**-126))) * back


def scale_of(message, rows, block):
    return message[pl.ds(rows + block * TAIL, TAIL), :][0:1, 0:1].astype(jnp.float32)


def put_scale(message, rows, block, scale):
    spread = jnp.full((TAIL, message.shape[1]), scale, jnp.float32).astype(jnp.bfloat16)
    message[pl.ds(rows + block * TAIL, TAIL), :] = spread


def local(kernel, out_shape, name, *operands, after=(), **options):
    count, skipped = len(operands), len(after)

    def body(*refs):
        kernel(*refs[:count], *refs[count + skipped :])

    return pl.pallas_call(
        body,
        out_shape=out_shape,
        in_specs=[pl.BlockSpec(memory_space=pltpu.SMEM)]
        + [pl.BlockSpec(memory_space=pltpu.VMEM)] * (count - 1)
        + [pl.BlockSpec(memory_space=pl.ANY)] * skipped,
        out_specs=jax.tree.map(lambda _: pl.BlockSpec(memory_space=pltpu.VMEM), out_shape),
        compiler_params=pltpu.CompilerParams(vmem_limit_bytes=VMEM),
        name=name,
        **options,
    )(*operands, *after)


def load_kernel(ids, a_ref, out_ref, diagonal, sem):
    height, cols = a_ref.shape
    block = cols // 4
    diagonal[...] = jnp.zeros_like(diagonal)

    @pl.when(ids[1] <= ids[0])
    def _():
        copy = pltpu.make_async_copy(a_ref, out_ref, sem)
        copy.start()
        copy.wait()

    for part in range(4):
        here = pl.ds(part * block, block)

        @pl.when(ids[1] == ids[0])
        def _():
            @pl.loop(0, height // block)
            def _(at):
                first = ids[3] + at * block
                rows = pl.ds(pl.multiple_of(at * block, block), block)

                @pl.when(first < part * block)
                def _():
                    out_ref[rows, here] = jnp.zeros((block, block), out_ref.dtype)

                @pl.when(first == part * block)
                def _():
                    tile = out_ref[rows, here]
                    empty = jnp.zeros_like(tile)
                    row = lax.broadcasted_iota(jnp.int32, tile.shape, 0)
                    col = lax.broadcasted_iota(jnp.int32, tile.shape, 1)
                    out_ref[rows, here] = jnp.where(row >= col, tile, empty)
                    on = jnp.where(row == col, tile, empty).astype(jnp.float32)
                    diagonal[:, here] = jnp.broadcast_to(jnp.sum(on, axis=0, keepdims=True), (8, block))


def load(ids, trailing):
    return pl.pallas_call(
        load_kernel,
        out_shape=[
            jax.ShapeDtypeStruct(trailing.shape, trailing.dtype),
            jax.ShapeDtypeStruct((8, trailing.shape[1]), jnp.float32),
        ],
        in_specs=[pl.BlockSpec(memory_space=pltpu.SMEM), pl.BlockSpec(memory_space=pltpu.HBM)],
        out_specs=[pl.BlockSpec(memory_space=pltpu.VMEM)] * 2,
        scratch_shapes=[pltpu.SemaphoreType.DMA],
        compiler_params=pltpu.CompilerParams(vmem_limit_bytes=VMEM),
        name="load",
    )(ids, trailing)


def line_kernel(places, ids, *refs):
    *came, out_ref = refs
    height = came[0].shape[0]
    for place, piece in zip(places, came):
        chip, there = place(ids[1])

        @pl.when(there)
        def _():
            out_ref[pl.ds(pl.multiple_of(chip * height, height), height), :] = piece[...]


def line(ids, came, places, after):
    height, width = came[0].shape
    chips = 4 if len(came) == 5 else len(came)
    out_shape = jax.ShapeDtypeStruct((height * chips, width), came[0].dtype)
    return local(functools.partial(line_kernel, places), out_shape, "line", ids, *came, after=after)


def half_kernel(height, ids, mine, other, *outs):
    rows, width = outs[0].shape
    count = rows // height
    for at in range(count // 2):
        chip = ids[2] * (count // 2) + at
        here = pl.ds(pl.multiple_of(chip * height, height), height)
        for core, ref in ((ids[2], mine), (1 - ids[2], other)):
            to = pl.ds(pl.multiple_of((2 * at + core) * height, height), height)
            for part, out_ref in enumerate(outs):
                out_ref[to, :] = ref[here, pl.ds(part * width, width)]


def half(ids, mine, other, height):
    rows, width = mine.shape
    out_shape = [jax.ShapeDtypeStruct((rows, width // 2), mine.dtype)] * 2
    return local(functools.partial(half_kernel, height), out_shape, "half", ids, mine, other)


def mirrored_kernel(piece, part_at, ids, a_ref, diagonal, mine, other, m_ref, msg_ref, turned):
    height, cols = a_ref.shape
    block = cols // 4
    used = ids[1] <= ids[0]
    these = pl.ds(part_at * m_ref.shape[1], m_ref.shape[1])

    @pl.loop(0, height // piece // 2)
    def _(at):
        rows = pl.ds(pl.multiple_of(at * piece, piece), piece)
        for core, ref in ((ids[2], mine), (1 - ids[2], other)):
            turned[:, pl.ds(pl.multiple_of((2 * at + core) * piece, piece), piece)] = ref[rows, these].T

    @pl.loop(0, 4)
    def _(part):
        here = pl.ds(pl.multiple_of(part * block, block), block)

        @pl.when(used)
        def _():
            m_ref[here, :] = jnp.dot(turned[...], a_ref[:, here], preferred_element_type=jnp.float32).T

        @pl.when(jnp.logical_not(used))
        def _():
            m_ref[here, :] = jnp.zeros((block, m_ref.shape[1]), jnp.float32)

        @pl.when(ids[1] == ids[0])
        def _():
            rows = pl.ds(pl.multiple_of(part * block - ids[3], block), block)
            m_ref[here, :] -= (turned[:, rows].astype(jnp.float32) * diagonal[0:1, here]).T

        total = m_ref[here, :]
        scale = scale_for(jnp.max(jnp.abs(total), keepdims=True))
        msg_ref[here, :] = encode(total, scale)
        put_scale(msg_ref, cols, part, scale)


def mirrored_product(ids, matrix, diagonal, mine, other, piece, part_at, after):
    rows, cols = matrix.shape
    width = mine.shape[1] // 2
    out_shape = [
        jax.ShapeDtypeStruct((cols, width), jnp.float32),
        jax.ShapeDtypeStruct((cols + 4 * TAIL, width), jnp.bfloat16),
    ]
    return local(
        functools.partial(mirrored_kernel, piece, part_at), out_shape, "mirrored_product",
        ids, matrix, diagonal, mine, other, after=after,
        scratch_shapes=[pltpu.VMEM((width, rows), jnp.bfloat16)],
    )


def relay_kernel(ids, m_ref, in_ref, sum_ref, msg_ref):
    rows, width = m_ref.shape
    height = rows // 4

    @pl.loop(0, 4)
    def _(part):
        at = pl.ds(pl.multiple_of(part * height, height), height)
        total = m_ref[at, :] + decode(in_ref[at, :], scale_of(in_ref, rows, part))
        scale = scale_for(jnp.max(jnp.abs(total), keepdims=True))
        sum_ref[at, :] = total
        msg_ref[at, :] = encode(total, scale)
        put_scale(msg_ref, rows, part, scale)


def relay(ids, partial, message, after):
    out_shape = [jax.ShapeDtypeStruct(x.shape, x.dtype) for x in (partial, message)]
    return local(relay_kernel, out_shape, "relay", ids, partial, message, after=after)


def pick(ids, panels, panel, sem):
    for place, ref in enumerate(panels):

        @pl.when(ids[4] == place)
        def _():
            copy = pltpu.make_async_copy(ref, panel, sem)
            copy.start()
            copy.wait()


def direct_kernel(ids, a_ref, *refs):
    *panels, keep_ref, give_ref, give_too, panel, sem = refs
    pick(ids, panels, panel, sem)
    rows_kernel(ids, a_ref, panel, give_ref, core=1 - ids[2], of=2)
    rows_kernel(ids, a_ref, panel, give_too, core=1 - ids[2], at=1, of=2)
    rows_kernel(ids, a_ref, panel, keep_ref)


def rows_kernel(ids, a_ref, panel, out_ref, core=None, at=0, of=1):
    core = ids[2] if core is None else core
    rows = out_ref.shape[0]
    height = rows * of // 4
    skip = at * rows

    @pl.when(ids[1] <= ids[0])
    def _():
        @pl.loop(0, 4 // of)
        def _(part):
            at = pl.ds(pl.multiple_of(core * rows * of + skip + part * height, height), height)
            to = pl.ds(pl.multiple_of(part * height, height), height)
            out_ref[to, :] = jnp.dot(a_ref[at, :], panel[...], preferred_element_type=jnp.float32)


def direct_product(ids, matrix, panels, after):
    rows, cols = matrix.shape
    width = panels[0].shape[1]
    out_shape = [jax.ShapeDtypeStruct((rows // parts, width), jnp.float32) for parts in (2, 4, 4)]
    return local(
        direct_kernel, out_shape, "direct_product", ids, matrix, *panels, after=after,
        scratch_shapes=[pltpu.VMEM((cols, width), jnp.bfloat16), pltpu.SemaphoreType.DMA],
    )


def pack_kernel(count, ids, a_ref, *refs):
    theirs, (sum_ref, in_ref, own_ref, *msgs, total) = refs[:count], refs[count:]
    height = own_ref.shape[0]
    rounds = len(msgs)
    rows = rounds * height
    tile = rows // 4
    chip, core = ids[1], ids[2]

    for part in range(4):
        at = pl.ds(part * tile, tile)
        b_ref, where = theirs[part * count // 4], part * tile % theirs[0].shape[0]
        total[at, :] = a_ref[at, :] + b_ref[pl.ds(where, tile), :]

    @pl.when(ids[0] == chip)
    def _():
        @pl.loop(0, 4)
        def _(part):
            at = pl.ds(pl.multiple_of(part * tile, tile), tile)
            total[at, :] += sum_ref[at, :] + decode(in_ref[at, :], scale_of(in_ref, rows, part))

    for step, msg in enumerate(msgs):
        at = pl.ds(pl.multiple_of(lax.rem(chip + step, rounds) * height, height), height)
        values = total[at, :]
        scale = scale_for(jnp.max(jnp.abs(values), keepdims=True))
        msg[pl.ds(0, height), :] = encode(values, scale)
        put_scale(msg, height, 0, scale)

    stays = (chip <= ids[0]) & (lax.div(chip, rounds // 2) == core)

    @pl.when(stays)
    def _():
        place = 2 * lax.rem(chip, rounds // 2) + core
        own_ref[...] = total[pl.ds(pl.multiple_of(place * height, height), height), :]

    @pl.when(jnp.logical_not(stays))
    def _():
        own_ref[...] = jnp.zeros_like(own_ref)


def pack(ids, mine, theirs, partial, message, rounds, after):
    rows, width = mine.shape
    height = rows // rounds
    out_shape = [
        jax.ShapeDtypeStruct((height, width), jnp.float32),
        *[jax.ShapeDtypeStruct((height + TAIL, width), jnp.bfloat16)] * rounds,
    ]
    return local(
        functools.partial(pack_kernel, len(theirs)), out_shape, "pack", ids, mine, *theirs, partial, message, after=after,
        scratch_shapes=[pltpu.VMEM((rows, width), jnp.float32)],
    )


def finish_kernel(ids, before, own, *refs):
    *messages, out_ref = refs
    height, width = own.shape
    total = own[...]
    for message in messages:
        total += decode(message[pl.ds(0, height), :], scale_of(message, height, 0))
    done = out_ref.shape[1] - width
    if done:
        out_ref[:, pl.ds(0, done)] = before[:, pl.ds(0, done)]
    out_ref[:, pl.ds(done, width)] = total


def finish(ids, before, arrays, after):
    height, width = arrays[0].shape
    done = 0 if before is None else before.shape[1]
    out_shape = jax.ShapeDtypeStruct((height, done + width), jnp.float32)
    return local(finish_kernel, out_shape, "finish", ids, arrays[0] if before is None else before, *arrays, after=after)


def shards(trailing, panel_vectors):
    rows_here, cols_here = trailing.shape
    piece = panel_vectors.shape[0]
    count = lax.axis_size("row")
    devices_along = lax.axis_size("col")
    chips = devices_along // 2
    bits = count.bit_length() - 1
    row, col = lax.axis_index("row"), lax.axis_index("col")
    chip, core = col // 2, col % 2

    def at(row, chip, core):
        return (row * chips + chip) * 2 + core

    def turned(place, core):
        if core == 0:
            return place
        return sum(((place >> b) & 1) << (bits - 1 - b) for b in range(bits))

    def send(x, pairs):
        return lax.ppermute(x, ("row", "col"), [(at(*s), at(*d)) for s, d in pairs])

    offset = row ^ chip
    reverse = sum(((offset >> b) & 1) << (bits - 1 - b) for b in range(bits))
    place = jnp.where(core == 0, offset, reverse)
    ids = jnp.stack([row, chip, core, row * rows_here - col * cols_here, place]).astype(jnp.int32)

    def needed(chip, core, place, bit):
        rest = range(0, count, 2 ** (bit + 1))
        return any(chip ^ turned(place | r, core) > chip for r in rest)

    everyone = [(k, c) for k in range(chips) for c in range(2)]

    active = [(r, k, c) for r in range(count) for k in range(r + 1) for c in range(2)]

    def spread(place, source):
        bit = place.bit_length() - 1
        before = place - (1 << bit)
        pairs = [
            ((k ^ turned(before, c), k, c), (k ^ turned(place, c), k, c))
            for k, c in everyone
            if needed(k, c, place, bit)
        ]
        return send(source, pairs)

    def collect(bit, message):
        pairs = [
            ((k ^ turned(p, c), k, c), (k ^ turned(p - (1 << bit), c), k, c))
            for k, c in everyone
            for p in range(1 << bit, 2 << bit)
            if needed(k, c, p, bit)
        ]
        return send(message, pairs)

    matrix, diagonal = load(ids, trailing)

    line_of = [(r, k, c) for r in range(count) for k in range(chips) for c in range(2)]

    def step(x, to, wanted):
        return send(x, [((r, k, c), (r, to(k), c)) for r, k, c in line_of if wanted(r, k)])

    def by_distance(block):
        came, places = [block], [lambda chip: (chip, chip >= 0)]
        for by in range(1, chips):
            came.append(step(block, lambda k: (k + by) % chips, lambda r, k: (k + by) % chips <= r))
            places.append(lambda chip, by=by: (lax.rem(chip + chips - by, chips), chip >= 0))
        return came, places

    four = [
        lambda chip: (chip, chip >= 0),
        lambda chip: (chip ^ 2, chip >= 0),
        lambda chip: (jnp.maximum(chip - 1, 0), chip > 0),
        lambda chip: (jnp.minimum(chip + 1, 3), chip < 3),
        lambda chip: (3 - chip, (chip == 0) | (chip == 3)),
    ]

    def two_away(block):
        return step(block, lambda k: k ^ 2, lambda r, k: k >= 2 or k + 2 <= r)

    def next_ones(block):
        up = step(block, lambda k: k + 1, lambda r, k: k + 1 <= r and k < 3)
        return [up, step(block, lambda k: k - 1, lambda r, k: 0 <= k - 1 <= r)]

    def ends(two):
        return step(two, lambda k: 3 * (k - 1), lambda r, k: k == 1 or (k == 2 and r == 3))

    swap = [((r, k, c), (r, k, 1 - c)) for r, k, c in active]

    def widen(panels, after):
        panels[0], panels[1], *_ = lax.optimization_barrier((panels[0], panels[1], *after))
        for place in range(2, count):
            panels.append(spread(place, panels[place - (1 << (place.bit_length() - 1))]))

    def relaying(partial, came, panels, after):
        for bit in reversed(range(bits - 1)):
            partial, message = relay(ids, partial, came, after)
            if panels:
                message, *panels[2:] = lax.optimization_barrier((message, *panels[2:]))
            came = collect(bit, message)
        return partial, came, message

    def deliver(keep, got, partial, came, after):
        own, *out = pack(ids, keep, got, partial, came, chips, after)
        arrays = [own]
        for step, x in enumerate(out):
            pairs = []
            for r, k, c in active:
                at = c * chips + (k + step) % chips
                if (at // 2, at % 2) != (k, c):
                    pairs.append(((r, k, c), (r, at // 2, at % 2)))
            arrays.append(send(x, pairs))
        return arrays

    if chips == 4:
        two = two_away(panel_vectors)
        came, places = [panel_vectors, two, *next_ones(panel_vectors)], four
        two, matrix = lax.optimization_barrier((two, matrix))
        came.append(ends(two))
    else:
        came, places = by_distance(panel_vectors)
    mine = line(ids, came, places, [])
    other = send(mine, swap)
    panels_a, panels_b = ([x] for x in half(ids, mine, other, piece))
    panels_a.append(spread(1, panels_a[0]))
    panels_b.append(spread(1, panels_b[0]))
    partial_a, message_a = mirrored_product(ids, matrix, diagonal, mine, other, piece, 0, [])
    to_a = collect(bits - 1, message_a)
    partial_b, message_b = mirrored_product(ids, matrix, diagonal, mine, other, piece, 1, [message_a])
    to_b = collect(bits - 1, message_b)
    widen(panels_a, [message_b, panels_b[1]])
    widen(panels_b, [panels_a[1]])
    partial_a, to_a, relayed = relaying(partial_a, to_a, [], [message_b])
    keep_a, *give_a = direct_product(ids, matrix, panels_a, [relayed])
    got_a = [send(x, swap) for x in give_a]
    keep_b, *give_b = direct_product(ids, matrix, panels_b, [keep_a])
    got_b = [send(x, swap) for x in give_b]
    partial_b, to_b, relayed = relaying(partial_b, to_b, [], [keep_b, to_a])
    arrays_a = deliver(keep_a, got_a, partial_a, to_a, [relayed])
    keep_b, *arrays_a[1:3] = lax.optimization_barrier((keep_b, *arrays_a[1:3]))
    arrays_b = deliver(keep_b, got_b, partial_b, to_b, [])
    result = finish(ids, None, arrays_a, [arrays_b[0]])
    return finish(ids, result, arrays_b, [])


def solution(mesh):
    in_specs = (P("row", "col"), P(("row", "col"), None))
    out_specs = P(("row", "col"), None)
    return jax.shard_map(shards, mesh=mesh, in_specs=in_specs, out_specs=out_specs, check_vma=False)
```

```python
import functools

import jax
import jax.numpy as jnp
from jax import lax
from jax.experimental import pallas as pl
from jax.experimental.pallas import tpu as pltpu
from jax.sharding import PartitionSpec as P

TOP = 1400.0
TAIL = 16
VMEM = 6 * 2**20


def scale_for(largest):
    scale = TOP / jnp.maximum(largest, 1e-30)
    return scale.astype(jnp.bfloat16).astype(jnp.float32)


def encode(values, scale):
    x = values * scale
    x2 = x * x
    x4 = x2 * x2
    return (x * jnp.abs(x) * x2 * (x4 * x4)).astype(jnp.bfloat16)


def decode(coded, scale):
    y = coded.astype(jnp.float32)
    back = jnp.where(scale > 0, 1.0 / scale, 0.0)
    return y * jnp.exp2(-11 / 12 * jnp.log2(jnp.maximum(jnp.abs(y), 2.0**-126))) * back


def scale_of(message, rows, block):
    return message[pl.ds(rows + block * TAIL, TAIL), :][0:1, 0:1].astype(jnp.float32)


def put_scale(message, rows, block, scale):
    spread = jnp.full((TAIL, message.shape[1]), scale, jnp.float32).astype(jnp.bfloat16)
    message[pl.ds(rows + block * TAIL, TAIL), :] = spread


def local(kernel, out_shape, name, *operands, after=(), **options):
    count, skipped = len(operands), len(after)

    def body(*refs):
        kernel(*refs[:count], *refs[count + skipped :])

    return pl.pallas_call(
        body,
        out_shape=out_shape,
        in_specs=[pl.BlockSpec(memory_space=pltpu.SMEM)]
        + [pl.BlockSpec(memory_space=pltpu.VMEM)] * (count - 1)
        + [pl.BlockSpec(memory_space=pl.ANY)] * skipped,
        out_specs=jax.tree.map(lambda _: pl.BlockSpec(memory_space=pltpu.VMEM), out_shape),
        compiler_params=pltpu.CompilerParams(vmem_limit_bytes=VMEM),
        name=name,
        **options,
    )(*operands, *after)


def load_kernel(ids, a_ref, out_ref, diagonal, sem):
    height, cols = a_ref.shape
    block = cols // 4
    diagonal[...] = jnp.zeros_like(diagonal)

    @pl.when(ids[1] <= ids[0])
    def _():
        copy = pltpu.make_async_copy(a_ref, out_ref, sem)
        copy.start()
        copy.wait()

    for part in range(4):
        here = pl.ds(part * block, block)

        @pl.when(ids[1] == ids[0])
        def _():
            @pl.loop(0, height // block)
            def _(at):
                first = ids[3] + at * block
                rows = pl.ds(pl.multiple_of(at * block, block), block)

                @pl.when(first < part * block)
                def _():
                    out_ref[rows, here] = jnp.zeros((block, block), out_ref.dtype)

                @pl.when(first == part * block)
                def _():
                    tile = out_ref[rows, here]
                    empty = jnp.zeros_like(tile)
                    row = lax.broadcasted_iota(jnp.int32, tile.shape, 0)
                    col = lax.broadcasted_iota(jnp.int32, tile.shape, 1)
                    out_ref[rows, here] = jnp.where(row >= col, tile, empty)
                    on = jnp.where(row == col, tile, empty).astype(jnp.float32)
                    diagonal[:, here] = jnp.broadcast_to(jnp.sum(on, axis=0, keepdims=True), (8, block))


def load(ids, trailing):
    return pl.pallas_call(
        load_kernel,
        out_shape=[
            jax.ShapeDtypeStruct(trailing.shape, trailing.dtype),
            jax.ShapeDtypeStruct((8, trailing.shape[1]), jnp.float32),
        ],
        in_specs=[pl.BlockSpec(memory_space=pltpu.SMEM), pl.BlockSpec(memory_space=pltpu.HBM)],
        out_specs=[pl.BlockSpec(memory_space=pltpu.VMEM)] * 2,
        scratch_shapes=[pltpu.SemaphoreType.DMA],
        compiler_params=pltpu.CompilerParams(vmem_limit_bytes=VMEM),
        name="load",
    )(ids, trailing)


def line_kernel(places, ids, *refs):
    *came, out_ref = refs
    height = came[0].shape[0]
    for place, piece in zip(places, came):
        chip, there = place(ids[1])

        @pl.when(there)
        def _():
            out_ref[pl.ds(pl.multiple_of(chip * height, height), height), :] = piece[...]


def line(ids, came, places, after):
    height, width = came[0].shape
    chips = 4 if len(came) == 5 else len(came)
    out_shape = jax.ShapeDtypeStruct((height * chips, width), came[0].dtype)
    return local(functools.partial(line_kernel, places), out_shape, "line", ids, *came, after=after)


def half_kernel(height, ids, mine, other, *outs):
    rows, width = outs[0].shape
    count = rows // height
    for at in range(count // 2):
        chip = ids[2] * (count // 2) + at
        here = pl.ds(pl.multiple_of(chip * height, height), height)
        for core, ref in ((ids[2], mine), (1 - ids[2], other)):
            to = pl.ds(pl.multiple_of((2 * at + core) * height, height), height)
            for part, out_ref in enumerate(outs):
                out_ref[to, :] = ref[here, pl.ds(part * width, width)]


def half(ids, mine, other, height):
    rows, width = mine.shape
    out_shape = [jax.ShapeDtypeStruct((rows, width // 2), mine.dtype)] * 2
    return local(functools.partial(half_kernel, height), out_shape, "half", ids, mine, other)


def mirrored_kernel(piece, part_at, ids, a_ref, diagonal, mine, other, m_ref, msg_ref, turned):
    height, cols = a_ref.shape
    block = cols // 4
    used = ids[1] <= ids[0]
    these = pl.ds(part_at * m_ref.shape[1], m_ref.shape[1])

    @pl.loop(0, height // piece // 2)
    def _(at):
        rows = pl.ds(pl.multiple_of(at * piece, piece), piece)
        for core, ref in ((ids[2], mine), (1 - ids[2], other)):
            turned[:, pl.ds(pl.multiple_of((2 * at + core) * piece, piece), piece)] = ref[rows, these].T

    @pl.loop(0, 4)
    def _(part):
        here = pl.ds(pl.multiple_of(part * block, block), block)

        @pl.when(used)
        def _():
            m_ref[here, :] = jnp.dot(turned[...], a_ref[:, here], preferred_element_type=jnp.float32).T

        @pl.when(jnp.logical_not(used))
        def _():
            m_ref[here, :] = jnp.zeros((block, m_ref.shape[1]), jnp.float32)

        @pl.when(ids[1] == ids[0])
        def _():
            rows = pl.ds(pl.multiple_of(part * block - ids[3], block), block)
            m_ref[here, :] -= (turned[:, rows].astype(jnp.float32) * diagonal[0:1, here]).T

        total = m_ref[here, :]
        scale = scale_for(jnp.max(jnp.abs(total), keepdims=True))
        msg_ref[here, :] = encode(total, scale)
        put_scale(msg_ref, cols, part, scale)


def mirrored_product(ids, matrix, diagonal, mine, other, piece, part_at, after):
    rows, cols = matrix.shape
    width = mine.shape[1] // 2
    out_shape = [
        jax.ShapeDtypeStruct((cols, width), jnp.float32),
        jax.ShapeDtypeStruct((cols + 4 * TAIL, width), jnp.bfloat16),
    ]
    return local(
        functools.partial(mirrored_kernel, piece, part_at), out_shape, "mirrored_product",
        ids, matrix, diagonal, mine, other, after=after,
        scratch_shapes=[pltpu.VMEM((width, rows), jnp.bfloat16)],
    )


def relay_kernel(ids, m_ref, in_ref, sum_ref, msg_ref):
    rows, width = m_ref.shape
    height = rows // 4

    @pl.loop(0, 4)
    def _(part):
        at = pl.ds(pl.multiple_of(part * height, height), height)
        total = m_ref[at, :] + decode(in_ref[at, :], scale_of(in_ref, rows, part))
        scale = scale_for(jnp.max(jnp.abs(total), keepdims=True))
        sum_ref[at, :] = total
        msg_ref[at, :] = encode(total, scale)
        put_scale(msg_ref, rows, part, scale)


def relay(ids, partial, message, after):
    out_shape = [jax.ShapeDtypeStruct(x.shape, x.dtype) for x in (partial, message)]
    return local(relay_kernel, out_shape, "relay", ids, partial, message, after=after)


def pick(ids, panels, panel, sem):
    for place, ref in enumerate(panels):

        @pl.when(ids[4] == place)
        def _():
            copy = pltpu.make_async_copy(ref, panel, sem)
            copy.start()
            copy.wait()


def direct_kernel(ids, a_ref, *refs):
    *panels, keep_ref, give_ref, give_too, panel, sem = refs
    pick(ids, panels, panel, sem)
    rows_kernel(ids, a_ref, panel, give_ref, core=1 - ids[2], of=2)
    rows_kernel(ids, a_ref, panel, give_too, core=1 - ids[2], at=1, of=2)
    rows_kernel(ids, a_ref, panel, keep_ref)


def rows_kernel(ids, a_ref, panel, out_ref, core=None, at=0, of=1):
    core = ids[2] if core is None else core
    rows = out_ref.shape[0]
    height = rows * of // 4
    skip = at * rows

    @pl.when(ids[1] <= ids[0])
    def _():
        @pl.loop(0, 4 // of)
        def _(part):
            at = pl.ds(pl.multiple_of(core * rows * of + skip + part * height, height), height)
            to = pl.ds(pl.multiple_of(part * height, height), height)
            out_ref[to, :] = jnp.dot(a_ref[at, :], panel[...], preferred_element_type=jnp.float32)


def direct_product(ids, matrix, panels, after):
    rows, cols = matrix.shape
    width = panels[0].shape[1]
    out_shape = [jax.ShapeDtypeStruct((rows // parts, width), jnp.float32) for parts in (2, 4, 4)]
    return local(
        direct_kernel, out_shape, "direct_product", ids, matrix, *panels, after=after,
        scratch_shapes=[pltpu.VMEM((cols, width), jnp.bfloat16), pltpu.SemaphoreType.DMA],
    )


def pack_kernel(count, ids, a_ref, *refs):
    theirs, (sum_ref, in_ref, own_ref, *msgs, total) = refs[:count], refs[count:]
    height = own_ref.shape[0]
    rounds = len(msgs)
    rows = rounds * height
    tile = rows // 4
    chip, core = ids[1], ids[2]

    for part in range(4):
        at = pl.ds(part * tile, tile)
        b_ref, where = theirs[part * count // 4], part * tile % theirs[0].shape[0]
        total[at, :] = a_ref[at, :] + b_ref[pl.ds(where, tile), :]

    @pl.when(ids[0] == chip)
    def _():
        @pl.loop(0, 4)
        def _(part):
            at = pl.ds(pl.multiple_of(part * tile, tile), tile)
            total[at, :] += sum_ref[at, :] + decode(in_ref[at, :], scale_of(in_ref, rows, part))

    for step, msg in enumerate(msgs):
        at = pl.ds(pl.multiple_of(lax.rem(chip + step, rounds) * height, height), height)
        values = total[at, :]
        scale = scale_for(jnp.max(jnp.abs(values), keepdims=True))
        msg[pl.ds(0, height), :] = encode(values, scale)
        put_scale(msg, height, 0, scale)

    stays = (chip <= ids[0]) & (lax.div(chip, rounds // 2) == core)

    @pl.when(stays)
    def _():
        place = 2 * lax.rem(chip, rounds // 2) + core
        own_ref[...] = total[pl.ds(pl.multiple_of(place * height, height), height), :]

    @pl.when(jnp.logical_not(stays))
    def _():
        own_ref[...] = jnp.zeros_like(own_ref)


def pack(ids, mine, theirs, partial, message, rounds, after):
    rows, width = mine.shape
    height = rows // rounds
    out_shape = [
        jax.ShapeDtypeStruct((height, width), jnp.float32),
        *[jax.ShapeDtypeStruct((height + TAIL, width), jnp.bfloat16)] * rounds,
    ]
    return local(
        functools.partial(pack_kernel, len(theirs)), out_shape, "pack", ids, mine, *theirs, partial, message, after=after,
        scratch_shapes=[pltpu.VMEM((rows, width), jnp.float32)],
    )


def finish_kernel(ids, before, own, *refs):
    *messages, out_ref = refs
    height, width = own.shape
    total = own[...]
    for message in messages:
        total += decode(message[pl.ds(0, height), :], scale_of(message, height, 0))
    done = out_ref.shape[1] - width
    if done:
        out_ref[:, pl.ds(0, done)] = before[:, pl.ds(0, done)]
    out_ref[:, pl.ds(done, width)] = total


def finish(ids, before, arrays, after):
    height, width = arrays[0].shape
    done = 0 if before is None else before.shape[1]
    out_shape = jax.ShapeDtypeStruct((height, done + width), jnp.float32)
    return local(finish_kernel, out_shape, "finish", ids, arrays[0] if before is None else before, *arrays, after=after)


def shards(trailing, panel_vectors):
    rows_here, cols_here = trailing.shape
    piece = panel_vectors.shape[0]
    count = lax.axis_size("row")
    devices_along = lax.axis_size("col")
    chips = devices_along // 2
    bits = count.bit_length() - 1
    row, col = lax.axis_index("row"), lax.axis_index("col")
    chip, core = col // 2, col % 2

    def at(row, chip, core):
        return (row * chips + chip) * 2 + core

    def turned(place, core):
        if core == 0:
            return place
        return sum(((place >> b) & 1) << (bits - 1 - b) for b in range(bits))

    def send(x, pairs):
        return lax.ppermute(x, ("row", "col"), [(at(*s), at(*d)) for s, d in pairs])

    offset = row ^ chip
    reverse = sum(((offset >> b) & 1) << (bits - 1 - b) for b in range(bits))
    place = jnp.where(core == 0, offset, reverse)
    ids = jnp.stack([row, chip, core, row * rows_here - col * cols_here, place]).astype(jnp.int32)

    def needed(chip, core, place, bit):
        rest = range(0, count, 2 ** (bit + 1))
        return any(chip ^ turned(place | r, core) > chip for r in rest)

    everyone = [(k, c) for k in range(chips) for c in range(2)]

    active = [(r, k, c) for r in range(count) for k in range(r + 1) for c in range(2)]

    def spread(place, source):
        bit = place.bit_length() - 1
        before = place - (1 << bit)
        pairs = [
            ((k ^ turned(before, c), k, c), (k ^ turned(place, c), k, c))
            for k, c in everyone
            if needed(k, c, place, bit)
        ]
        return send(source, pairs)

    def collect(bit, message):
        pairs = [
            ((k ^ turned(p, c), k, c), (k ^ turned(p - (1 << bit), c), k, c))
            for k, c in everyone
            for p in range(1 << bit, 2 << bit)
            if needed(k, c, p, bit)
        ]
        return send(message, pairs)

    matrix, diagonal = load(ids, trailing)

    line_of = [(r, k, c) for r in range(count) for k in range(chips) for c in range(2)]

    def step(x, to, wanted):
        return send(x, [((r, k, c), (r, to(k), c)) for r, k, c in line_of if wanted(r, k)])

    def by_distance(block):
        came, places = [block], [lambda chip: (chip, chip >= 0)]
        for by in range(1, chips):
            came.append(step(block, lambda k: (k + by) % chips, lambda r, k: (k + by) % chips <= r))
            places.append(lambda chip, by=by: (lax.rem(chip + chips - by, chips), chip >= 0))
        return came, places

    four = [
        lambda chip: (chip, chip >= 0),
        lambda chip: (chip ^ 2, chip >= 0),
        lambda chip: (jnp.maximum(chip - 1, 0), chip > 0),
        lambda chip: (jnp.minimum(chip + 1, 3), chip < 3),
        lambda chip: (3 - chip, (chip == 0) | (chip == 3)),
    ]

    def two_away(block):
        return step(block, lambda k: k ^ 2, lambda r, k: k >= 2 or k + 2 <= r)

    def next_ones(block):
        up = step(block, lambda k: k + 1, lambda r, k: k + 1 <= r and k < 3)
        return [up, step(block, lambda k: k - 1, lambda r, k: 0 <= k - 1 <= r)]

    def ends(two):
        return step(two, lambda k: 3 * (k - 1), lambda r, k: k == 1 or (k == 2 and r == 3))

    swap = [((r, k, c), (r, k, 1 - c)) for r, k, c in active]

    def widen(panels, after):
        panels[0], panels[1], *_ = lax.optimization_barrier((panels[0], panels[1], *after))
        for place in range(2, count):
            panels.append(spread(place, panels[place - (1 << (place.bit_length() - 1))]))

    def relaying(partial, came, panels, after):
        for bit in reversed(range(bits - 1)):
            partial, message = relay(ids, partial, came, after)
            if panels:
                message, *panels[2:] = lax.optimization_barrier((message, *panels[2:]))
            came = collect(bit, message)
        return partial, came, message

    def deliver(keep, got, partial, came, after):
        own, *out = pack(ids, keep, got, partial, came, chips, after)
        arrays = [own]
        for step, x in enumerate(out):
            pairs = []
            for r, k, c in active:
                at = c * chips + (k + step) % chips
                if (at // 2, at % 2) != (k, c):
                    pairs.append(((r, k, c), (r, at // 2, at % 2)))
            arrays.append(send(x, pairs))
        return arrays

    if chips == 4:
        two = two_away(panel_vectors)
        came, places = [panel_vectors, two, *next_ones(panel_vectors)], four
        two, matrix = lax.optimization_barrier((two, matrix))
        came.append(ends(two))
    else:
        came, places = by_distance(panel_vectors)
    mine = line(ids, came, places, [])
    other = send(mine, swap)
    panels_a, panels_b = ([x] for x in half(ids, mine, other, piece))
    panels_a.append(spread(1, panels_a[0]))
    panels_b.append(spread(1, panels_b[0]))
    partial_a, message_a = mirrored_product(ids, matrix, diagonal, mine, other, piece, 0, [])
    to_a = collect(bits - 1, message_a)
    partial_b, message_b = mirrored_product(ids, matrix, diagonal, mine, other, piece, 1, [message_a])
    to_b = collect(bits - 1, message_b)
    widen(panels_a, [message_b, panels_b[1]])
    widen(panels_b, [panels_a[1]])
    partial_a, to_a, relayed = relaying(partial_a, to_a, [], [message_b])
    keep_a, *give_a = direct_product(ids, matrix, panels_a, [relayed])
    got_a = [send(x, swap) for x in give_a]
    partial_b, to_b, relayed = relaying(partial_b, to_b, [], [keep_a, to_a, panels_b[2]])
    arrays_a = deliver(keep_a, got_a, partial_a, to_a, [relayed, *panels_b[3:]])
    keep_b, *give_b = direct_product(ids, matrix, panels_b, [arrays_a[0]])
    give_b, to_b, *arrays_a[1:3] = lax.optimization_barrier((give_b, to_b, *arrays_a[1:3]))
    got_b = [send(x, swap) for x in give_b]
    arrays_b = deliver(keep_b, got_b, partial_b, to_b, [])
    result = finish(ids, None, arrays_a, [arrays_b[0]])
    return finish(ids, result, arrays_b, [])


def solution(mesh):
    in_specs = (P("row", "col"), P(("row", "col"), None))
    out_specs = P(("row", "col"), None)
    return jax.shard_map(shards, mesh=mesh, in_specs=in_specs, out_specs=out_specs, check_vma=False)
```

```python
import functools

import jax
import jax.numpy as jnp
from jax import lax
from jax.experimental import pallas as pl
from jax.experimental.pallas import tpu as pltpu
from jax.sharding import PartitionSpec as P

TOP = 1400.0
TAIL = 16
VMEM = 6 * 2**20


def scale_for(largest):
    scale = TOP / jnp.maximum(largest, 1e-30)
    return scale.astype(jnp.bfloat16).astype(jnp.float32)


def encode(values, scale):
    x = values * scale
    x2 = x * x
    x4 = x2 * x2
    return (x * jnp.abs(x) * x2 * (x4 * x4)).astype(jnp.bfloat16)


def decode(coded, scale):
    y = coded.astype(jnp.float32)
    back = jnp.where(scale > 0, 1.0 / scale, 0.0)
    return y * jnp.exp2(-11 / 12 * jnp.log2(jnp.maximum(jnp.abs(y), 2.0**-126))) * back


def scale_of(message, rows, block):
    return message[pl.ds(rows + block * TAIL, TAIL), :][0:1, 0:1].astype(jnp.float32)


def put_scale(message, rows, block, scale):
    spread = jnp.full((TAIL, message.shape[1]), scale, jnp.float32).astype(jnp.bfloat16)
    message[pl.ds(rows + block * TAIL, TAIL), :] = spread


def local(kernel, out_shape, name, *operands, after=(), **options):
    count, skipped = len(operands), len(after)

    def body(*refs):
        kernel(*refs[:count], *refs[count + skipped :])

    return pl.pallas_call(
        body,
        out_shape=out_shape,
        in_specs=[pl.BlockSpec(memory_space=pltpu.SMEM)]
        + [pl.BlockSpec(memory_space=pltpu.VMEM)] * (count - 1)
        + [pl.BlockSpec(memory_space=pl.ANY)] * skipped,
        out_specs=jax.tree.map(lambda _: pl.BlockSpec(memory_space=pltpu.VMEM), out_shape),
        compiler_params=pltpu.CompilerParams(vmem_limit_bytes=VMEM),
        name=name,
        **options,
    )(*operands, *after)


def load_kernel(ids, a_ref, out_ref, diagonal, sem):
    height, cols = a_ref.shape
    block = cols // 4
    diagonal[...] = jnp.zeros_like(diagonal)

    @pl.when(ids[1] <= ids[0])
    def _():
        copy = pltpu.make_async_copy(a_ref, out_ref, sem)
        copy.start()
        copy.wait()

    for part in range(4):
        here = pl.ds(part * block, block)

        @pl.when(ids[1] == ids[0])
        def _():
            @pl.loop(0, height // block)
            def _(at):
                first = ids[3] + at * block
                rows = pl.ds(pl.multiple_of(at * block, block), block)

                @pl.when(first < part * block)
                def _():
                    out_ref[rows, here] = jnp.zeros((block, block), out_ref.dtype)

                @pl.when(first == part * block)
                def _():
                    tile = out_ref[rows, here]
                    empty = jnp.zeros_like(tile)
                    row = lax.broadcasted_iota(jnp.int32, tile.shape, 0)
                    col = lax.broadcasted_iota(jnp.int32, tile.shape, 1)
                    out_ref[rows, here] = jnp.where(row >= col, tile, empty)
                    on = jnp.where(row == col, tile, empty).astype(jnp.float32)
                    diagonal[:, here] = jnp.broadcast_to(jnp.sum(on, axis=0, keepdims=True), (8, block))


def load(ids, trailing):
    return pl.pallas_call(
        load_kernel,
        out_shape=[
            jax.ShapeDtypeStruct(trailing.shape, trailing.dtype),
            jax.ShapeDtypeStruct((8, trailing.shape[1]), jnp.float32),
        ],
        in_specs=[pl.BlockSpec(memory_space=pltpu.SMEM), pl.BlockSpec(memory_space=pltpu.HBM)],
        out_specs=[pl.BlockSpec(memory_space=pltpu.VMEM)] * 2,
        scratch_shapes=[pltpu.SemaphoreType.DMA],
        compiler_params=pltpu.CompilerParams(vmem_limit_bytes=VMEM),
        name="load",
    )(ids, trailing)


def line_kernel(places, ids, *refs):
    *came, out_ref = refs
    height = came[0].shape[0]
    for place, piece in zip(places, came):
        chip, there = place(ids[1])

        @pl.when(there)
        def _():
            out_ref[pl.ds(pl.multiple_of(chip * height, height), height), :] = piece[...]


def line(ids, came, places, after):
    height, width = came[0].shape
    chips = 4 if len(came) == 5 else len(came)
    out_shape = jax.ShapeDtypeStruct((height * chips, width), came[0].dtype)
    return local(functools.partial(line_kernel, places), out_shape, "line", ids, *came, after=after)


def half_kernel(height, ids, mine, other, *outs):
    rows, width = outs[0].shape
    count = rows // height
    for at in range(count // 2):
        chip = ids[2] * (count // 2) + at
        here = pl.ds(pl.multiple_of(chip * height, height), height)
        for core, ref in ((ids[2], mine), (1 - ids[2], other)):
            to = pl.ds(pl.multiple_of((2 * at + core) * height, height), height)
            for part, out_ref in enumerate(outs):
                out_ref[to, :] = ref[here, pl.ds(part * width, width)]


def half(ids, mine, other, height):
    rows, width = mine.shape
    out_shape = [jax.ShapeDtypeStruct((rows, width // 2), mine.dtype)] * 2
    return local(functools.partial(half_kernel, height), out_shape, "half", ids, mine, other)


def mirrored_kernel(piece, part_at, ids, a_ref, diagonal, mine, other, m_ref, msg_ref, turned):
    height, cols = a_ref.shape
    block = cols // 4
    used = ids[1] <= ids[0]
    these = pl.ds(part_at * m_ref.shape[1], m_ref.shape[1])

    @pl.loop(0, height // piece // 2)
    def _(at):
        rows = pl.ds(pl.multiple_of(at * piece, piece), piece)
        for core, ref in ((ids[2], mine), (1 - ids[2], other)):
            turned[:, pl.ds(pl.multiple_of((2 * at + core) * piece, piece), piece)] = ref[rows, these].T

    @pl.loop(0, 4)
    def _(part):
        here = pl.ds(pl.multiple_of(part * block, block), block)

        @pl.when(used)
        def _():
            m_ref[here, :] = jnp.dot(turned[...], a_ref[:, here], preferred_element_type=jnp.float32).T

        @pl.when(jnp.logical_not(used))
        def _():
            m_ref[here, :] = jnp.zeros((block, m_ref.shape[1]), jnp.float32)

        @pl.when(ids[1] == ids[0])
        def _():
            rows = pl.ds(pl.multiple_of(part * block - ids[3], block), block)
            m_ref[here, :] -= (turned[:, rows].astype(jnp.float32) * diagonal[0:1, here]).T

        total = m_ref[here, :]
        scale = scale_for(jnp.max(jnp.abs(total), keepdims=True))
        msg_ref[here, :] = encode(total, scale)
        put_scale(msg_ref, cols, part, scale)


def mirrored_product(ids, matrix, diagonal, mine, other, piece, part_at, after):
    rows, cols = matrix.shape
    width = mine.shape[1] // 2
    out_shape = [
        jax.ShapeDtypeStruct((cols, width), jnp.float32),
        jax.ShapeDtypeStruct((cols + 4 * TAIL, width), jnp.bfloat16),
    ]
    return local(
        functools.partial(mirrored_kernel, piece, part_at), out_shape, "mirrored_product",
        ids, matrix, diagonal, mine, other, after=after,
        scratch_shapes=[pltpu.VMEM((width, rows), jnp.bfloat16)],
    )


def relay_kernel(ids, m_ref, in_ref, sum_ref, msg_ref):
    rows, width = m_ref.shape
    height = rows // 4

    @pl.loop(0, 4)
    def _(part):
        at = pl.ds(pl.multiple_of(part * height, height), height)
        total = m_ref[at, :] + decode(in_ref[at, :], scale_of(in_ref, rows, part))
        scale = scale_for(jnp.max(jnp.abs(total), keepdims=True))
        sum_ref[at, :] = total
        msg_ref[at, :] = encode(total, scale)
        put_scale(msg_ref, rows, part, scale)


def relay(ids, partial, message, after):
    out_shape = [jax.ShapeDtypeStruct(x.shape, x.dtype) for x in (partial, message)]
    return local(relay_kernel, out_shape, "relay", ids, partial, message, after=after)


def pick(ids, panels, panel, sem):
    for place, ref in enumerate(panels):

        @pl.when(ids[4] == place)
        def _():
            copy = pltpu.make_async_copy(ref, panel, sem)
            copy.start()
            copy.wait()


def direct_kernel(ids, a_ref, *refs):
    *panels, keep_ref, give_ref, give_too, panel, sem = refs
    pick(ids, panels, panel, sem)
    rows_kernel(ids, a_ref, panel, give_ref, core=1 - ids[2], of=2)
    rows_kernel(ids, a_ref, panel, give_too, core=1 - ids[2], at=1, of=2)
    rows_kernel(ids, a_ref, panel, keep_ref)


def rows_kernel(ids, a_ref, panel, out_ref, core=None, at=0, of=1):
    core = ids[2] if core is None else core
    rows = out_ref.shape[0]
    height = rows * of // 4
    skip = at * rows

    @pl.when(ids[1] <= ids[0])
    def _():
        @pl.loop(0, 4 // of)
        def _(part):
            at = pl.ds(pl.multiple_of(core * rows * of + skip + part * height, height), height)
            to = pl.ds(pl.multiple_of(part * height, height), height)
            out_ref[to, :] = jnp.dot(a_ref[at, :], panel[...], preferred_element_type=jnp.float32)


def direct_product(ids, matrix, panels, after):
    rows, cols = matrix.shape
    width = panels[0].shape[1]
    out_shape = [jax.ShapeDtypeStruct((rows // parts, width), jnp.float32) for parts in (2, 4, 4)]
    return local(
        direct_kernel, out_shape, "direct_product", ids, matrix, *panels, after=after,
        scratch_shapes=[pltpu.VMEM((cols, width), jnp.bfloat16), pltpu.SemaphoreType.DMA],
    )


def pack_kernel(count, ids, a_ref, *refs):
    theirs, (sum_ref, in_ref, own_ref, *msgs, total) = refs[:count], refs[count:]
    height = own_ref.shape[0]
    rounds = len(msgs)
    rows = rounds * height
    tile = rows // 4
    chip, core = ids[1], ids[2]

    for part in range(4):
        at = pl.ds(part * tile, tile)
        b_ref, where = theirs[part * count // 4], part * tile % theirs[0].shape[0]
        total[at, :] = a_ref[at, :] + b_ref[pl.ds(where, tile), :]

    @pl.when(ids[0] == chip)
    def _():
        @pl.loop(0, 4)
        def _(part):
            at = pl.ds(pl.multiple_of(part * tile, tile), tile)
            total[at, :] += sum_ref[at, :] + decode(in_ref[at, :], scale_of(in_ref, rows, part))

    for step, msg in enumerate(msgs):
        at = pl.ds(pl.multiple_of(lax.rem(chip + step, rounds) * height, height), height)
        values = total[at, :]
        scale = scale_for(jnp.max(jnp.abs(values), keepdims=True))
        msg[pl.ds(0, height), :] = encode(values, scale)
        put_scale(msg, height, 0, scale)

    stays = (chip <= ids[0]) & (lax.div(chip, rounds // 2) == core)

    @pl.when(stays)
    def _():
        place = 2 * lax.rem(chip, rounds // 2) + core
        own_ref[...] = total[pl.ds(pl.multiple_of(place * height, height), height), :]

    @pl.when(jnp.logical_not(stays))
    def _():
        own_ref[...] = jnp.zeros_like(own_ref)


def pack(ids, mine, theirs, partial, message, rounds, after):
    rows, width = mine.shape
    height = rows // rounds
    out_shape = [
        jax.ShapeDtypeStruct((height, width), jnp.float32),
        *[jax.ShapeDtypeStruct((height + TAIL, width), jnp.bfloat16)] * rounds,
    ]
    return local(
        functools.partial(pack_kernel, len(theirs)), out_shape, "pack", ids, mine, *theirs, partial, message, after=after,
        scratch_shapes=[pltpu.VMEM((rows, width), jnp.float32)],
    )


def finish_kernel(ids, before, own, *refs):
    *messages, out_ref = refs
    height, width = own.shape
    total = own[...]
    for message in messages:
        total += decode(message[pl.ds(0, height), :], scale_of(message, height, 0))
    done = out_ref.shape[1] - width
    if done:
        out_ref[:, pl.ds(0, done)] = before[:, pl.ds(0, done)]
    out_ref[:, pl.ds(done, width)] = total


def finish(ids, before, arrays, after):
    height, width = arrays[0].shape
    done = 0 if before is None else before.shape[1]
    out_shape = jax.ShapeDtypeStruct((height, done + width), jnp.float32)
    return local(finish_kernel, out_shape, "finish", ids, arrays[0] if before is None else before, *arrays, after=after)


def shards(trailing, panel_vectors):
    rows_here, cols_here = trailing.shape
    piece = panel_vectors.shape[0]
    count = lax.axis_size("row")
    devices_along = lax.axis_size("col")
    chips = devices_along // 2
    bits = count.bit_length() - 1
    row, col = lax.axis_index("row"), lax.axis_index("col")
    chip, core = col // 2, col % 2

    def at(row, chip, core):
        return (row * chips + chip) * 2 + core

    def turned(place, core):
        if core == 0:
            return place
        return sum(((place >> b) & 1) << (bits - 1 - b) for b in range(bits))

    def send(x, pairs):
        return lax.ppermute(x, ("row", "col"), [(at(*s), at(*d)) for s, d in pairs])

    offset = row ^ chip
    reverse = sum(((offset >> b) & 1) << (bits - 1 - b) for b in range(bits))
    place = jnp.where(core == 0, offset, reverse)
    ids = jnp.stack([row, chip, core, row * rows_here - col * cols_here, place]).astype(jnp.int32)

    def needed(chip, core, place, bit):
        rest = range(0, count, 2 ** (bit + 1))
        return any(chip ^ turned(place | r, core) > chip for r in rest)

    everyone = [(k, c) for k in range(chips) for c in range(2)]

    active = [(r, k, c) for r in range(count) for k in range(r + 1) for c in range(2)]

    def spread(place, source):
        bit = place.bit_length() - 1
        before = place - (1 << bit)
        pairs = [
            ((k ^ turned(before, c), k, c), (k ^ turned(place, c), k, c))
            for k, c in everyone
            if needed(k, c, place, bit)
        ]
        return send(source, pairs)

    def collect(bit, message):
        pairs = [
            ((k ^ turned(p, c), k, c), (k ^ turned(p - (1 << bit), c), k, c))
            for k, c in everyone
            for p in range(1 << bit, 2 << bit)
            if needed(k, c, p, bit)
        ]
        return send(message, pairs)

    matrix, diagonal = load(ids, trailing)

    line_of = [(r, k, c) for r in range(count) for k in range(chips) for c in range(2)]

    def step(x, to, wanted):
        return send(x, [((r, k, c), (r, to(k), c)) for r, k, c in line_of if wanted(r, k)])

    def by_distance(block):
        came, places = [block], [lambda chip: (chip, chip >= 0)]
        for by in range(1, chips):
            came.append(step(block, lambda k: (k + by) % chips, lambda r, k: (k + by) % chips <= r))
            places.append(lambda chip, by=by: (lax.rem(chip + chips - by, chips), chip >= 0))
        return came, places

    four = [
        lambda chip: (chip, chip >= 0),
        lambda chip: (chip ^ 2, chip >= 0),
        lambda chip: (chip ^ 1, chip >= 0),
        lambda chip: (3 - chip, (chip == 0) | (chip == 3)),
        lambda chip: (3 - chip, (chip == 1) | (chip == 2)),
    ]

    swap = [((r, k, c), (r, k, 1 - c)) for r, k, c in active]

    def widen(panels, after):
        panels[0], panels[1], *_ = lax.optimization_barrier((panels[0], panels[1], *after))
        for place in range(2, count):
            panels.append(spread(place, panels[place - (1 << (place.bit_length() - 1))]))

    def relaying(partial, came, panels, after):
        for bit in reversed(range(bits - 1)):
            partial, message = relay(ids, partial, came, after)
            if panels:
                message, *panels[2:] = lax.optimization_barrier((message, *panels[2:]))
            came = collect(bit, message)
        return partial, came, message

    def deliver(keep, got, partial, came, after):
        own, *out = pack(ids, keep, got, partial, came, chips, after)
        arrays = [own]
        for step, x in enumerate(out):
            pairs = []
            for r, k, c in active:
                at = c * chips + (k + step) % chips
                if (at // 2, at % 2) != (k, c):
                    pairs.append(((r, k, c), (r, at // 2, at % 2)))
            arrays.append(send(x, pairs))
        return arrays

    if chips == 4:
        two = step(panel_vectors, lambda k: k ^ 2, lambda r, k: k >= 2 or k + 2 <= r)
        near = step(panel_vectors, lambda k: k ^ 1, lambda r, k: k ^ 1 <= r)
        two, near, own, matrix = lax.optimization_barrier((two, near, panel_vectors, matrix))
        ends = step(two, lambda k: 3 * (k - 1), lambda r, k: k == 1 or (k == 2 and r == 3))
        middle = step(own, lambda k: 3 - k, lambda r, k: k in (1, 2) and 3 - k <= r)
        came, places = [panel_vectors, two, near, ends, middle], four
    else:
        came, places = by_distance(panel_vectors)
    mine = line(ids, came, places, [])
    other = send(mine, swap)
    panels_a, panels_b = ([x] for x in half(ids, mine, other, piece))
    panels_a.append(spread(1, panels_a[0]))
    panels_b.append(spread(1, panels_b[0]))
    partial_a, message_a = mirrored_product(ids, matrix, diagonal, mine, other, piece, 0, [])
    to_a = collect(bits - 1, message_a)
    partial_b, message_b = mirrored_product(ids, matrix, diagonal, mine, other, piece, 1, [message_a])
    to_b = collect(bits - 1, message_b)
    widen(panels_a, [message_b])
    widen(panels_b, [panels_a[1]])
    partial_a, to_a, relayed = relaying(partial_a, to_a, [], [message_b, panels_b[1]])
    keep_a, *give_a = direct_product(ids, matrix, panels_a, [relayed])
    got_a = [send(x, swap) for x in give_a]
    partial_b, to_b, relayed = relaying(partial_b, to_b, [], [keep_a, to_a, panels_b[2]])
    arrays_a = deliver(keep_a, got_a, partial_a, to_a, [relayed, *panels_b[3:]])
    keep_b, *give_b = direct_product(ids, matrix, panels_b, [arrays_a[0]])
    give_b, to_b, *arrays_a[1:3] = lax.optimization_barrier((give_b, to_b, *arrays_a[1:3]))
    got_b = [send(x, swap) for x in give_b]
    arrays_b = deliver(keep_b, got_b, partial_b, to_b, [])
    result = finish(ids, None, arrays_a, [arrays_b[0]])
    return finish(ids, result, arrays_b, [])


def solution(mesh):
    in_specs = (P("row", "col"), P(("row", "col"), None))
    out_specs = P(("row", "col"), None)
    return jax.shard_map(shards, mesh=mesh, in_specs=in_specs, out_specs=out_specs, check_vma=False)
```

```python
import functools

import jax
import jax.numpy as jnp
from jax import lax
from jax.experimental import pallas as pl
from jax.experimental.pallas import tpu as pltpu
from jax.sharding import PartitionSpec as P

TOP = 1400.0
TAIL = 16
VMEM = 6 * 2**20


def scale_for(largest):
    scale = TOP / jnp.maximum(largest, 1e-30)
    return scale.astype(jnp.bfloat16).astype(jnp.float32)


def encode(values, scale):
    x = values * scale
    x2 = x * x
    x4 = x2 * x2
    return (x * jnp.abs(x) * x2 * (x4 * x4)).astype(jnp.bfloat16)


def decode(coded, scale):
    y = coded.astype(jnp.float32)
    back = jnp.where(scale > 0, 1.0 / scale, 0.0)
    return y * jnp.exp2(-11 / 12 * jnp.log2(jnp.maximum(jnp.abs(y), 2.0**-126))) * back


def scale_of(message, rows, block):
    return message[pl.ds(rows + block * TAIL, TAIL), :][0:1, 0:1].astype(jnp.float32)


def put_scale(message, rows, block, scale):
    spread = jnp.full((TAIL, message.shape[1]), scale, jnp.float32).astype(jnp.bfloat16)
    message[pl.ds(rows + block * TAIL, TAIL), :] = spread


def local(kernel, out_shape, name, *operands, after=(), **options):
    count, skipped = len(operands), len(after)

    def body(*refs):
        kernel(*refs[:count], *refs[count + skipped :])

    return pl.pallas_call(
        body,
        out_shape=out_shape,
        in_specs=[pl.BlockSpec(memory_space=pltpu.SMEM)]
        + [pl.BlockSpec(memory_space=pltpu.VMEM)] * (count - 1)
        + [pl.BlockSpec(memory_space=pl.ANY)] * skipped,
        out_specs=jax.tree.map(lambda _: pl.BlockSpec(memory_space=pltpu.VMEM), out_shape),
        compiler_params=pltpu.CompilerParams(vmem_limit_bytes=VMEM),
        name=name,
        **options,
    )(*operands, *after)


def load_kernel(ids, a_ref, out_ref, diagonal, sem):
    height, cols = a_ref.shape
    block = cols // 4
    diagonal[...] = jnp.zeros_like(diagonal)

    @pl.when(ids[1] <= ids[0])
    def _():
        copy = pltpu.make_async_copy(a_ref, out_ref, sem)
        copy.start()
        copy.wait()

    for part in range(4):
        here = pl.ds(part * block, block)

        @pl.when(ids[1] == ids[0])
        def _():
            @pl.loop(0, height // block)
            def _(at):
                first = ids[3] + at * block
                rows = pl.ds(pl.multiple_of(at * block, block), block)

                @pl.when(first < part * block)
                def _():
                    out_ref[rows, here] = jnp.zeros((block, block), out_ref.dtype)

                @pl.when(first == part * block)
                def _():
                    tile = out_ref[rows, here]
                    empty = jnp.zeros_like(tile)
                    row = lax.broadcasted_iota(jnp.int32, tile.shape, 0)
                    col = lax.broadcasted_iota(jnp.int32, tile.shape, 1)
                    out_ref[rows, here] = jnp.where(row >= col, tile, empty)
                    on = jnp.where(row == col, tile, empty).astype(jnp.float32)
                    diagonal[:, here] = jnp.broadcast_to(jnp.sum(on, axis=0, keepdims=True), (8, block))


def load(ids, trailing):
    return pl.pallas_call(
        load_kernel,
        out_shape=[
            jax.ShapeDtypeStruct(trailing.shape, trailing.dtype),
            jax.ShapeDtypeStruct((8, trailing.shape[1]), jnp.float32),
        ],
        in_specs=[pl.BlockSpec(memory_space=pltpu.SMEM), pl.BlockSpec(memory_space=pltpu.HBM)],
        out_specs=[pl.BlockSpec(memory_space=pltpu.VMEM)] * 2,
        scratch_shapes=[pltpu.SemaphoreType.DMA],
        compiler_params=pltpu.CompilerParams(vmem_limit_bytes=VMEM),
        name="load",
    )(ids, trailing)


def line_kernel(places, ids, *refs):
    *came, out_ref = refs
    height = came[0].shape[0]
    for place, piece in zip(places, came):
        chip, there = place(ids[1])

        @pl.when(there)
        def _():
            out_ref[pl.ds(pl.multiple_of(chip * height, height), height), :] = piece[...]


def line(ids, came, places, after):
    height, width = came[0].shape
    chips = 4 if len(came) == 5 else len(came)
    out_shape = jax.ShapeDtypeStruct((height * chips, width), came[0].dtype)
    return local(functools.partial(line_kernel, places), out_shape, "line", ids, *came, after=after)


def half_kernel(height, ids, mine, other, *outs):
    rows, width = outs[0].shape
    count = rows // height
    for at in range(count // 2):
        chip = ids[2] * (count // 2) + at
        here = pl.ds(pl.multiple_of(chip * height, height), height)
        for core, ref in ((ids[2], mine), (1 - ids[2], other)):
            to = pl.ds(pl.multiple_of((2 * at + core) * height, height), height)
            for part, out_ref in enumerate(outs):
                out_ref[to, :] = ref[here, pl.ds(part * width, width)]


def half(ids, mine, other, height):
    rows, width = mine.shape
    out_shape = [jax.ShapeDtypeStruct((rows, width // 2), mine.dtype)] * 2
    return local(functools.partial(half_kernel, height), out_shape, "half", ids, mine, other)


def mirrored_kernel(piece, part_at, ids, a_ref, diagonal, mine, other, m_ref, msg_ref, turned):
    height, cols = a_ref.shape
    block = cols // 4
    used = ids[1] <= ids[0]
    these = pl.ds(part_at * m_ref.shape[1], m_ref.shape[1])

    @pl.loop(0, height // piece // 2)
    def _(at):
        rows = pl.ds(pl.multiple_of(at * piece, piece), piece)
        for core, ref in ((ids[2], mine), (1 - ids[2], other)):
            turned[:, pl.ds(pl.multiple_of((2 * at + core) * piece, piece), piece)] = ref[rows, these].T

    @pl.loop(0, 4)
    def _(part):
        here = pl.ds(pl.multiple_of(part * block, block), block)

        @pl.when(used)
        def _():
            m_ref[here, :] = jnp.dot(turned[...], a_ref[:, here], preferred_element_type=jnp.float32).T

        @pl.when(jnp.logical_not(used))
        def _():
            m_ref[here, :] = jnp.zeros((block, m_ref.shape[1]), jnp.float32)

        @pl.when(ids[1] == ids[0])
        def _():
            rows = pl.ds(pl.multiple_of(part * block - ids[3], block), block)
            m_ref[here, :] -= (turned[:, rows].astype(jnp.float32) * diagonal[0:1, here]).T

        total = m_ref[here, :]
        scale = scale_for(jnp.max(jnp.abs(total), keepdims=True))
        msg_ref[here, :] = encode(total, scale)
        put_scale(msg_ref, cols, part, scale)


def mirrored_product(ids, matrix, diagonal, mine, other, piece, part_at, after):
    rows, cols = matrix.shape
    width = mine.shape[1] // 2
    out_shape = [
        jax.ShapeDtypeStruct((cols, width), jnp.float32),
        jax.ShapeDtypeStruct((cols + 4 * TAIL, width), jnp.bfloat16),
    ]
    return local(
        functools.partial(mirrored_kernel, piece, part_at), out_shape, "mirrored_product",
        ids, matrix, diagonal, mine, other, after=after,
        scratch_shapes=[pltpu.VMEM((width, rows), jnp.bfloat16)],
    )


def relay_kernel(ids, m_ref, in_ref, sum_ref, msg_ref):
    rows, width = m_ref.shape
    height = rows // 4

    @pl.loop(0, 4)
    def _(part):
        at = pl.ds(pl.multiple_of(part * height, height), height)
        total = m_ref[at, :] + decode(in_ref[at, :], scale_of(in_ref, rows, part))
        scale = scale_for(jnp.max(jnp.abs(total), keepdims=True))
        sum_ref[at, :] = total
        msg_ref[at, :] = encode(total, scale)
        put_scale(msg_ref, rows, part, scale)


def relay(ids, partial, message, after):
    out_shape = [jax.ShapeDtypeStruct(x.shape, x.dtype) for x in (partial, message)]
    return local(relay_kernel, out_shape, "relay", ids, partial, message, after=after)


def pick(ids, panels, panel, sem):
    for place, ref in enumerate(panels):

        @pl.when(ids[4] == place)
        def _():
            copy = pltpu.make_async_copy(ref, panel, sem)
            copy.start()
            copy.wait()


def direct_kernel(ids, a_ref, *refs):
    *panels, keep_ref, give_ref, give_too, panel, sem = refs
    pick(ids, panels, panel, sem)
    rows_kernel(ids, a_ref, panel, give_ref, core=1 - ids[2], of=2)
    rows_kernel(ids, a_ref, panel, give_too, core=1 - ids[2], at=1, of=2)
    rows_kernel(ids, a_ref, panel, keep_ref)


def rows_kernel(ids, a_ref, panel, out_ref, core=None, at=0, of=1):
    core = ids[2] if core is None else core
    rows = out_ref.shape[0]
    height = rows * of // 4
    skip = at * rows

    @pl.when(ids[1] <= ids[0])
    def _():
        @pl.loop(0, 4 // of)
        def _(part):
            at = pl.ds(pl.multiple_of(core * rows * of + skip + part * height, height), height)
            to = pl.ds(pl.multiple_of(part * height, height), height)
            out_ref[to, :] = jnp.dot(a_ref[at, :], panel[...], preferred_element_type=jnp.float32)


def direct_product(ids, matrix, panels, after):
    rows, cols = matrix.shape
    width = panels[0].shape[1]
    out_shape = [jax.ShapeDtypeStruct((rows // parts, width), jnp.float32) for parts in (2, 4, 4)]
    return local(
        direct_kernel, out_shape, "direct_product", ids, matrix, *panels, after=after,
        scratch_shapes=[pltpu.VMEM((cols, width), jnp.bfloat16), pltpu.SemaphoreType.DMA],
    )


def pack_kernel(count, ids, a_ref, *refs):
    theirs, (sum_ref, in_ref, own_ref, *msgs, total) = refs[:count], refs[count:]
    height = own_ref.shape[0]
    rounds = len(msgs)
    rows = rounds * height
    tile = rows // 4
    chip, core = ids[1], ids[2]

    for part in range(4):
        at = pl.ds(part * tile, tile)
        b_ref, where = theirs[part * count // 4], part * tile % theirs[0].shape[0]
        total[at, :] = a_ref[at, :] + b_ref[pl.ds(where, tile), :]

    @pl.when(ids[0] == chip)
    def _():
        @pl.loop(0, 4)
        def _(part):
            at = pl.ds(pl.multiple_of(part * tile, tile), tile)
            total[at, :] += sum_ref[at, :] + decode(in_ref[at, :], scale_of(in_ref, rows, part))

    for step, msg in enumerate(msgs):
        at = pl.ds(pl.multiple_of(lax.rem(chip + step, rounds) * height, height), height)
        values = total[at, :]
        scale = scale_for(jnp.max(jnp.abs(values), keepdims=True))
        msg[pl.ds(0, height), :] = encode(values, scale)
        put_scale(msg, height, 0, scale)

    stays = (chip <= ids[0]) & (lax.div(chip, rounds // 2) == core)

    @pl.when(stays)
    def _():
        place = 2 * lax.rem(chip, rounds // 2) + core
        own_ref[...] = total[pl.ds(pl.multiple_of(place * height, height), height), :]

    @pl.when(jnp.logical_not(stays))
    def _():
        own_ref[...] = jnp.zeros_like(own_ref)


def pack(ids, mine, theirs, partial, message, rounds, after):
    rows, width = mine.shape
    height = rows // rounds
    out_shape = [
        jax.ShapeDtypeStruct((height, width), jnp.float32),
        *[jax.ShapeDtypeStruct((height + TAIL, width), jnp.bfloat16)] * rounds,
    ]
    return local(
        functools.partial(pack_kernel, len(theirs)), out_shape, "pack", ids, mine, *theirs, partial, message, after=after,
        scratch_shapes=[pltpu.VMEM((rows, width), jnp.float32)],
    )


def finish_kernel(ids, before, own, *refs):
    *messages, out_ref = refs
    height, width = own.shape
    total = own[...]
    for message in messages:
        total += decode(message[pl.ds(0, height), :], scale_of(message, height, 0))
    done = out_ref.shape[1] - width
    if done:
        out_ref[:, pl.ds(0, done)] = before[:, pl.ds(0, done)]
    out_ref[:, pl.ds(done, width)] = total


def finish(ids, before, arrays, after):
    height, width = arrays[0].shape
    done = 0 if before is None else before.shape[1]
    out_shape = jax.ShapeDtypeStruct((height, done + width), jnp.float32)
    return local(finish_kernel, out_shape, "finish", ids, arrays[0] if before is None else before, *arrays, after=after)


def shards(trailing, panel_vectors):
    rows_here, cols_here = trailing.shape
    piece = panel_vectors.shape[0]
    count = lax.axis_size("row")
    devices_along = lax.axis_size("col")
    chips = devices_along // 2
    bits = count.bit_length() - 1
    row, col = lax.axis_index("row"), lax.axis_index("col")
    chip, core = col // 2, col % 2

    def at(row, chip, core):
        return (row * chips + chip) * 2 + core

    def turned(place, core):
        if core == 0:
            return place
        return sum(((place >> b) & 1) << (bits - 1 - b) for b in range(bits))

    def send(x, pairs):
        return lax.ppermute(x, ("row", "col"), [(at(*s), at(*d)) for s, d in pairs])

    offset = row ^ chip
    reverse = sum(((offset >> b) & 1) << (bits - 1 - b) for b in range(bits))
    place = jnp.where(core == 0, offset, reverse)
    ids = jnp.stack([row, chip, core, row * rows_here - col * cols_here, place]).astype(jnp.int32)

    def needed(chip, core, place, bit):
        rest = range(0, count, 2 ** (bit + 1))
        return any(chip ^ turned(place | r, core) > chip for r in rest)

    everyone = [(k, c) for k in range(chips) for c in range(2)]

    active = [(r, k, c) for r in range(count) for k in range(r + 1) for c in range(2)]

    def spread(place, source):
        bit = place.bit_length() - 1
        before = place - (1 << bit)
        pairs = [
            ((k ^ turned(before, c), k, c), (k ^ turned(place, c), k, c))
            for k, c in everyone
            if needed(k, c, place, bit)
        ]
        return send(source, pairs)

    def collect(bit, message):
        pairs = [
            ((k ^ turned(p, c), k, c), (k ^ turned(p - (1 << bit), c), k, c))
            for k, c in everyone
            for p in range(1 << bit, 2 << bit)
            if needed(k, c, p, bit)
        ]
        return send(message, pairs)

    matrix, diagonal = load(ids, trailing)

    line_of = [(r, k, c) for r in range(count) for k in range(chips) for c in range(2)]

    def step(x, to, wanted):
        return send(x, [((r, k, c), (r, to(k), c)) for r, k, c in line_of if wanted(r, k)])

    def by_distance(block):
        came, places = [block], [lambda chip: (chip, chip >= 0)]
        for by in range(1, chips):
            came.append(step(block, lambda k: (k + by) % chips, lambda r, k: (k + by) % chips <= r))
            places.append(lambda chip, by=by: (lax.rem(chip + chips - by, chips), chip >= 0))
        return came, places

    four = [
        lambda chip: (chip, chip >= 0),
        lambda chip: (chip ^ 2, chip >= 0),
        lambda chip: (jnp.maximum(chip - 1, 0), chip > 0),
        lambda chip: (jnp.minimum(chip + 1, 3), chip < 3),
        lambda chip: (3 - chip, (chip == 0) | (chip == 3)),
    ]

    def two_away(block):
        return step(block, lambda k: k ^ 2, lambda r, k: k >= 2 or k + 2 <= r)

    def next_ones(block):
        up = step(block, lambda k: k + 1, lambda r, k: k + 1 <= r and k < 3)
        return [up, step(block, lambda k: k - 1, lambda r, k: 0 <= k - 1 <= r)]

    def ends(two):
        return step(two, lambda k: 3 * (k - 1), lambda r, k: k == 1 or (k == 2 and r == 3))

    swap = [((r, k, c), (r, k, 1 - c)) for r, k, c in active]

    def widen(panels, after):
        panels[0], panels[1], *_ = lax.optimization_barrier((panels[0], panels[1], *after))
        for place in range(2, count):
            panels.append(spread(place, panels[place - (1 << (place.bit_length() - 1))]))

    def relaying(partial, came, panels, after):
        for bit in reversed(range(bits - 1)):
            partial, message = relay(ids, partial, came, after)
            if panels:
                message, *panels[2:] = lax.optimization_barrier((message, *panels[2:]))
            came = collect(bit, message)
        return partial, came, message

    def deliver(keep, got, partial, came, after):
        own, *out = pack(ids, keep, got, partial, came, chips, after)
        arrays = [own]
        for step, x in enumerate(out):
            pairs = []
            for r, k, c in active:
                at = c * chips + (k + step) % chips
                if (at // 2, at % 2) != (k, c):
                    pairs.append(((r, k, c), (r, at // 2, at % 2)))
            arrays.append(send(x, pairs))
        return arrays

    if chips == 4:
        two = two_away(panel_vectors)
        came, places = [panel_vectors, two, *next_ones(panel_vectors)], four
        two, matrix = lax.optimization_barrier((two, matrix))
        came.append(ends(two))
    else:
        came, places = by_distance(panel_vectors)
    mine = line(ids, came, places, [])
    other = send(mine, swap)
    panels_a, panels_b = ([x] for x in half(ids, mine, other, piece))
    panels_a.append(spread(1, panels_a[0]))
    panels_b.append(spread(1, panels_b[0]))
    partial_a, message_a = mirrored_product(ids, matrix, diagonal, mine, other, piece, 0, [])
    to_a = collect(bits - 1, message_a)
    partial_b, message_b = mirrored_product(ids, matrix, diagonal, mine, other, piece, 1, [message_a])
    to_b = collect(bits - 1, message_b)
    widen(panels_a, [message_b])
    widen(panels_b, [panels_a[1]])
    partial_a, to_a, relayed = relaying(partial_a, to_a, [], [message_b, panels_b[1]])
    keep_a, *give_a = direct_product(ids, matrix, panels_a, [relayed])
    got_a = [send(x, swap) for x in give_a]
    partial_b, to_b, relayed = relaying(partial_b, to_b, [], [keep_a, to_a, panels_b[2]])
    arrays_a = deliver(keep_a, got_a, partial_a, to_a, [relayed, *panels_b[3:]])
    keep_b, *give_b = direct_product(ids, matrix, panels_b, [arrays_a[0]])
    give_b, to_b, *arrays_a[1:3] = lax.optimization_barrier((give_b, to_b, *arrays_a[1:3]))
    got_b = [send(x, swap) for x in give_b]
    arrays_b = deliver(keep_b, got_b, partial_b, to_b, [])
    result = finish(ids, None, arrays_a, [arrays_b[0]])
    return finish(ids, result, arrays_b, [])


def solution(mesh):
    in_specs = (P("row", "col"), P(("row", "col"), None))
    out_specs = P(("row", "col"), None)
    return jax.shard_map(shards, mesh=mesh, in_specs=in_specs, out_specs=out_specs, check_vma=False)
```

```python
import functools

import jax
import jax.numpy as jnp
from jax import lax
from jax.experimental import pallas as pl
from jax.experimental.pallas import tpu as pltpu
from jax.sharding import PartitionSpec as P

TOP = 1400.0
TAIL = 16
VMEM = 6 * 2**20


def scale_for(largest):
    scale = TOP / jnp.maximum(largest, 1e-30)
    return scale.astype(jnp.bfloat16).astype(jnp.float32)


def encode(values, scale):
    x = values * scale
    x2 = x * x
    x4 = x2 * x2
    return (x * jnp.abs(x) * x2 * (x4 * x4)).astype(jnp.bfloat16)


def decode(coded, scale):
    y = coded.astype(jnp.float32)
    back = jnp.where(scale > 0, 1.0 / scale, 0.0)
    return y * jnp.exp2(-11 / 12 * jnp.log2(jnp.maximum(jnp.abs(y), 2.0**-126))) * back


def scale_of(message, rows, block):
    return message[pl.ds(rows + block * TAIL, TAIL), :][0:1, 0:1].astype(jnp.float32)


def put_scale(message, rows, block, scale):
    spread = jnp.full((TAIL, message.shape[1]), scale, jnp.float32).astype(jnp.bfloat16)
    message[pl.ds(rows + block * TAIL, TAIL), :] = spread


def local(kernel, out_shape, name, *operands, after=(), **options):
    count, skipped = len(operands), len(after)

    def body(*refs):
        kernel(*refs[:count], *refs[count + skipped :])

    return pl.pallas_call(
        body,
        out_shape=out_shape,
        in_specs=[pl.BlockSpec(memory_space=pltpu.SMEM)]
        + [pl.BlockSpec(memory_space=pltpu.VMEM)] * (count - 1)
        + [pl.BlockSpec(memory_space=pl.ANY)] * skipped,
        out_specs=jax.tree.map(lambda _: pl.BlockSpec(memory_space=pltpu.VMEM), out_shape),
        compiler_params=pltpu.CompilerParams(vmem_limit_bytes=VMEM),
        name=name,
        **options,
    )(*operands, *after)


def load_kernel(ids, a_ref, out_ref, diagonal, sem):
    height, cols = a_ref.shape
    block = cols // 4
    diagonal[...] = jnp.zeros_like(diagonal)

    @pl.when(ids[1] <= ids[0])
    def _():
        copy = pltpu.make_async_copy(a_ref, out_ref, sem)
        copy.start()
        copy.wait()

    for part in range(4):
        here = pl.ds(part * block, block)

        @pl.when(ids[1] == ids[0])
        def _():
            @pl.loop(0, height // block)
            def _(at):
                first = ids[3] + at * block
                rows = pl.ds(pl.multiple_of(at * block, block), block)

                @pl.when(first < part * block)
                def _():
                    out_ref[rows, here] = jnp.zeros((block, block), out_ref.dtype)

                @pl.when(first == part * block)
                def _():
                    tile = out_ref[rows, here]
                    empty = jnp.zeros_like(tile)
                    row = lax.broadcasted_iota(jnp.int32, tile.shape, 0)
                    col = lax.broadcasted_iota(jnp.int32, tile.shape, 1)
                    out_ref[rows, here] = jnp.where(row >= col, tile, empty)
                    on = jnp.where(row == col, tile, empty).astype(jnp.float32)
                    diagonal[:, here] = jnp.broadcast_to(jnp.sum(on, axis=0, keepdims=True), (8, block))


def load(ids, trailing):
    return pl.pallas_call(
        load_kernel,
        out_shape=[
            jax.ShapeDtypeStruct(trailing.shape, trailing.dtype),
            jax.ShapeDtypeStruct((8, trailing.shape[1]), jnp.float32),
        ],
        in_specs=[pl.BlockSpec(memory_space=pltpu.SMEM), pl.BlockSpec(memory_space=pltpu.HBM)],
        out_specs=[pl.BlockSpec(memory_space=pltpu.VMEM)] * 2,
        scratch_shapes=[pltpu.SemaphoreType.DMA],
        compiler_params=pltpu.CompilerParams(vmem_limit_bytes=VMEM),
        name="load",
    )(ids, trailing)


def line_kernel(places, ids, *refs):
    *came, out_ref = refs
    height = came[0].shape[0]
    for place, piece in zip(places, came):
        chip, there = place(ids[1])

        @pl.when(there)
        def _():
            out_ref[pl.ds(pl.multiple_of(chip * height, height), height), :] = piece[...]


def line(ids, came, places, after):
    height, width = came[0].shape
    chips = 4 if len(came) == 5 else len(came)
    out_shape = jax.ShapeDtypeStruct((height * chips, width), came[0].dtype)
    return local(functools.partial(line_kernel, places), out_shape, "line", ids, *came, after=after)


def half_kernel(height, ids, mine, other, *outs):
    rows, width = outs[0].shape
    count = rows // height
    for at in range(count // 2):
        chip = ids[2] * (count // 2) + at
        here = pl.ds(pl.multiple_of(chip * height, height), height)
        for core, ref in ((ids[2], mine), (1 - ids[2], other)):
            to = pl.ds(pl.multiple_of((2 * at + core) * height, height), height)
            for part, out_ref in enumerate(outs):
                out_ref[to, :] = ref[here, pl.ds(part * width, width)]


def half(ids, mine, other, height):
    rows, width = mine.shape
    out_shape = [jax.ShapeDtypeStruct((rows, width // 2), mine.dtype)] * 2
    return local(functools.partial(half_kernel, height), out_shape, "half", ids, mine, other)


def mirrored_kernel(piece, part_at, ids, a_ref, diagonal, mine, other, m_ref, msg_ref, turned):
    height, cols = a_ref.shape
    block = cols // 4
    used = ids[1] <= ids[0]
    these = pl.ds(part_at * m_ref.shape[1], m_ref.shape[1])

    @pl.loop(0, height // piece // 2)
    def _(at):
        rows = pl.ds(pl.multiple_of(at * piece, piece), piece)
        for core, ref in ((ids[2], mine), (1 - ids[2], other)):
            turned[:, pl.ds(pl.multiple_of((2 * at + core) * piece, piece), piece)] = ref[rows, these].T

    @pl.loop(0, 4)
    def _(part):
        here = pl.ds(pl.multiple_of(part * block, block), block)

        @pl.when(used)
        def _():
            m_ref[here, :] = jnp.dot(turned[...], a_ref[:, here], preferred_element_type=jnp.float32).T

        @pl.when(jnp.logical_not(used))
        def _():
            m_ref[here, :] = jnp.zeros((block, m_ref.shape[1]), jnp.float32)

        @pl.when(ids[1] == ids[0])
        def _():
            rows = pl.ds(pl.multiple_of(part * block - ids[3], block), block)
            m_ref[here, :] -= (turned[:, rows].astype(jnp.float32) * diagonal[0:1, here]).T

        total = m_ref[here, :]
        scale = scale_for(jnp.max(jnp.abs(total), keepdims=True))
        msg_ref[here, :] = encode(total, scale)
        put_scale(msg_ref, cols, part, scale)


def mirrored_product(ids, matrix, diagonal, mine, other, piece, part_at, after):
    rows, cols = matrix.shape
    width = mine.shape[1] // 2
    out_shape = [
        jax.ShapeDtypeStruct((cols, width), jnp.float32),
        jax.ShapeDtypeStruct((cols + 4 * TAIL, width), jnp.bfloat16),
    ]
    return local(
        functools.partial(mirrored_kernel, piece, part_at), out_shape, "mirrored_product",
        ids, matrix, diagonal, mine, other, after=after,
        scratch_shapes=[pltpu.VMEM((width, rows), jnp.bfloat16)],
    )


def relay_kernel(ids, m_ref, in_ref, sum_ref, msg_ref):
    rows, width = m_ref.shape
    height = rows // 4

    @pl.loop(0, 4)
    def _(part):
        at = pl.ds(pl.multiple_of(part * height, height), height)
        total = m_ref[at, :] + decode(in_ref[at, :], scale_of(in_ref, rows, part))
        scale = scale_for(jnp.max(jnp.abs(total), keepdims=True))
        sum_ref[at, :] = total
        msg_ref[at, :] = encode(total, scale)
        put_scale(msg_ref, rows, part, scale)


def relay(ids, partial, message, after):
    out_shape = [jax.ShapeDtypeStruct(x.shape, x.dtype) for x in (partial, message)]
    return local(relay_kernel, out_shape, "relay", ids, partial, message, after=after)


def pick(ids, panels, panel, sem):
    for place, ref in enumerate(panels):

        @pl.when(ids[4] == place)
        def _():
            copy = pltpu.make_async_copy(ref, panel, sem)
            copy.start()
            copy.wait()


def give_kernel(ids, a_ref, *refs):
    *panels, give_ref, give_too, panel, sem = refs
    pick(ids, panels, panel, sem)
    rows_kernel(ids, a_ref, panel, give_ref, core=1 - ids[2], of=2)
    rows_kernel(ids, a_ref, panel, give_too, core=1 - ids[2], at=1, of=2)


def direct_kernel(ids, a_ref, *refs):
    *panels, keep_ref, give_ref, give_too, panel, sem = refs
    pick(ids, panels, panel, sem)
    rows_kernel(ids, a_ref, panel, give_ref, core=1 - ids[2], of=2)
    rows_kernel(ids, a_ref, panel, give_too, core=1 - ids[2], at=1, of=2)
    rows_kernel(ids, a_ref, panel, keep_ref)


def rows_kernel(ids, a_ref, panel, out_ref, core=None, at=0, of=1):
    core = ids[2] if core is None else core
    rows = out_ref.shape[0]
    height = rows * of // 4
    skip = at * rows

    @pl.when(ids[1] <= ids[0])
    def _():
        @pl.loop(0, 4 // of)
        def _(part):
            at = pl.ds(pl.multiple_of(core * rows * of + skip + part * height, height), height)
            to = pl.ds(pl.multiple_of(part * height, height), height)
            out_ref[to, :] = jnp.dot(a_ref[at, :], panel[...], preferred_element_type=jnp.float32)


def direct_product(ids, matrix, panels, after):
    rows, cols = matrix.shape
    width = panels[0].shape[1]
    out_shape = [jax.ShapeDtypeStruct((rows // parts, width), jnp.float32) for parts in (2, 4, 4)]
    return local(
        direct_kernel, out_shape, "direct_product", ids, matrix, *panels, after=after,
        scratch_shapes=[pltpu.VMEM((cols, width), jnp.bfloat16), pltpu.SemaphoreType.DMA],
    )


def give_product(ids, matrix, panels, after):
    rows, cols = matrix.shape
    width = panels[0].shape[1]
    out_shape = [
        *[jax.ShapeDtypeStruct((rows // 4, width), jnp.float32)] * 2,
        jax.ShapeDtypeStruct((cols, width), jnp.bfloat16),
    ]
    return local(
        give_kernel, out_shape, "give_product", ids, matrix, *panels, after=after,
        scratch_shapes=[pltpu.SemaphoreType.DMA],
    )


def keep_product(ids, matrix, panel, after):
    rows, cols = matrix.shape
    width = panel.shape[1]
    out_shape = jax.ShapeDtypeStruct((rows // 2, width), jnp.float32)
    return local(
        rows_kernel, out_shape, "keep_product", ids, matrix, panel, after=after
    )


def pack_kernel(count, ids, a_ref, *refs):
    theirs, (sum_ref, in_ref, own_ref, *msgs, total) = refs[:count], refs[count:]
    height = own_ref.shape[0]
    rounds = len(msgs)
    rows = rounds * height
    tile = rows // 4
    chip, core = ids[1], ids[2]

    for part in range(4):
        at = pl.ds(part * tile, tile)
        b_ref, where = theirs[part * count // 4], part * tile % theirs[0].shape[0]
        total[at, :] = a_ref[at, :] + b_ref[pl.ds(where, tile), :]

    @pl.when(ids[0] == chip)
    def _():
        @pl.loop(0, 4)
        def _(part):
            at = pl.ds(pl.multiple_of(part * tile, tile), tile)
            total[at, :] += sum_ref[at, :] + decode(in_ref[at, :], scale_of(in_ref, rows, part))

    for step, msg in enumerate(msgs):
        at = pl.ds(pl.multiple_of(lax.rem(chip + step, rounds) * height, height), height)
        values = total[at, :]
        scale = scale_for(jnp.max(jnp.abs(values), keepdims=True))
        msg[pl.ds(0, height), :] = encode(values, scale)
        put_scale(msg, height, 0, scale)

    stays = (chip <= ids[0]) & (lax.div(chip, rounds // 2) == core)

    @pl.when(stays)
    def _():
        place = 2 * lax.rem(chip, rounds // 2) + core
        own_ref[...] = total[pl.ds(pl.multiple_of(place * height, height), height), :]

    @pl.when(jnp.logical_not(stays))
    def _():
        own_ref[...] = jnp.zeros_like(own_ref)


def pack(ids, mine, theirs, partial, message, rounds, after):
    rows, width = mine.shape
    height = rows // rounds
    out_shape = [
        jax.ShapeDtypeStruct((height, width), jnp.float32),
        *[jax.ShapeDtypeStruct((height + TAIL, width), jnp.bfloat16)] * rounds,
    ]
    return local(
        functools.partial(pack_kernel, len(theirs)), out_shape, "pack", ids, mine, *theirs, partial, message, after=after,
        scratch_shapes=[pltpu.VMEM((rows, width), jnp.float32)],
    )


def finish_kernel(ids, before, own, *refs):
    *messages, out_ref = refs
    height, width = own.shape
    total = own[...]
    for message in messages:
        total += decode(message[pl.ds(0, height), :], scale_of(message, height, 0))
    done = out_ref.shape[1] - width
    if done:
        out_ref[:, pl.ds(0, done)] = before[:, pl.ds(0, done)]
    out_ref[:, pl.ds(done, width)] = total


def finish(ids, before, arrays, after):
    height, width = arrays[0].shape
    done = 0 if before is None else before.shape[1]
    out_shape = jax.ShapeDtypeStruct((height, done + width), jnp.float32)
    return local(finish_kernel, out_shape, "finish", ids, arrays[0] if before is None else before, *arrays, after=after)


def shards(trailing, panel_vectors):
    rows_here, cols_here = trailing.shape
    piece = panel_vectors.shape[0]
    count = lax.axis_size("row")
    devices_along = lax.axis_size("col")
    chips = devices_along // 2
    bits = count.bit_length() - 1
    row, col = lax.axis_index("row"), lax.axis_index("col")
    chip, core = col // 2, col % 2

    def at(row, chip, core):
        return (row * chips + chip) * 2 + core

    def turned(place, core):
        if core == 0:
            return place
        return sum(((place >> b) & 1) << (bits - 1 - b) for b in range(bits))

    def send(x, pairs):
        return lax.ppermute(x, ("row", "col"), [(at(*s), at(*d)) for s, d in pairs])

    offset = row ^ chip
    reverse = sum(((offset >> b) & 1) << (bits - 1 - b) for b in range(bits))
    place = jnp.where(core == 0, offset, reverse)
    ids = jnp.stack([row, chip, core, row * rows_here - col * cols_here, place]).astype(jnp.int32)

    def needed(chip, core, place, bit):
        rest = range(0, count, 2 ** (bit + 1))
        return any(chip ^ turned(place | r, core) > chip for r in rest)

    everyone = [(k, c) for k in range(chips) for c in range(2)]

    active = [(r, k, c) for r in range(count) for k in range(r + 1) for c in range(2)]

    def spread(place, source):
        bit = place.bit_length() - 1
        before = place - (1 << bit)
        pairs = [
            ((k ^ turned(before, c), k, c), (k ^ turned(place, c), k, c))
            for k, c in everyone
            if needed(k, c, place, bit)
        ]
        return send(source, pairs)

    def collect(bit, message):
        pairs = [
            ((k ^ turned(p, c), k, c), (k ^ turned(p - (1 << bit), c), k, c))
            for k, c in everyone
            for p in range(1 << bit, 2 << bit)
            if needed(k, c, p, bit)
        ]
        return send(message, pairs)

    matrix, diagonal = load(ids, trailing)

    line_of = [(r, k, c) for r in range(count) for k in range(chips) for c in range(2)]

    def step(x, to, wanted):
        return send(x, [((r, k, c), (r, to(k), c)) for r, k, c in line_of if wanted(r, k)])

    def by_distance(block):
        came, places = [block], [lambda chip: (chip, chip >= 0)]
        for by in range(1, chips):
            came.append(step(block, lambda k: (k + by) % chips, lambda r, k: (k + by) % chips <= r))
            places.append(lambda chip, by=by: (lax.rem(chip + chips - by, chips), chip >= 0))
        return came, places

    four = [
        lambda chip: (chip, chip >= 0),
        lambda chip: (chip ^ 2, chip >= 0),
        lambda chip: (jnp.maximum(chip - 1, 0), chip > 0),
        lambda chip: (jnp.minimum(chip + 1, 3), chip < 3),
        lambda chip: (3 - chip, (chip == 0) | (chip == 3)),
    ]

    def two_away(block):
        return step(block, lambda k: k ^ 2, lambda r, k: k >= 2 or k + 2 <= r)

    def next_ones(block):
        up = step(block, lambda k: k + 1, lambda r, k: k + 1 <= r and k < 3)
        return [up, step(block, lambda k: k - 1, lambda r, k: 0 <= k - 1 <= r)]

    def ends(two):
        return step(two, lambda k: 3 * (k - 1), lambda r, k: k == 1 or (k == 2 and r == 3))

    swap = [((r, k, c), (r, k, 1 - c)) for r, k, c in active]

    def widen(panels, after):
        panels[0], panels[1], *_ = lax.optimization_barrier((panels[0], panels[1], *after))
        for place in range(2, count):
            panels.append(spread(place, panels[place - (1 << (place.bit_length() - 1))]))

    def relaying(partial, came, panels, after):
        for bit in reversed(range(bits - 1)):
            partial, message = relay(ids, partial, came, after)
            if panels:
                message, *panels[2:] = lax.optimization_barrier((message, *panels[2:]))
            came = collect(bit, message)
        return partial, came, message

    def deliver(keep, got, partial, came, after):
        own, *out = pack(ids, keep, got, partial, came, chips, after)
        arrays = [own]
        for step, x in enumerate(out):
            pairs = []
            for r, k, c in active:
                at = c * chips + (k + step) % chips
                if (at // 2, at % 2) != (k, c):
                    pairs.append(((r, k, c), (r, at // 2, at % 2)))
            arrays.append(send(x, pairs))
        return arrays

    if chips == 4:
        two = two_away(panel_vectors)
        came, places = [panel_vectors, two, *next_ones(panel_vectors)], four
        two, matrix = lax.optimization_barrier((two, matrix))
        came.append(ends(two))
    else:
        came, places = by_distance(panel_vectors)
    mine = line(ids, came, places, [])
    other = send(mine, swap)
    panels_a, panels_b = ([x] for x in half(ids, mine, other, piece))
    panels_a.append(spread(1, panels_a[0]))
    panels_b.append(spread(1, panels_b[0]))
    partial_a, message_a = mirrored_product(ids, matrix, diagonal, mine, other, piece, 0, [])
    to_a = collect(bits - 1, message_a)
    partial_b, message_b = mirrored_product(ids, matrix, diagonal, mine, other, piece, 1, [message_a])
    to_b = collect(bits - 1, message_b)
    widen(panels_a, [message_b])
    widen(panels_b, [panels_a[1]])
    partial_a, to_a, relayed = relaying(partial_a, to_a, [], [message_b, panels_b[1]])
    keep_a, *give_a = direct_product(ids, matrix, panels_a, [relayed])
    got_a = [send(x, swap) for x in give_a]
    partial_b, to_b, relayed = relaying(partial_b, to_b, [], [keep_a, to_a, panels_b[2]])
    arrays_a = deliver(keep_a, got_a, partial_a, to_a, [relayed, *panels_b[3:]])
    *give_b, panel_b = give_product(ids, matrix, panels_b, [arrays_a[0]])
    got_b = [send(x, swap) for x in give_b]
    keep_b = keep_product(ids, matrix, panel_b, [to_b])
    keep_b, *arrays_a[1:3] = lax.optimization_barrier((keep_b, *arrays_a[1:3]))
    arrays_b = deliver(keep_b, got_b, partial_b, to_b, [])
    result = finish(ids, None, arrays_a, [arrays_b[0]])
    return finish(ids, result, arrays_b, [])


def solution(mesh):
    in_specs = (P("row", "col"), P(("row", "col"), None))
    out_specs = P(("row", "col"), None)
    return jax.shard_map(shards, mesh=mesh, in_specs=in_specs, out_specs=out_specs, check_vma=False)
```

```python
import functools

import jax
import jax.numpy as jnp
from jax import lax
from jax.experimental import pallas as pl
from jax.experimental.pallas import tpu as pltpu
from jax.sharding import PartitionSpec as P

TOP = 1400.0
TAIL = 16
VMEM = 6 * 2**20


def scale_for(largest):
    scale = TOP / jnp.maximum(largest, 1e-30)
    return scale.astype(jnp.bfloat16).astype(jnp.float32)


def encode(values, scale):
    x = values * scale
    x2 = x * x
    x4 = x2 * x2
    return (x * jnp.abs(x) * x2 * (x4 * x4)).astype(jnp.bfloat16)


def decode(coded, scale):
    y = coded.astype(jnp.float32)
    back = jnp.where(scale > 0, 1.0 / scale, 0.0)
    return y * jnp.exp2(-11 / 12 * jnp.log2(jnp.maximum(jnp.abs(y), 2.0**-126))) * back


def scale_of(message, rows, block):
    return message[pl.ds(rows + block * TAIL, TAIL), :][0:1, 0:1].astype(jnp.float32)


def put_scale(message, rows, block, scale):
    spread = jnp.full((TAIL, message.shape[1]), scale, jnp.float32).astype(jnp.bfloat16)
    message[pl.ds(rows + block * TAIL, TAIL), :] = spread


def local(kernel, out_shape, name, *operands, after=(), **options):
    count, skipped = len(operands), len(after)

    def body(*refs):
        kernel(*refs[:count], *refs[count + skipped :])

    return pl.pallas_call(
        body,
        out_shape=out_shape,
        in_specs=[pl.BlockSpec(memory_space=pltpu.SMEM)]
        + [pl.BlockSpec(memory_space=pltpu.VMEM)] * (count - 1)
        + [pl.BlockSpec(memory_space=pl.ANY)] * skipped,
        out_specs=jax.tree.map(lambda _: pl.BlockSpec(memory_space=pltpu.VMEM), out_shape),
        compiler_params=pltpu.CompilerParams(vmem_limit_bytes=VMEM),
        name=name,
        **options,
    )(*operands, *after)


def load_kernel(ids, a_ref, out_ref, diagonal, sem):
    height, cols = a_ref.shape
    block = cols // 4
    diagonal[...] = jnp.zeros_like(diagonal)

    @pl.when(ids[1] <= ids[0])
    def _():
        copy = pltpu.make_async_copy(a_ref, out_ref, sem)
        copy.start()
        copy.wait()

    for part in range(4):
        here = pl.ds(part * block, block)

        @pl.when(ids[1] == ids[0])
        def _():
            @pl.loop(0, height // block)
            def _(at):
                first = ids[3] + at * block
                rows = pl.ds(pl.multiple_of(at * block, block), block)

                @pl.when(first < part * block)
                def _():
                    out_ref[rows, here] = jnp.zeros((block, block), out_ref.dtype)

                @pl.when(first == part * block)
                def _():
                    tile = out_ref[rows, here]
                    empty = jnp.zeros_like(tile)
                    row = lax.broadcasted_iota(jnp.int32, tile.shape, 0)
                    col = lax.broadcasted_iota(jnp.int32, tile.shape, 1)
                    out_ref[rows, here] = jnp.where(row >= col, tile, empty)
                    on = jnp.where(row == col, tile, empty).astype(jnp.float32)
                    diagonal[:, here] = jnp.broadcast_to(jnp.sum(on, axis=0, keepdims=True), (8, block))


def load(ids, trailing):
    return pl.pallas_call(
        load_kernel,
        out_shape=[
            jax.ShapeDtypeStruct(trailing.shape, trailing.dtype),
            jax.ShapeDtypeStruct((8, trailing.shape[1]), jnp.float32),
        ],
        in_specs=[pl.BlockSpec(memory_space=pltpu.SMEM), pl.BlockSpec(memory_space=pltpu.HBM)],
        out_specs=[pl.BlockSpec(memory_space=pltpu.VMEM)] * 2,
        scratch_shapes=[pltpu.SemaphoreType.DMA],
        compiler_params=pltpu.CompilerParams(vmem_limit_bytes=VMEM),
        name="load",
    )(ids, trailing)


def line_kernel(places, ids, *refs):
    *came, out_a, out_b = refs
    height = came[0].shape[0]
    width = out_a.shape[1]
    for place, piece in zip(places, came):
        chip, there = place(ids[1])

        @pl.when(there)
        def _():
            to = pl.ds(pl.multiple_of(chip * height, height), height)
            out_a[to, :] = piece[:, pl.ds(0, width)]
            out_b[to, :] = piece[:, pl.ds(width, width)]


def line(ids, came, places, after):
    height, width = came[0].shape
    chips = 4 if len(came) == 5 else len(came)
    out_shape = [jax.ShapeDtypeStruct((height * chips, width // 2), came[0].dtype)] * 2
    return local(functools.partial(line_kernel, places), out_shape, "line", ids, *came, after=after)


def half_kernel(height, ids, mine, other, out_ref):
    count = out_ref.shape[0] // height
    for at in range(count // 2):
        chip = ids[2] * (count // 2) + at
        here = pl.ds(pl.multiple_of(chip * height, height), height)
        for core, ref in ((ids[2], mine), (1 - ids[2], other)):
            to = pl.ds(pl.multiple_of((2 * at + core) * height, height), height)
            out_ref[to, :] = ref[here, :]


def half(ids, mine, other, height):
    out_shape = jax.ShapeDtypeStruct(mine.shape, mine.dtype)
    return local(functools.partial(half_kernel, height), out_shape, "half", ids, mine, other)


def mirrored_kernel(piece, ids, a_ref, diagonal, mine, other, m_ref, msg_ref, turned):
    height, cols = a_ref.shape
    block = cols // 4
    used = ids[1] <= ids[0]

    @pl.loop(0, height // piece // 2)
    def _(at):
        rows = pl.ds(pl.multiple_of(at * piece, piece), piece)
        for core, ref in ((ids[2], mine), (1 - ids[2], other)):
            turned[:, pl.ds(pl.multiple_of((2 * at + core) * piece, piece), piece)] = ref[rows, :].T

    @pl.loop(0, 4)
    def _(part):
        here = pl.ds(pl.multiple_of(part * block, block), block)

        @pl.when(used)
        def _():
            m_ref[here, :] = jnp.dot(turned[...], a_ref[:, here], preferred_element_type=jnp.float32).T

        @pl.when(jnp.logical_not(used))
        def _():
            m_ref[here, :] = jnp.zeros((block, m_ref.shape[1]), jnp.float32)

        @pl.when(ids[1] == ids[0])
        def _():
            rows = pl.ds(pl.multiple_of(part * block - ids[3], block), block)
            m_ref[here, :] -= (turned[:, rows].astype(jnp.float32) * diagonal[0:1, here]).T

        total = m_ref[here, :]
        scale = scale_for(jnp.max(jnp.abs(total), keepdims=True))
        msg_ref[here, :] = encode(total, scale)
        put_scale(msg_ref, cols, part, scale)


def mirrored_product(ids, matrix, diagonal, mine, other, piece, after):
    rows, cols = matrix.shape
    width = mine.shape[1]
    out_shape = [
        jax.ShapeDtypeStruct((cols, width), jnp.float32),
        jax.ShapeDtypeStruct((cols + 4 * TAIL, width), jnp.bfloat16),
    ]
    return local(
        functools.partial(mirrored_kernel, piece), out_shape, "mirrored_product",
        ids, matrix, diagonal, mine, other, after=after,
        scratch_shapes=[pltpu.VMEM((width, rows), jnp.bfloat16)],
    )


def relay_kernel(ids, m_ref, in_ref, sum_ref, msg_ref):
    rows, width = m_ref.shape
    height = rows // 4

    @pl.loop(0, 4)
    def _(part):
        at = pl.ds(pl.multiple_of(part * height, height), height)
        total = m_ref[at, :] + decode(in_ref[at, :], scale_of(in_ref, rows, part))
        scale = scale_for(jnp.max(jnp.abs(total), keepdims=True))
        sum_ref[at, :] = total
        msg_ref[at, :] = encode(total, scale)
        put_scale(msg_ref, rows, part, scale)


def relay(ids, partial, message, after):
    out_shape = [jax.ShapeDtypeStruct(x.shape, x.dtype) for x in (partial, message)]
    return local(relay_kernel, out_shape, "relay", ids, partial, message, after=after)


def pick(ids, panels, panel, sem):
    for place, ref in enumerate(panels):

        @pl.when(ids[4] == place)
        def _():
            copy = pltpu.make_async_copy(ref, panel, sem)
            copy.start()
            copy.wait()


def give_kernel(ids, a_ref, *refs):
    *panels, give_ref, give_too, panel, sem = refs
    pick(ids, panels, panel, sem)
    rows_kernel(ids, a_ref, panel, give_ref, core=1 - ids[2], of=2)
    rows_kernel(ids, a_ref, panel, give_too, core=1 - ids[2], at=1, of=2)


def direct_kernel(ids, a_ref, *refs):
    *panels, keep_ref, give_ref, give_too, panel, sem = refs
    pick(ids, panels, panel, sem)
    rows_kernel(ids, a_ref, panel, give_ref, core=1 - ids[2], of=2)
    rows_kernel(ids, a_ref, panel, give_too, core=1 - ids[2], at=1, of=2)
    rows_kernel(ids, a_ref, panel, keep_ref)


def rows_kernel(ids, a_ref, panel, out_ref, core=None, at=0, of=1):
    core = ids[2] if core is None else core
    rows = out_ref.shape[0]
    height = rows * of // 4
    skip = at * rows

    @pl.when(ids[1] <= ids[0])
    def _():
        @pl.loop(0, 4 // of)
        def _(part):
            at = pl.ds(pl.multiple_of(core * rows * of + skip + part * height, height), height)
            to = pl.ds(pl.multiple_of(part * height, height), height)
            out_ref[to, :] = jnp.dot(a_ref[at, :], panel[...], preferred_element_type=jnp.float32)


def direct_product(ids, matrix, panels, after):
    rows, cols = matrix.shape
    width = panels[0].shape[1]
    out_shape = [jax.ShapeDtypeStruct((rows // parts, width), jnp.float32) for parts in (2, 4, 4)]
    return local(
        direct_kernel, out_shape, "direct_product", ids, matrix, *panels, after=after,
        scratch_shapes=[pltpu.VMEM((cols, width), jnp.bfloat16), pltpu.SemaphoreType.DMA],
    )


def give_product(ids, matrix, panels, after):
    rows, cols = matrix.shape
    width = panels[0].shape[1]
    out_shape = [
        *[jax.ShapeDtypeStruct((rows // 4, width), jnp.float32)] * 2,
        jax.ShapeDtypeStruct((cols, width), jnp.bfloat16),
    ]
    return local(
        give_kernel, out_shape, "give_product", ids, matrix, *panels, after=after,
        scratch_shapes=[pltpu.SemaphoreType.DMA],
    )


def keep_product(ids, matrix, panel, after):
    rows, cols = matrix.shape
    width = panel.shape[1]
    out_shape = jax.ShapeDtypeStruct((rows // 2, width), jnp.float32)
    return local(
        rows_kernel, out_shape, "keep_product", ids, matrix, panel, after=after
    )


def pack_kernel(count, ids, a_ref, *refs):
    theirs, (sum_ref, in_ref, own_ref, *msgs, total) = refs[:count], refs[count:]
    height = own_ref.shape[0]
    rounds = len(msgs)
    rows = rounds * height
    tile = rows // 4
    chip, core = ids[1], ids[2]

    for part in range(4):
        at = pl.ds(part * tile, tile)
        b_ref, where = theirs[part * count // 4], part * tile % theirs[0].shape[0]
        total[at, :] = a_ref[at, :] + b_ref[pl.ds(where, tile), :]

    @pl.when(ids[0] == chip)
    def _():
        @pl.loop(0, 4)
        def _(part):
            at = pl.ds(pl.multiple_of(part * tile, tile), tile)
            total[at, :] += sum_ref[at, :] + decode(in_ref[at, :], scale_of(in_ref, rows, part))

    for step, msg in enumerate(msgs):
        at = pl.ds(pl.multiple_of(lax.rem(chip + step, rounds) * height, height), height)
        values = total[at, :]
        scale = scale_for(jnp.max(jnp.abs(values), keepdims=True))
        msg[pl.ds(0, height), :] = encode(values, scale)
        put_scale(msg, height, 0, scale)

    stays = (chip <= ids[0]) & (lax.div(chip, rounds // 2) == core)

    @pl.when(stays)
    def _():
        place = 2 * lax.rem(chip, rounds // 2) + core
        own_ref[...] = total[pl.ds(pl.multiple_of(place * height, height), height), :]

    @pl.when(jnp.logical_not(stays))
    def _():
        own_ref[...] = jnp.zeros_like(own_ref)


def pack(ids, mine, theirs, partial, message, rounds, after):
    rows, width = mine.shape
    height = rows // rounds
    out_shape = [
        jax.ShapeDtypeStruct((height, width), jnp.float32),
        *[jax.ShapeDtypeStruct((height + TAIL, width), jnp.bfloat16)] * rounds,
    ]
    return local(
        functools.partial(pack_kernel, len(theirs)), out_shape, "pack", ids, mine, *theirs, partial, message, after=after,
        scratch_shapes=[pltpu.VMEM((rows, width), jnp.float32)],
    )


def finish_kernel(ids, before, own, *refs):
    *messages, out_ref = refs
    height, width = own.shape
    total = own[...]
    for message in messages:
        total += decode(message[pl.ds(0, height), :], scale_of(message, height, 0))
    done = out_ref.shape[1] - width
    if done:
        out_ref[:, pl.ds(0, done)] = before[:, pl.ds(0, done)]
    out_ref[:, pl.ds(done, width)] = total


def finish(ids, before, arrays, after):
    height, width = arrays[0].shape
    done = 0 if before is None else before.shape[1]
    out_shape = jax.ShapeDtypeStruct((height, done + width), jnp.float32)
    return local(finish_kernel, out_shape, "finish", ids, arrays[0] if before is None else before, *arrays, after=after)


def shards(trailing, panel_vectors):
    rows_here, cols_here = trailing.shape
    piece = panel_vectors.shape[0]
    count = lax.axis_size("row")
    devices_along = lax.axis_size("col")
    chips = devices_along // 2
    bits = count.bit_length() - 1
    row, col = lax.axis_index("row"), lax.axis_index("col")
    chip, core = col // 2, col % 2

    def at(row, chip, core):
        return (row * chips + chip) * 2 + core

    def turned(place, core):
        if core == 0:
            return place
        return sum(((place >> b) & 1) << (bits - 1 - b) for b in range(bits))

    def send(x, pairs):
        return lax.ppermute(x, ("row", "col"), [(at(*s), at(*d)) for s, d in pairs])

    offset = row ^ chip
    reverse = sum(((offset >> b) & 1) << (bits - 1 - b) for b in range(bits))
    place = jnp.where(core == 0, offset, reverse)
    ids = jnp.stack([row, chip, core, row * rows_here - col * cols_here, place]).astype(jnp.int32)

    def needed(chip, core, place, bit):
        rest = range(0, count, 2 ** (bit + 1))
        return any(chip ^ turned(place | r, core) > chip for r in rest)

    everyone = [(k, c) for k in range(chips) for c in range(2)]

    active = [(r, k, c) for r in range(count) for k in range(r + 1) for c in range(2)]

    def spread(place, source):
        bit = place.bit_length() - 1
        before = place - (1 << bit)
        pairs = [
            ((k ^ turned(before, c), k, c), (k ^ turned(place, c), k, c))
            for k, c in everyone
            if needed(k, c, place, bit)
        ]
        return send(source, pairs)

    def collect(bit, message):
        pairs = [
            ((k ^ turned(p, c), k, c), (k ^ turned(p - (1 << bit), c), k, c))
            for k, c in everyone
            for p in range(1 << bit, 2 << bit)
            if needed(k, c, p, bit)
        ]
        return send(message, pairs)

    matrix, diagonal = load(ids, trailing)

    line_of = [(r, k, c) for r in range(count) for k in range(chips) for c in range(2)]

    def step(x, to, wanted):
        return send(x, [((r, k, c), (r, to(k), c)) for r, k, c in line_of if wanted(r, k)])

    def by_distance(block):
        came, places = [block], [lambda chip: (chip, chip >= 0)]
        for by in range(1, chips):
            came.append(step(block, lambda k: (k + by) % chips, lambda r, k: (k + by) % chips <= r))
            places.append(lambda chip, by=by: (lax.rem(chip + chips - by, chips), chip >= 0))
        return came, places

    four = [
        lambda chip: (chip, chip >= 0),
        lambda chip: (chip ^ 2, chip >= 0),
        lambda chip: (jnp.maximum(chip - 1, 0), chip > 0),
        lambda chip: (jnp.minimum(chip + 1, 3), chip < 3),
        lambda chip: (3 - chip, (chip == 0) | (chip == 3)),
    ]

    def two_away(block):
        return step(block, lambda k: k ^ 2, lambda r, k: k >= 2 or k + 2 <= r)

    def next_ones(block):
        up = step(block, lambda k: k + 1, lambda r, k: k + 1 <= r and k < 3)
        return [up, step(block, lambda k: k - 1, lambda r, k: 0 <= k - 1 <= r)]

    def ends(two):
        return step(two, lambda k: 3 * (k - 1), lambda r, k: k == 1 or (k == 2 and r == 3))

    swap = [((r, k, c), (r, k, 1 - c)) for r, k, c in active]

    def widen(panels, after):
        panels[0], panels[1], *_ = lax.optimization_barrier((panels[0], panels[1], *after))
        for place in range(2, count):
            panels.append(spread(place, panels[place - (1 << (place.bit_length() - 1))]))

    def relaying(partial, came, panels, after):
        for bit in reversed(range(bits - 1)):
            partial, message = relay(ids, partial, came, after)
            if panels:
                message, *panels[2:] = lax.optimization_barrier((message, *panels[2:]))
            came = collect(bit, message)
        return partial, came, message

    def deliver(keep, got, partial, came, after):
        own, *out = pack(ids, keep, got, partial, came, chips, after)
        arrays = [own]
        for step, x in enumerate(out):
            pairs = []
            for r, k, c in active:
                at = c * chips + (k + step) % chips
                if (at // 2, at % 2) != (k, c):
                    pairs.append(((r, k, c), (r, at // 2, at % 2)))
            arrays.append(send(x, pairs))
        return arrays

    if chips == 4:
        two = two_away(panel_vectors)
        came, places = [panel_vectors, two, *next_ones(panel_vectors)], four
        two, matrix = lax.optimization_barrier((two, matrix))
        came.append(ends(two))
    else:
        came, places = by_distance(panel_vectors)
    mine_a, mine_b = line(ids, came, places, [])
    other_a, other_b = send(mine_a, swap), send(mine_b, swap)
    panels_a, panels_b = [half(ids, mine_a, other_a, piece)], [half(ids, mine_b, other_b, piece)]
    panels_a.append(spread(1, panels_a[0]))
    panels_b.append(spread(1, panels_b[0]))
    partial_a, message_a = mirrored_product(ids, matrix, diagonal, mine_a, other_a, piece, [])
    to_a = collect(bits - 1, message_a)
    partial_b, message_b = mirrored_product(ids, matrix, diagonal, mine_b, other_b, piece, [message_a])
    to_b = collect(bits - 1, message_b)
    widen(panels_a, [message_b])
    widen(panels_b, [panels_a[1]])
    partial_a, to_a, relayed = relaying(partial_a, to_a, [], [message_b, panels_b[1]])
    keep_a, *give_a = direct_product(ids, matrix, panels_a, [relayed])
    got_a = [send(x, swap) for x in give_a]
    partial_b, to_b, relayed = relaying(partial_b, to_b, [], [keep_a, to_a, panels_b[2]])
    arrays_a = deliver(keep_a, got_a, partial_a, to_a, [relayed, *panels_b[3:]])
    *give_b, panel_b = give_product(ids, matrix, panels_b, [arrays_a[0]])
    got_b = [send(x, swap) for x in give_b]
    keep_b = keep_product(ids, matrix, panel_b, [to_b])
    keep_b, arrays_a[1] = lax.optimization_barrier((keep_b, arrays_a[1]))
    arrays_b = deliver(keep_b, got_b, partial_b, to_b, [])
    result = finish(ids, None, arrays_a, [arrays_b[0]])
    return finish(ids, result, arrays_b, [])


def solution(mesh):
    in_specs = (P("row", "col"), P(("row", "col"), None))
    out_specs = P(("row", "col"), None)
    return jax.shard_map(shards, mesh=mesh, in_specs=in_specs, out_specs=out_specs, check_vma=False)
```

```python
import functools

import jax
import jax.numpy as jnp
from jax import lax
from jax.experimental import pallas as pl
from jax.experimental.pallas import tpu as pltpu
from jax.sharding import PartitionSpec as P

TOP = 1400.0
TAIL = 16
VMEM = 6 * 2**20


def scale_for(largest):
    scale = TOP / jnp.maximum(largest, 1e-30)
    return scale.astype(jnp.bfloat16).astype(jnp.float32)


def encode(values, scale):
    x = values * scale
    x2 = x * x
    x4 = x2 * x2
    return (x * jnp.abs(x) * x2 * (x4 * x4)).astype(jnp.bfloat16)


def decode(coded, scale):
    y = coded.astype(jnp.float32)
    back = jnp.where(scale > 0, 1.0 / scale, 0.0)
    return y * jnp.exp2(-11 / 12 * jnp.log2(jnp.maximum(jnp.abs(y), 2.0**-126))) * back


def scale_of(message, rows, block):
    return message[pl.ds(rows + block * TAIL, TAIL), :][0:1, 0:1].astype(jnp.float32)


def put_scale(message, rows, block, scale):
    spread = jnp.full((TAIL, message.shape[1]), scale, jnp.float32).astype(jnp.bfloat16)
    message[pl.ds(rows + block * TAIL, TAIL), :] = spread


def local(kernel, out_shape, name, *operands, after=(), **options):
    count, skipped = len(operands), len(after)

    def body(*refs):
        kernel(*refs[:count], *refs[count + skipped :])

    return pl.pallas_call(
        body,
        out_shape=out_shape,
        in_specs=[pl.BlockSpec(memory_space=pltpu.SMEM)]
        + [pl.BlockSpec(memory_space=pltpu.VMEM)] * (count - 1)
        + [pl.BlockSpec(memory_space=pl.ANY)] * skipped,
        out_specs=jax.tree.map(lambda _: pl.BlockSpec(memory_space=pltpu.VMEM), out_shape),
        compiler_params=pltpu.CompilerParams(vmem_limit_bytes=VMEM),
        name=name,
        **options,
    )(*operands, *after)


def load_kernel(ids, a_ref, out_ref, diagonal, sem):
    height, cols = a_ref.shape
    block = cols // 4
    diagonal[...] = jnp.zeros_like(diagonal)

    @pl.when(ids[1] <= ids[0])
    def _():
        copy = pltpu.make_async_copy(a_ref, out_ref, sem)
        copy.start()
        copy.wait()

    for part in range(4):
        here = pl.ds(part * block, block)

        @pl.when(ids[1] == ids[0])
        def _():
            @pl.loop(0, height // block)
            def _(at):
                first = ids[3] + at * block
                rows = pl.ds(pl.multiple_of(at * block, block), block)

                @pl.when(first < part * block)
                def _():
                    out_ref[rows, here] = jnp.zeros((block, block), out_ref.dtype)

                @pl.when(first == part * block)
                def _():
                    tile = out_ref[rows, here]
                    empty = jnp.zeros_like(tile)
                    row = lax.broadcasted_iota(jnp.int32, tile.shape, 0)
                    col = lax.broadcasted_iota(jnp.int32, tile.shape, 1)
                    out_ref[rows, here] = jnp.where(row >= col, tile, empty)
                    on = jnp.where(row == col, tile, empty).astype(jnp.float32)
                    diagonal[:, here] = jnp.broadcast_to(jnp.sum(on, axis=0, keepdims=True), (8, block))


def load(ids, trailing):
    return pl.pallas_call(
        load_kernel,
        out_shape=[
            jax.ShapeDtypeStruct(trailing.shape, trailing.dtype),
            jax.ShapeDtypeStruct((8, trailing.shape[1]), jnp.float32),
        ],
        in_specs=[pl.BlockSpec(memory_space=pltpu.SMEM), pl.BlockSpec(memory_space=pltpu.HBM)],
        out_specs=[pl.BlockSpec(memory_space=pltpu.VMEM)] * 2,
        scratch_shapes=[pltpu.SemaphoreType.DMA],
        compiler_params=pltpu.CompilerParams(vmem_limit_bytes=VMEM),
        name="load",
    )(ids, trailing)


def line_kernel(places, ids, *refs):
    *came, out_a, out_b = refs
    height = came[0].shape[0]
    width = out_a.shape[1]
    for place, piece in zip(places, came):
        chip, there = place(ids[1])

        @pl.when(there)
        def _():
            to = pl.ds(pl.multiple_of(chip * height, height), height)
            out_a[to, :] = piece[:, pl.ds(0, width)]
            out_b[to, :] = piece[:, pl.ds(width, width)]


def line(ids, came, places, after):
    height, width = came[0].shape
    chips = 4 if len(came) == 5 else len(came)
    out_shape = [jax.ShapeDtypeStruct((height * chips, width // 2), came[0].dtype)] * 2
    return local(functools.partial(line_kernel, places), out_shape, "line", ids, *came, after=after)


def half_kernel(height, ids, mine, other, out_ref):
    count = out_ref.shape[0] // height
    for at in range(count // 2):
        chip = ids[2] * (count // 2) + at
        here = pl.ds(pl.multiple_of(chip * height, height), height)
        for core, ref in ((ids[2], mine), (1 - ids[2], other)):
            to = pl.ds(pl.multiple_of((2 * at + core) * height, height), height)
            out_ref[to, :] = ref[here, :]


def half(ids, mine, other, height):
    out_shape = jax.ShapeDtypeStruct(mine.shape, mine.dtype)
    return local(functools.partial(half_kernel, height), out_shape, "half", ids, mine, other)


def mirrored_kernel(piece, ids, a_ref, diagonal, mine, other, m_ref, msg_ref, turned):
    height, cols = a_ref.shape
    block = cols // 4
    used = ids[1] <= ids[0]

    @pl.loop(0, height // piece // 2)
    def _(at):
        rows = pl.ds(pl.multiple_of(at * piece, piece), piece)
        for core, ref in ((ids[2], mine), (1 - ids[2], other)):
            turned[:, pl.ds(pl.multiple_of((2 * at + core) * piece, piece), piece)] = ref[rows, :].T

    @pl.loop(0, 4)
    def _(part):
        here = pl.ds(pl.multiple_of(part * block, block), block)

        @pl.when(used)
        def _():
            m_ref[here, :] = jnp.dot(turned[...], a_ref[:, here], preferred_element_type=jnp.float32).T

        @pl.when(jnp.logical_not(used))
        def _():
            m_ref[here, :] = jnp.zeros((block, m_ref.shape[1]), jnp.float32)

        @pl.when(ids[1] == ids[0])
        def _():
            rows = pl.ds(pl.multiple_of(part * block - ids[3], block), block)
            m_ref[here, :] -= (turned[:, rows].astype(jnp.float32) * diagonal[0:1, here]).T

        total = m_ref[here, :]
        scale = scale_for(jnp.max(jnp.abs(total), keepdims=True))
        msg_ref[here, :] = encode(total, scale)
        put_scale(msg_ref, cols, part, scale)


def mirrored_product(ids, matrix, diagonal, mine, other, piece, after):
    rows, cols = matrix.shape
    width = mine.shape[1]
    out_shape = [
        jax.ShapeDtypeStruct((cols, width), jnp.float32),
        jax.ShapeDtypeStruct((cols + 4 * TAIL, width), jnp.bfloat16),
    ]
    return local(
        functools.partial(mirrored_kernel, piece), out_shape, "mirrored_product",
        ids, matrix, diagonal, mine, other, after=after,
        scratch_shapes=[pltpu.VMEM((width, rows), jnp.bfloat16)],
    )


def relay_kernel(ids, m_ref, in_ref, sum_ref, msg_ref):
    rows, width = m_ref.shape
    height = rows // 4

    @pl.loop(0, 4)
    def _(part):
        at = pl.ds(pl.multiple_of(part * height, height), height)
        total = m_ref[at, :] + decode(in_ref[at, :], scale_of(in_ref, rows, part))
        scale = scale_for(jnp.max(jnp.abs(total), keepdims=True))
        sum_ref[at, :] = total
        msg_ref[at, :] = encode(total, scale)
        put_scale(msg_ref, rows, part, scale)


def relay(ids, partial, message, after):
    out_shape = [jax.ShapeDtypeStruct(x.shape, x.dtype) for x in (partial, message)]
    return local(relay_kernel, out_shape, "relay", ids, partial, message, after=after)


def pick(ids, panels, panel, sem):
    for place, ref in enumerate(panels):

        @pl.when(ids[4] == place)
        def _():
            copy = pltpu.make_async_copy(ref, panel, sem)
            copy.start()
            copy.wait()


def give_kernel(ids, a_ref, *refs):
    *panels, give_ref, give_too, panel, sem = refs
    pick(ids, panels, panel, sem)
    rows_kernel(ids, a_ref, panel, give_ref, core=1 - ids[2], of=2)
    rows_kernel(ids, a_ref, panel, give_too, core=1 - ids[2], at=1, of=2)


def direct_kernel(ids, a_ref, *refs):
    *panels, keep_ref, give_ref, give_too, panel, sem = refs
    pick(ids, panels, panel, sem)
    rows_kernel(ids, a_ref, panel, give_ref, core=1 - ids[2], of=2)
    rows_kernel(ids, a_ref, panel, give_too, core=1 - ids[2], at=1, of=2)
    rows_kernel(ids, a_ref, panel, keep_ref)


def rows_kernel(ids, a_ref, panel, out_ref, core=None, at=0, of=1):
    core = ids[2] if core is None else core
    rows = out_ref.shape[0]
    height = rows * of // 4
    skip = at * rows

    @pl.when(ids[1] <= ids[0])
    def _():
        @pl.loop(0, 4 // of)
        def _(part):
            at = pl.ds(pl.multiple_of(core * rows * of + skip + part * height, height), height)
            to = pl.ds(pl.multiple_of(part * height, height), height)
            out_ref[to, :] = jnp.dot(a_ref[at, :], panel[...], preferred_element_type=jnp.float32)


def direct_product(ids, matrix, panels, after):
    rows, cols = matrix.shape
    width = panels[0].shape[1]
    out_shape = [jax.ShapeDtypeStruct((rows // parts, width), jnp.float32) for parts in (2, 4, 4)]
    return local(
        direct_kernel, out_shape, "direct_product", ids, matrix, *panels, after=after,
        scratch_shapes=[pltpu.VMEM((cols, width), jnp.bfloat16), pltpu.SemaphoreType.DMA],
    )


def give_product(ids, matrix, panels, after):
    rows, cols = matrix.shape
    width = panels[0].shape[1]
    out_shape = [
        *[jax.ShapeDtypeStruct((rows // 4, width), jnp.float32)] * 2,
        jax.ShapeDtypeStruct((cols, width), jnp.bfloat16),
    ]
    return local(
        give_kernel, out_shape, "give_product", ids, matrix, *panels, after=after,
        scratch_shapes=[pltpu.SemaphoreType.DMA],
    )


def keep_product(ids, matrix, panel, after):
    rows, cols = matrix.shape
    width = panel.shape[1]
    out_shape = jax.ShapeDtypeStruct((rows // 2, width), jnp.float32)
    return local(
        rows_kernel, out_shape, "keep_product", ids, matrix, panel, after=after
    )


def pack_kernel(count, ids, a_ref, *refs):
    theirs, (sum_ref, in_ref, own_ref, *msgs, total) = refs[:count], refs[count:]
    height = own_ref.shape[0]
    rounds = len(msgs)
    rows = rounds * height
    tile = rows // 4
    chip, core = ids[1], ids[2]

    for part in range(4):
        at = pl.ds(part * tile, tile)
        b_ref, where = theirs[part * count // 4], part * tile % theirs[0].shape[0]
        total[at, :] = a_ref[at, :] + b_ref[pl.ds(where, tile), :]

    @pl.when(ids[0] == chip)
    def _():
        @pl.loop(0, 4)
        def _(part):
            at = pl.ds(pl.multiple_of(part * tile, tile), tile)
            total[at, :] += sum_ref[at, :] + decode(in_ref[at, :], scale_of(in_ref, rows, part))

    for step, msg in enumerate(msgs):
        at = pl.ds(pl.multiple_of(lax.rem(chip + step, rounds) * height, height), height)
        values = total[at, :]
        scale = scale_for(jnp.max(jnp.abs(values), keepdims=True))
        msg[pl.ds(0, height), :] = encode(values, scale)
        put_scale(msg, height, 0, scale)

    stays = (chip <= ids[0]) & (lax.div(chip, rounds // 2) == core)

    @pl.when(stays)
    def _():
        place = 2 * lax.rem(chip, rounds // 2) + core
        own_ref[...] = total[pl.ds(pl.multiple_of(place * height, height), height), :]

    @pl.when(jnp.logical_not(stays))
    def _():
        own_ref[...] = jnp.zeros_like(own_ref)


def pack(ids, mine, theirs, partial, message, rounds, after):
    rows, width = mine.shape
    height = rows // rounds
    out_shape = [
        jax.ShapeDtypeStruct((height, width), jnp.float32),
        *[jax.ShapeDtypeStruct((height + TAIL, width), jnp.bfloat16)] * rounds,
    ]
    return local(
        functools.partial(pack_kernel, len(theirs)), out_shape, "pack", ids, mine, *theirs, partial, message, after=after,
        scratch_shapes=[pltpu.VMEM((rows, width), jnp.float32)],
    )


def finish_kernel(ids, before, own, *refs):
    *messages, out_ref = refs
    height, width = own.shape
    total = own[...]
    for message in messages:
        total += decode(message[pl.ds(0, height), :], scale_of(message, height, 0))
    done = out_ref.shape[1] - width
    if done:
        out_ref[:, pl.ds(0, done)] = before[:, pl.ds(0, done)]
    out_ref[:, pl.ds(done, width)] = total


def finish(ids, before, arrays, after):
    height, width = arrays[0].shape
    done = 0 if before is None else before.shape[1]
    out_shape = jax.ShapeDtypeStruct((height, done + width), jnp.float32)
    return local(finish_kernel, out_shape, "finish", ids, arrays[0] if before is None else before, *arrays, after=after)


def shards(trailing, panel_vectors):
    rows_here, cols_here = trailing.shape
    piece = panel_vectors.shape[0]
    count = lax.axis_size("row")
    devices_along = lax.axis_size("col")
    chips = devices_along // 2
    bits = count.bit_length() - 1
    row, col = lax.axis_index("row"), lax.axis_index("col")
    chip, core = col // 2, col % 2

    def at(row, chip, core):
        return (row * chips + chip) * 2 + core

    def turned(place, core):
        if core == 0:
            return place
        return sum(((place >> b) & 1) << (bits - 1 - b) for b in range(bits))

    def send(x, pairs):
        return lax.ppermute(x, ("row", "col"), [(at(*s), at(*d)) for s, d in pairs])

    offset = row ^ chip
    reverse = sum(((offset >> b) & 1) << (bits - 1 - b) for b in range(bits))
    place = jnp.where(core == 0, offset, reverse)
    ids = jnp.stack([row, chip, core, row * rows_here - col * cols_here, place]).astype(jnp.int32)

    def needed(chip, core, place, bit):
        rest = range(0, count, 2 ** (bit + 1))
        return any(chip ^ turned(place | r, core) > chip for r in rest)

    everyone = [(k, c) for k in range(chips) for c in range(2)]

    active = [(r, k, c) for r in range(count) for k in range(r + 1) for c in range(2)]

    def spread(place, source):
        bit = place.bit_length() - 1
        before = place - (1 << bit)
        pairs = [
            ((k ^ turned(before, c), k, c), (k ^ turned(place, c), k, c))
            for k, c in everyone
            if needed(k, c, place, bit)
        ]
        return send(source, pairs)

    def collect(bit, message):
        pairs = [
            ((k ^ turned(p, c), k, c), (k ^ turned(p - (1 << bit), c), k, c))
            for k, c in everyone
            for p in range(1 << bit, 2 << bit)
            if needed(k, c, p, bit)
        ]
        return send(message, pairs)

    matrix, diagonal = load(ids, trailing)

    line_of = [(r, k, c) for r in range(count) for k in range(chips) for c in range(2)]

    def step(x, to, wanted):
        return send(x, [((r, k, c), (r, to(k), c)) for r, k, c in line_of if wanted(r, k)])

    def by_distance(block):
        came, places = [block], [lambda chip: (chip, chip >= 0)]
        for by in range(1, chips):
            came.append(step(block, lambda k: (k + by) % chips, lambda r, k: (k + by) % chips <= r))
            places.append(lambda chip, by=by: (lax.rem(chip + chips - by, chips), chip >= 0))
        return came, places

    four = [
        lambda chip: (chip, chip >= 0),
        lambda chip: (chip ^ 2, chip >= 0),
        lambda chip: (jnp.maximum(chip - 1, 0), chip > 0),
        lambda chip: (jnp.minimum(chip + 1, 3), chip < 3),
        lambda chip: (3 - chip, (chip == 0) | (chip == 3)),
    ]

    def two_away(block):
        return step(block, lambda k: k ^ 2, lambda r, k: k >= 2 or k + 2 <= r)

    def next_ones(block):
        up = step(block, lambda k: k + 1, lambda r, k: k + 1 <= r and k < 3)
        return [up, step(block, lambda k: k - 1, lambda r, k: 0 <= k - 1 <= r)]

    def ends(two):
        return step(two, lambda k: 3 * (k - 1), lambda r, k: k == 1 or (k == 2 and r == 3))

    swap = [((r, k, c), (r, k, 1 - c)) for r, k, c in active]

    def widen(panels, after):
        panels[0], panels[1], *_ = lax.optimization_barrier((panels[0], panels[1], *after))
        for place in range(2, count):
            panels.append(spread(place, panels[place - (1 << (place.bit_length() - 1))]))

    def relaying(partial, came, panels, after):
        for bit in reversed(range(bits - 1)):
            partial, message = relay(ids, partial, came, after)
            if panels:
                message, *panels[2:] = lax.optimization_barrier((message, *panels[2:]))
            came = collect(bit, message)
        return partial, came, message

    def deliver(keep, got, partial, came, after):
        own, *out = pack(ids, keep, got, partial, came, chips, after)
        arrays = [own]
        for step, x in enumerate(out):
            pairs = []
            for r, k, c in active:
                at = c * chips + (k + step) % chips
                if (at // 2, at % 2) != (k, c):
                    pairs.append(((r, k, c), (r, at // 2, at % 2)))
            arrays.append(send(x, pairs))
        return arrays

    if chips == 4:
        two = two_away(panel_vectors)
        later, matrix = lax.optimization_barrier((panel_vectors, matrix))
        came, places = [panel_vectors, two, *next_ones(later)], four
        two, matrix = lax.optimization_barrier((two, matrix))
        came.append(ends(two))
    else:
        came, places = by_distance(panel_vectors)
    mine_a, mine_b = line(ids, came, places, [])
    other_a, other_b = send(mine_a, swap), send(mine_b, swap)
    panels_a, panels_b = [half(ids, mine_a, other_a, piece)], [half(ids, mine_b, other_b, piece)]
    panels_a.append(spread(1, panels_a[0]))
    panels_b.append(spread(1, panels_b[0]))
    partial_a, message_a = mirrored_product(ids, matrix, diagonal, mine_a, other_a, piece, [])
    to_a = collect(bits - 1, message_a)
    partial_b, message_b = mirrored_product(ids, matrix, diagonal, mine_b, other_b, piece, [message_a])
    to_b = collect(bits - 1, message_b)
    widen(panels_a, [message_b])
    widen(panels_b, [panels_a[1]])
    partial_a, to_a, relayed = relaying(partial_a, to_a, [], [message_b, panels_b[1]])
    keep_a, *give_a = direct_product(ids, matrix, panels_a, [relayed])
    got_a = [send(x, swap) for x in give_a]
    partial_b, to_b, relayed = relaying(partial_b, to_b, [], [keep_a, to_a, panels_b[2]])
    arrays_a = deliver(keep_a, got_a, partial_a, to_a, [relayed, *panels_b[3:]])
    *give_b, panel_b = give_product(ids, matrix, panels_b, [arrays_a[0]])
    got_b = [send(x, swap) for x in give_b]
    keep_b = keep_product(ids, matrix, panel_b, [to_b])
    keep_b, arrays_a[1] = lax.optimization_barrier((keep_b, arrays_a[1]))
    arrays_b = deliver(keep_b, got_b, partial_b, to_b, [])
    result = finish(ids, None, arrays_a, [arrays_b[0]])
    return finish(ids, result, arrays_b, [])


def solution(mesh):
    in_specs = (P("row", "col"), P(("row", "col"), None))
    out_specs = P(("row", "col"), None)
    return jax.shard_map(shards, mesh=mesh, in_specs=in_specs, out_specs=out_specs, check_vma=False)
```

```python
import functools

import jax
import jax.numpy as jnp
from jax import lax
from jax.experimental import pallas as pl
from jax.experimental.pallas import tpu as pltpu
from jax.sharding import PartitionSpec as P

TOP = 1400.0
TAIL = 16
VMEM = 6 * 2**20


def scale_for(largest):
    scale = TOP / jnp.maximum(largest, 1e-30)
    return scale.astype(jnp.bfloat16).astype(jnp.float32)


def encode(values, scale):
    x = values * scale
    x2 = x * x
    x4 = x2 * x2
    return (x * jnp.abs(x) * x2 * (x4 * x4)).astype(jnp.bfloat16)


def decode(coded, scale):
    y = coded.astype(jnp.float32)
    back = jnp.where(scale > 0, 1.0 / scale, 0.0)
    return y * jnp.exp2(-11 / 12 * jnp.log2(jnp.maximum(jnp.abs(y), 2.0**-126))) * back


def scale_of(message, rows, block):
    return message[pl.ds(rows + block * TAIL, TAIL), :][0:1, 0:1].astype(jnp.float32)


def put_scale(message, rows, block, scale):
    spread = jnp.full((TAIL, message.shape[1]), scale, jnp.float32).astype(jnp.bfloat16)
    message[pl.ds(rows + block * TAIL, TAIL), :] = spread


def local(kernel, out_shape, name, *operands, after=(), **options):
    count, skipped = len(operands), len(after)

    def body(*refs):
        kernel(*refs[:count], *refs[count + skipped :])

    return pl.pallas_call(
        body,
        out_shape=out_shape,
        in_specs=[pl.BlockSpec(memory_space=pltpu.SMEM)]
        + [pl.BlockSpec(memory_space=pltpu.VMEM)] * (count - 1)
        + [pl.BlockSpec(memory_space=pl.ANY)] * skipped,
        out_specs=jax.tree.map(lambda _: pl.BlockSpec(memory_space=pltpu.VMEM), out_shape),
        compiler_params=pltpu.CompilerParams(vmem_limit_bytes=VMEM),
        name=name,
        **options,
    )(*operands, *after)


def load_kernel(ids, a_ref, out_ref, diagonal, sem):
    height, cols = a_ref.shape
    block = cols // 4
    diagonal[...] = jnp.zeros_like(diagonal)

    @pl.when(ids[1] <= ids[0])
    def _():
        copy = pltpu.make_async_copy(a_ref, out_ref, sem)
        copy.start()
        copy.wait()

    for part in range(4):
        here = pl.ds(part * block, block)

        @pl.when(ids[1] == ids[0])
        def _():
            @pl.loop(0, height // block)
            def _(at):
                first = ids[3] + at * block
                rows = pl.ds(pl.multiple_of(at * block, block), block)

                @pl.when(first < part * block)
                def _():
                    out_ref[rows, here] = jnp.zeros((block, block), out_ref.dtype)

                @pl.when(first == part * block)
                def _():
                    tile = out_ref[rows, here]
                    empty = jnp.zeros_like(tile)
                    row = lax.broadcasted_iota(jnp.int32, tile.shape, 0)
                    col = lax.broadcasted_iota(jnp.int32, tile.shape, 1)
                    out_ref[rows, here] = jnp.where(row >= col, tile, empty)
                    on = jnp.where(row == col, tile, empty).astype(jnp.float32)
                    diagonal[:, here] = jnp.broadcast_to(jnp.sum(on, axis=0, keepdims=True), (8, block))


def load(ids, trailing):
    return pl.pallas_call(
        load_kernel,
        out_shape=[
            jax.ShapeDtypeStruct(trailing.shape, trailing.dtype),
            jax.ShapeDtypeStruct((8, trailing.shape[1]), jnp.float32),
        ],
        in_specs=[pl.BlockSpec(memory_space=pltpu.SMEM), pl.BlockSpec(memory_space=pltpu.HBM)],
        out_specs=[pl.BlockSpec(memory_space=pltpu.VMEM)] * 2,
        scratch_shapes=[pltpu.SemaphoreType.DMA],
        compiler_params=pltpu.CompilerParams(vmem_limit_bytes=VMEM),
        name="load",
    )(ids, trailing)


def line_kernel(places, ids, *refs):
    *came, out_a, out_b = refs
    height = came[0].shape[0]
    width = out_a.shape[1]
    for place, piece in zip(places, came):
        chip, there = place(ids[1])

        @pl.when(there)
        def _():
            to = pl.ds(pl.multiple_of(chip * height, height), height)
            out_a[to, :] = piece[:, pl.ds(0, width)]
            out_b[to, :] = piece[:, pl.ds(width, width)]


def line(ids, came, places, after):
    height, width = came[0].shape
    chips = 4 if len(came) == 5 else len(came)
    out_shape = [jax.ShapeDtypeStruct((height * chips, width // 2), came[0].dtype)] * 2
    return local(functools.partial(line_kernel, places), out_shape, "line", ids, *came, after=after)


def half_kernel(height, ids, mine, other, out_ref):
    count = out_ref.shape[0] // height
    for at in range(count // 2):
        chip = ids[2] * (count // 2) + at
        here = pl.ds(pl.multiple_of(chip * height, height), height)
        for core, ref in ((ids[2], mine), (1 - ids[2], other)):
            to = pl.ds(pl.multiple_of((2 * at + core) * height, height), height)
            out_ref[to, :] = ref[here, :]


def half(ids, mine, other, height):
    out_shape = jax.ShapeDtypeStruct(mine.shape, mine.dtype)
    return local(functools.partial(half_kernel, height), out_shape, "half", ids, mine, other)


def mirrored_kernel(piece, ids, a_ref, diagonal, mine, other, m_ref, msg_ref, turned):
    height, cols = a_ref.shape
    block = cols // 4
    used = ids[1] <= ids[0]

    @pl.loop(0, height // piece // 2)
    def _(at):
        rows = pl.ds(pl.multiple_of(at * piece, piece), piece)
        for core, ref in ((ids[2], mine), (1 - ids[2], other)):
            turned[:, pl.ds(pl.multiple_of((2 * at + core) * piece, piece), piece)] = ref[rows, :].T

    @pl.loop(0, 4)
    def _(part):
        here = pl.ds(pl.multiple_of(part * block, block), block)

        @pl.when(used)
        def _():
            m_ref[here, :] = jnp.dot(turned[...], a_ref[:, here], preferred_element_type=jnp.float32).T

        @pl.when(jnp.logical_not(used))
        def _():
            m_ref[here, :] = jnp.zeros((block, m_ref.shape[1]), jnp.float32)

        @pl.when(ids[1] == ids[0])
        def _():
            rows = pl.ds(pl.multiple_of(part * block - ids[3], block), block)
            m_ref[here, :] -= (turned[:, rows].astype(jnp.float32) * diagonal[0:1, here]).T

        total = m_ref[here, :]
        scale = scale_for(jnp.max(jnp.abs(total), keepdims=True))
        msg_ref[here, :] = encode(total, scale)
        put_scale(msg_ref, cols, part, scale)


def mirrored_product(ids, matrix, diagonal, mine, other, piece, after):
    rows, cols = matrix.shape
    width = mine.shape[1]
    out_shape = [
        jax.ShapeDtypeStruct((cols, width), jnp.float32),
        jax.ShapeDtypeStruct((cols + 4 * TAIL, width), jnp.bfloat16),
    ]
    return local(
        functools.partial(mirrored_kernel, piece), out_shape, "mirrored_product",
        ids, matrix, diagonal, mine, other, after=after,
        scratch_shapes=[pltpu.VMEM((width, rows), jnp.bfloat16)],
    )


def relay_kernel(ids, m_ref, in_ref, sum_ref, msg_ref):
    rows, width = m_ref.shape
    height = rows // 4

    @pl.loop(0, 4)
    def _(part):
        at = pl.ds(pl.multiple_of(part * height, height), height)
        total = m_ref[at, :] + decode(in_ref[at, :], scale_of(in_ref, rows, part))
        scale = scale_for(jnp.max(jnp.abs(total), keepdims=True))
        sum_ref[at, :] = total
        msg_ref[at, :] = encode(total, scale)
        put_scale(msg_ref, rows, part, scale)


def relay(ids, partial, message, after):
    out_shape = [jax.ShapeDtypeStruct(x.shape, x.dtype) for x in (partial, message)]
    return local(relay_kernel, out_shape, "relay", ids, partial, message, after=after)


def pick(ids, panels, panel, sem):
    for place, ref in enumerate(panels):

        @pl.when(ids[4] == place)
        def _():
            copy = pltpu.make_async_copy(ref, panel, sem)
            copy.start()
            copy.wait()


def give_kernel(ids, a_ref, *refs):
    *panels, give_ref, give_too, panel, sem = refs
    pick(ids, panels, panel, sem)
    rows_kernel(ids, a_ref, panel, give_ref, core=1 - ids[2], of=2)
    rows_kernel(ids, a_ref, panel, give_too, core=1 - ids[2], at=1, of=2)


def direct_kernel(ids, a_ref, *refs):
    *panels, keep_ref, give_ref, give_too, panel, sem = refs
    pick(ids, panels, panel, sem)
    rows_kernel(ids, a_ref, panel, give_ref, core=1 - ids[2], of=2)
    rows_kernel(ids, a_ref, panel, give_too, core=1 - ids[2], at=1, of=2)
    rows_kernel(ids, a_ref, panel, keep_ref)


def rows_kernel(ids, a_ref, panel, out_ref, core=None, at=0, of=1):
    core = ids[2] if core is None else core
    rows = out_ref.shape[0]
    height = rows * of // 4
    skip = at * rows

    @pl.when(ids[1] <= ids[0])
    def _():
        @pl.loop(0, 4 // of)
        def _(part):
            at = pl.ds(pl.multiple_of(core * rows * of + skip + part * height, height), height)
            to = pl.ds(pl.multiple_of(part * height, height), height)
            out_ref[to, :] = jnp.dot(a_ref[at, :], panel[...], preferred_element_type=jnp.float32)


def direct_product(ids, matrix, panels, after):
    rows, cols = matrix.shape
    width = panels[0].shape[1]
    out_shape = [jax.ShapeDtypeStruct((rows // parts, width), jnp.float32) for parts in (2, 4, 4)]
    return local(
        direct_kernel, out_shape, "direct_product", ids, matrix, *panels, after=after,
        scratch_shapes=[pltpu.VMEM((cols, width), jnp.bfloat16), pltpu.SemaphoreType.DMA],
    )


def give_product(ids, matrix, panels, after):
    rows, cols = matrix.shape
    width = panels[0].shape[1]
    out_shape = [
        *[jax.ShapeDtypeStruct((rows // 4, width), jnp.float32)] * 2,
        jax.ShapeDtypeStruct((cols, width), jnp.bfloat16),
    ]
    return local(
        give_kernel, out_shape, "give_product", ids, matrix, *panels, after=after,
        scratch_shapes=[pltpu.SemaphoreType.DMA],
    )


def keep_product(ids, matrix, panel, after):
    rows, cols = matrix.shape
    width = panel.shape[1]
    out_shape = jax.ShapeDtypeStruct((rows // 2, width), jnp.float32)
    return local(
        rows_kernel, out_shape, "keep_product", ids, matrix, panel, after=after
    )


def pack_kernel(count, sides, ids, a_ref, *refs):
    theirs, (sum_ref, in_ref, own_ref, *msgs, total) = refs[:count], refs[count:]
    height = own_ref.shape[0]
    rounds = len(msgs)
    rows = rounds * height
    tile = rows // 4
    chip, core = ids[1], ids[2]

    for part in range(4):
        at = pl.ds(part * tile, tile)
        b_ref, where = theirs[part * count // 4], part * tile % theirs[0].shape[0]
        total[at, :] = a_ref[at, :] + b_ref[pl.ds(where, tile), :]

    @pl.when(ids[0] == chip)
    def _():
        @pl.loop(0, 4)
        def _(part):
            at = pl.ds(pl.multiple_of(part * tile, tile), tile)
            total[at, :] += sum_ref[at, :] + decode(in_ref[at, :], scale_of(in_ref, rows, part))

    for step, msg in enumerate(msgs):
        at = pl.ds(pl.multiple_of(lax.rem(chip + step, rounds) * height, height), height)
        values = total[at, :]
        scale = scale_for(jnp.max(jnp.abs(values), keepdims=True))
        msg[pl.ds(0, height), :] = encode(values, scale)
        put_scale(msg, height, 0, scale)

    each = rounds // sides
    stays = (chip <= ids[0]) & (lax.div(chip, sides) == core)

    @pl.when(stays)
    def _():
        place = each * lax.rem(chip, sides) + (core if each > 1 else 0)
        own_ref[...] = total[pl.ds(pl.multiple_of(place * height, height), height), :]

    @pl.when(jnp.logical_not(stays))
    def _():
        own_ref[...] = jnp.zeros_like(own_ref)


def pack(ids, mine, theirs, partial, message, rounds, sides, after):
    rows, width = mine.shape
    height = rows // rounds
    out_shape = [
        jax.ShapeDtypeStruct((height, width), jnp.float32),
        *[jax.ShapeDtypeStruct((height + TAIL, width), jnp.bfloat16)] * rounds,
    ]
    return local(
        functools.partial(pack_kernel, len(theirs), sides), out_shape, "pack", ids, mine, *theirs, partial, message, after=after,
        scratch_shapes=[pltpu.VMEM((rows, width), jnp.float32)],
    )


def add_kernel(ids, own, *refs):
    *messages, keep_ref, give_ref, give_too = refs
    height, half_way = keep_ref.shape[0], give_ref.shape[0]
    for core, first, out_ref in ((ids[2], 0, keep_ref), (1 - ids[2], 0, give_ref), (1 - ids[2], half_way, give_too)):
        at = pl.ds(pl.multiple_of(core * height + first, half_way), out_ref.shape[0])
        total = own[at, :]
        for message in messages:
            total += decode(message[at, :], scale_of(message, own.shape[0], 0))
        out_ref[...] = total


def add(ids, arrays, after):
    rows, width = arrays[0].shape
    out_shape = [jax.ShapeDtypeStruct((rows // parts, width), jnp.float32) for parts in (2, 4, 4)]
    return local(add_kernel, out_shape, "add", ids, *arrays, after=after)


def finish_kernel(ids, mine, other, other_too, own, *refs):
    *messages, out_ref = refs
    height, width = own.shape
    half_way = other.shape[0]
    for first, ref in ((0, other), (half_way, other_too)):
        at = pl.ds(first, half_way)
        out_ref[at, pl.ds(0, width)] = mine[at, :] + ref[...]
    total = own[...]
    for message in messages:
        total += decode(message[pl.ds(0, height), :], scale_of(message, height, 0))
    out_ref[:, pl.ds(width, width)] = total


def finish(ids, mine, others, arrays):
    height, width = mine.shape
    out_shape = jax.ShapeDtypeStruct((height, 2 * width), jnp.float32)
    return local(finish_kernel, out_shape, "finish", ids, mine, *others, *arrays)


def shards(trailing, panel_vectors):
    rows_here, cols_here = trailing.shape
    piece = panel_vectors.shape[0]
    count = lax.axis_size("row")
    devices_along = lax.axis_size("col")
    chips = devices_along // 2
    bits = count.bit_length() - 1
    row, col = lax.axis_index("row"), lax.axis_index("col")
    chip, core = col // 2, col % 2

    def at(row, chip, core):
        return (row * chips + chip) * 2 + core

    def turned(place, core):
        if core == 0:
            return place
        return sum(((place >> b) & 1) << (bits - 1 - b) for b in range(bits))

    def send(x, pairs):
        return lax.ppermute(x, ("row", "col"), [(at(*s), at(*d)) for s, d in pairs])

    offset = row ^ chip
    reverse = sum(((offset >> b) & 1) << (bits - 1 - b) for b in range(bits))
    place = jnp.where(core == 0, offset, reverse)
    ids = jnp.stack([row, chip, core, row * rows_here - col * cols_here, place]).astype(jnp.int32)

    def needed(chip, core, place, bit):
        rest = range(0, count, 2 ** (bit + 1))
        return any(chip ^ turned(place | r, core) > chip for r in rest)

    everyone = [(k, c) for k in range(chips) for c in range(2)]

    active = [(r, k, c) for r in range(count) for k in range(r + 1) for c in range(2)]

    def spread(place, source):
        bit = place.bit_length() - 1
        before = place - (1 << bit)
        pairs = [
            ((k ^ turned(before, c), k, c), (k ^ turned(place, c), k, c))
            for k, c in everyone
            if needed(k, c, place, bit)
        ]
        return send(source, pairs)

    def collect(bit, message):
        pairs = [
            ((k ^ turned(p, c), k, c), (k ^ turned(p - (1 << bit), c), k, c))
            for k, c in everyone
            for p in range(1 << bit, 2 << bit)
            if needed(k, c, p, bit)
        ]
        return send(message, pairs)

    matrix, diagonal = load(ids, trailing)

    line_of = [(r, k, c) for r in range(count) for k in range(chips) for c in range(2)]

    def step(x, to, wanted):
        return send(x, [((r, k, c), (r, to(k), c)) for r, k, c in line_of if wanted(r, k)])

    def by_distance(block):
        came, places = [block], [lambda chip: (chip, chip >= 0)]
        for by in range(1, chips):
            came.append(step(block, lambda k: (k + by) % chips, lambda r, k: (k + by) % chips <= r))
            places.append(lambda chip, by=by: (lax.rem(chip + chips - by, chips), chip >= 0))
        return came, places

    four = [
        lambda chip: (chip, chip >= 0),
        lambda chip: (chip ^ 2, chip >= 0),
        lambda chip: (jnp.maximum(chip - 1, 0), chip > 0),
        lambda chip: (jnp.minimum(chip + 1, 3), chip < 3),
        lambda chip: (3 - chip, (chip == 0) | (chip == 3)),
    ]

    def two_away(block):
        return step(block, lambda k: k ^ 2, lambda r, k: k >= 2 or k + 2 <= r)

    def next_ones(block):
        up = step(block, lambda k: k + 1, lambda r, k: k + 1 <= r and k < 3)
        return [up, step(block, lambda k: k - 1, lambda r, k: 0 <= k - 1 <= r)]

    def ends(two):
        return step(two, lambda k: 3 * (k - 1), lambda r, k: k == 1 or (k == 2 and r == 3))

    swap = [((r, k, c), (r, k, 1 - c)) for r, k, c in active]

    def widen(panels, after):
        panels[0], panels[1], *_ = lax.optimization_barrier((panels[0], panels[1], *after))
        for place in range(2, count):
            panels.append(spread(place, panels[place - (1 << (place.bit_length() - 1))]))

    def relaying(partial, came, panels, after):
        for bit in reversed(range(bits - 1)):
            partial, message = relay(ids, partial, came, after)
            if panels:
                message, *panels[2:] = lax.optimization_barrier((message, *panels[2:]))
            came = collect(bit, message)
        return partial, came, message

    def deliver(keep, got, partial, came, rounds, after):
        sides = chips // 2
        own, *out = pack(ids, keep, got, partial, came, rounds, sides, after)
        arrays = [own]
        for step, x in enumerate(out):
            pairs = []
            for r, k, c in active:
                at = (k + step) % rounds
                to = (c * sides + at // 2, at % 2) if rounds > sides else (c * sides + at, k // sides)
                if to != (k, c):
                    pairs.append(((r, k, c), (r, *to)))
            arrays.append(send(x, pairs))
        return arrays

    all_swap = [((r, k, c), (r, k, 1 - c)) for r, k, c in line_of]

    if chips == 4:
        two = two_away(panel_vectors)
        came, places = [panel_vectors, two, *next_ones(panel_vectors)], four
        two, matrix = lax.optimization_barrier((two, matrix))
        came.append(ends(two))
    else:
        came, places = by_distance(panel_vectors)
    mine_a, mine_b = line(ids, came, places, [])
    other_a, other_b = send(mine_a, swap), send(mine_b, swap)
    panels_a, panels_b = [half(ids, mine_a, other_a, piece)], [half(ids, mine_b, other_b, piece)]
    panels_a.append(spread(1, panels_a[0]))
    panels_b.append(spread(1, panels_b[0]))
    partial_a, message_a = mirrored_product(ids, matrix, diagonal, mine_a, other_a, piece, [])
    to_a = collect(bits - 1, message_a)
    partial_b, message_b = mirrored_product(ids, matrix, diagonal, mine_b, other_b, piece, [message_a])
    to_b = collect(bits - 1, message_b)
    widen(panels_a, [message_b])
    widen(panels_b, [panels_a[1]])
    partial_a, to_a, relayed = relaying(partial_a, to_a, [], [message_b, panels_b[1]])
    keep_a, *give_a = direct_product(ids, matrix, panels_a, [relayed])
    got_a = [send(x, swap) for x in give_a]
    partial_b, to_b, relayed = relaying(partial_b, to_b, [], [keep_a, to_a, panels_b[2]])
    arrays_a = deliver(keep_a, got_a, partial_a, to_a, chips // 2, [relayed, *panels_b[3:]])
    *give_b, panel_b = give_product(ids, matrix, panels_b, [arrays_a[0]])
    got_b = [send(x, swap) for x in give_b]
    keep_b = keep_product(ids, matrix, panel_b, [to_b])
    arrays_b = deliver(keep_b, got_b, partial_b, to_b, chips, [])
    mine_sum, *gives = add(ids, arrays_a, [arrays_b[1]])
    return finish(ids, mine_sum, [send(x, all_swap) for x in gives], arrays_b)


def solution(mesh):
    in_specs = (P("row", "col"), P(("row", "col"), None))
    out_specs = P(("row", "col"), None)
    return jax.shard_map(shards, mesh=mesh, in_specs=in_specs, out_specs=out_specs, check_vma=False)
```

```python
import functools

import jax
import jax.numpy as jnp
from jax import lax
from jax.experimental import pallas as pl
from jax.experimental.pallas import tpu as pltpu
from jax.sharding import PartitionSpec as P

TOP = 1400.0
TAIL = 16
VMEM = 6 * 2**20


def scale_for(largest):
    scale = TOP / jnp.maximum(largest, 1e-30)
    return scale.astype(jnp.bfloat16).astype(jnp.float32)


def encode(values, scale):
    x = values * scale
    x2 = x * x
    x4 = x2 * x2
    return (x * jnp.abs(x) * x2 * (x4 * x4)).astype(jnp.bfloat16)


def decode(coded, scale):
    y = coded.astype(jnp.float32)
    back = jnp.where(scale > 0, 1.0 / scale, 0.0)
    return y * jnp.exp2(-11 / 12 * jnp.log2(jnp.maximum(jnp.abs(y), 2.0**-126))) * back


def scale_of(message, rows, block):
    return message[pl.ds(rows + block * TAIL, TAIL), :][0:1, 0:1].astype(jnp.float32)


def put_scale(message, rows, block, scale):
    spread = jnp.full((TAIL, message.shape[1]), scale, jnp.float32).astype(jnp.bfloat16)
    message[pl.ds(rows + block * TAIL, TAIL), :] = spread


def local(kernel, out_shape, name, *operands, after=(), **options):
    count, skipped = len(operands), len(after)

    def body(*refs):
        kernel(*refs[:count], *refs[count + skipped :])

    return pl.pallas_call(
        body,
        out_shape=out_shape,
        in_specs=[pl.BlockSpec(memory_space=pltpu.SMEM)]
        + [pl.BlockSpec(memory_space=pltpu.VMEM)] * (count - 1)
        + [pl.BlockSpec(memory_space=pl.ANY)] * skipped,
        out_specs=jax.tree.map(lambda _: pl.BlockSpec(memory_space=pltpu.VMEM), out_shape),
        compiler_params=pltpu.CompilerParams(vmem_limit_bytes=VMEM),
        name=name,
        **options,
    )(*operands, *after)


def load_kernel(ids, a_ref, out_ref, diagonal, sem):
    height, cols = a_ref.shape
    block = cols // 4
    diagonal[...] = jnp.zeros_like(diagonal)

    @pl.when(ids[1] <= ids[0])
    def _():
        copy = pltpu.make_async_copy(a_ref, out_ref, sem)
        copy.start()
        copy.wait()

    for part in range(4):
        here = pl.ds(part * block, block)

        @pl.when(ids[1] == ids[0])
        def _():
            @pl.loop(0, height // block)
            def _(at):
                first = ids[3] + at * block
                rows = pl.ds(pl.multiple_of(at * block, block), block)

                @pl.when(first < part * block)
                def _():
                    out_ref[rows, here] = jnp.zeros((block, block), out_ref.dtype)

                @pl.when(first == part * block)
                def _():
                    tile = out_ref[rows, here]
                    empty = jnp.zeros_like(tile)
                    row = lax.broadcasted_iota(jnp.int32, tile.shape, 0)
                    col = lax.broadcasted_iota(jnp.int32, tile.shape, 1)
                    out_ref[rows, here] = jnp.where(row >= col, tile, empty)
                    on = jnp.where(row == col, tile, empty).astype(jnp.float32)
                    diagonal[:, here] = jnp.broadcast_to(jnp.sum(on, axis=0, keepdims=True), (8, block))


def load(ids, trailing):
    return pl.pallas_call(
        load_kernel,
        out_shape=[
            jax.ShapeDtypeStruct(trailing.shape, trailing.dtype),
            jax.ShapeDtypeStruct((8, trailing.shape[1]), jnp.float32),
        ],
        in_specs=[pl.BlockSpec(memory_space=pltpu.SMEM), pl.BlockSpec(memory_space=pltpu.HBM)],
        out_specs=[pl.BlockSpec(memory_space=pltpu.VMEM)] * 2,
        scratch_shapes=[pltpu.SemaphoreType.DMA],
        compiler_params=pltpu.CompilerParams(vmem_limit_bytes=VMEM),
        name="load",
    )(ids, trailing)


def line_kernel(places, ids, *refs):
    *came, out_a, out_b = refs
    height = came[0].shape[0]
    width = out_a.shape[1]
    for place, piece in zip(places, came):
        chip, there = place(ids[1])

        @pl.when(there)
        def _():
            to = pl.ds(pl.multiple_of(chip * height, height), height)
            out_a[to, :] = piece[:, pl.ds(0, width)]
            out_b[to, :] = piece[:, pl.ds(width, width)]


def line(ids, came, places, after):
    height, width = came[0].shape
    chips = 4 if len(came) == 5 else len(came)
    out_shape = [jax.ShapeDtypeStruct((height * chips, width // 2), came[0].dtype)] * 2
    return local(functools.partial(line_kernel, places), out_shape, "line", ids, *came, after=after)


def half_kernel(height, ids, mine, other, out_ref):
    count = out_ref.shape[0] // height
    for at in range(count // 2):
        chip = ids[2] * (count // 2) + at
        here = pl.ds(pl.multiple_of(chip * height, height), height)
        for core, ref in ((ids[2], mine), (1 - ids[2], other)):
            to = pl.ds(pl.multiple_of((2 * at + core) * height, height), height)
            out_ref[to, :] = ref[here, :]


def half(ids, mine, other, height):
    out_shape = jax.ShapeDtypeStruct(mine.shape, mine.dtype)
    return local(functools.partial(half_kernel, height), out_shape, "half", ids, mine, other)


def mirrored_kernel(piece, ids, a_ref, diagonal, mine, other, m_ref, msg_ref, turned):
    height, cols = a_ref.shape
    block = cols // 4
    used = ids[1] <= ids[0]

    @pl.loop(0, height // piece // 2)
    def _(at):
        rows = pl.ds(pl.multiple_of(at * piece, piece), piece)
        for core, ref in ((ids[2], mine), (1 - ids[2], other)):
            turned[:, pl.ds(pl.multiple_of((2 * at + core) * piece, piece), piece)] = ref[rows, :].T

    @pl.loop(0, 4)
    def _(part):
        here = pl.ds(pl.multiple_of(part * block, block), block)

        @pl.when(used & (ids[1] != ids[0]))
        def _():
            m_ref[here, :] = jnp.dot(turned[...], a_ref[:, here], preferred_element_type=jnp.float32).T

        @pl.when(ids[1] == ids[0])
        def _():
            rows = pl.ds(pl.multiple_of(part * block - ids[3], block), block)
            total = jnp.dot(turned[...], a_ref[:, here], preferred_element_type=jnp.float32)
            m_ref[here, :] = (total - turned[:, rows].astype(jnp.float32) * diagonal[0:1, here]).T

        @pl.when(jnp.logical_not(used))
        def _():
            m_ref[here, :] = jnp.zeros((block, m_ref.shape[1]), jnp.float32)

        total = m_ref[here, :]
        scale = scale_for(jnp.max(jnp.abs(total), keepdims=True))
        msg_ref[here, :] = encode(total, scale)
        put_scale(msg_ref, cols, part, scale)


def mirrored_product(ids, matrix, diagonal, mine, other, piece, after):
    rows, cols = matrix.shape
    width = mine.shape[1]
    out_shape = [
        jax.ShapeDtypeStruct((cols, width), jnp.float32),
        jax.ShapeDtypeStruct((cols + 4 * TAIL, width), jnp.bfloat16),
    ]
    return local(
        functools.partial(mirrored_kernel, piece), out_shape, "mirrored_product",
        ids, matrix, diagonal, mine, other, after=after,
        scratch_shapes=[pltpu.VMEM((width, rows), jnp.bfloat16)],
    )


def relay_kernel(ids, m_ref, in_ref, sum_ref, msg_ref):
    rows, width = m_ref.shape
    height = rows // 4

    @pl.loop(0, 4)
    def _(part):
        at = pl.ds(pl.multiple_of(part * height, height), height)
        total = m_ref[at, :] + decode(in_ref[at, :], scale_of(in_ref, rows, part))
        scale = scale_for(jnp.max(jnp.abs(total), keepdims=True))
        sum_ref[at, :] = total
        msg_ref[at, :] = encode(total, scale)
        put_scale(msg_ref, rows, part, scale)


def relay(ids, partial, message, after):
    out_shape = [jax.ShapeDtypeStruct(x.shape, x.dtype) for x in (partial, message)]
    return local(relay_kernel, out_shape, "relay", ids, partial, message, after=after)


def pick(ids, panels, panel, sem):
    for place, ref in enumerate(panels):

        @pl.when(ids[4] == place)
        def _():
            copy = pltpu.make_async_copy(ref, panel, sem)
            copy.start()
            copy.wait()


def give_kernel(ids, a_ref, *refs):
    *panels, give_ref, give_too, panel, sem = refs
    pick(ids, panels, panel, sem)
    rows_kernel(ids, a_ref, panel, give_ref, core=1 - ids[2], of=2)
    rows_kernel(ids, a_ref, panel, give_too, core=1 - ids[2], at=1, of=2)


def direct_kernel(ids, a_ref, *refs):
    *panels, keep_ref, give_ref, give_too, panel, sem = refs
    pick(ids, panels, panel, sem)
    rows_kernel(ids, a_ref, panel, give_ref, core=1 - ids[2], of=2)
    rows_kernel(ids, a_ref, panel, give_too, core=1 - ids[2], at=1, of=2)
    rows_kernel(ids, a_ref, panel, keep_ref)


def rows_kernel(ids, a_ref, panel, out_ref, core=None, at=0, of=1):
    core = ids[2] if core is None else core
    rows = out_ref.shape[0]
    height = rows * of // 4
    skip = at * rows

    @pl.when(ids[1] <= ids[0])
    def _():
        @pl.loop(0, 4 // of)
        def _(part):
            at = pl.ds(pl.multiple_of(core * rows * of + skip + part * height, height), height)
            to = pl.ds(pl.multiple_of(part * height, height), height)
            out_ref[to, :] = jnp.dot(a_ref[at, :], panel[...], preferred_element_type=jnp.float32)


def direct_product(ids, matrix, panels, after):
    rows, cols = matrix.shape
    width = panels[0].shape[1]
    out_shape = [jax.ShapeDtypeStruct((rows // parts, width), jnp.float32) for parts in (2, 4, 4)]
    return local(
        direct_kernel, out_shape, "direct_product", ids, matrix, *panels, after=after,
        scratch_shapes=[pltpu.VMEM((cols, width), jnp.bfloat16), pltpu.SemaphoreType.DMA],
    )


def give_product(ids, matrix, panels, after):
    rows, cols = matrix.shape
    width = panels[0].shape[1]
    out_shape = [
        *[jax.ShapeDtypeStruct((rows // 4, width), jnp.float32)] * 2,
        jax.ShapeDtypeStruct((cols, width), jnp.bfloat16),
    ]
    return local(
        give_kernel, out_shape, "give_product", ids, matrix, *panels, after=after,
        scratch_shapes=[pltpu.SemaphoreType.DMA],
    )


def keep_product(ids, matrix, panel, after):
    rows, cols = matrix.shape
    width = panel.shape[1]
    out_shape = jax.ShapeDtypeStruct((rows // 2, width), jnp.float32)
    return local(
        rows_kernel, out_shape, "keep_product", ids, matrix, panel, after=after
    )


def pack_kernel(count, sides, ids, a_ref, *refs):
    theirs, (sum_ref, in_ref, own_ref, *msgs, total) = refs[:count], refs[count:]
    height = own_ref.shape[0]
    rounds = len(msgs)
    rows = rounds * height
    tile = rows // 4
    chip, core = ids[1], ids[2]

    for part in range(4):
        at = pl.ds(part * tile, tile)
        b_ref, where = theirs[part * count // 4], part * tile % theirs[0].shape[0]
        total[at, :] = a_ref[at, :] + b_ref[pl.ds(where, tile), :]

    @pl.when(ids[0] == chip)
    def _():
        @pl.loop(0, 4)
        def _(part):
            at = pl.ds(pl.multiple_of(part * tile, tile), tile)
            total[at, :] += sum_ref[at, :] + decode(in_ref[at, :], scale_of(in_ref, rows, part))

    for step, msg in enumerate(msgs):
        at = pl.ds(pl.multiple_of(lax.rem(chip + step, rounds) * height, height), height)
        values = total[at, :]
        scale = scale_for(jnp.max(jnp.abs(values), keepdims=True))
        msg[pl.ds(0, height), :] = encode(values, scale)
        put_scale(msg, height, 0, scale)

    each = rounds // sides
    stays = (chip <= ids[0]) & (lax.div(chip, sides) == core)

    @pl.when(stays)
    def _():
        place = each * lax.rem(chip, sides) + (core if each > 1 else 0)
        own_ref[...] = total[pl.ds(pl.multiple_of(place * height, height), height), :]

    @pl.when(jnp.logical_not(stays))
    def _():
        own_ref[...] = jnp.zeros_like(own_ref)


def pack(ids, mine, theirs, partial, message, rounds, sides, after):
    rows, width = mine.shape
    height = rows // rounds
    out_shape = [
        jax.ShapeDtypeStruct((height, width), jnp.float32),
        *[jax.ShapeDtypeStruct((height + TAIL, width), jnp.bfloat16)] * rounds,
    ]
    return local(
        functools.partial(pack_kernel, len(theirs), sides), out_shape, "pack", ids, mine, *theirs, partial, message, after=after,
        scratch_shapes=[pltpu.VMEM((rows, width), jnp.float32)],
    )


def add_kernel(ids, own, *refs):
    *messages, keep_ref, give_ref, give_too = refs
    height, half_way = keep_ref.shape[0], give_ref.shape[0]
    for core, first, out_ref in ((ids[2], 0, keep_ref), (1 - ids[2], 0, give_ref), (1 - ids[2], half_way, give_too)):
        at = pl.ds(pl.multiple_of(core * height + first, half_way), out_ref.shape[0])
        total = own[at, :]
        for message in messages:
            total += decode(message[at, :], scale_of(message, own.shape[0], 0))
        out_ref[...] = total


def add(ids, arrays, after):
    rows, width = arrays[0].shape
    out_shape = [jax.ShapeDtypeStruct((rows // parts, width), jnp.float32) for parts in (2, 4, 4)]
    return local(add_kernel, out_shape, "add", ids, *arrays, after=after)


def finish_kernel(ids, mine, other, other_too, own, *refs):
    *messages, out_ref = refs
    height, width = own.shape
    half_way = other.shape[0]
    for first, ref in ((0, other), (half_way, other_too)):
        at = pl.ds(first, half_way)
        out_ref[at, pl.ds(0, width)] = mine[at, :] + ref[...]
    total = own[...]
    for message in messages:
        total += decode(message[pl.ds(0, height), :], scale_of(message, height, 0))
    out_ref[:, pl.ds(width, width)] = total


def finish(ids, mine, others, arrays):
    height, width = mine.shape
    out_shape = jax.ShapeDtypeStruct((height, 2 * width), jnp.float32)
    return local(finish_kernel, out_shape, "finish", ids, mine, *others, *arrays)


def shards(trailing, panel_vectors):
    rows_here, cols_here = trailing.shape
    piece = panel_vectors.shape[0]
    count = lax.axis_size("row")
    devices_along = lax.axis_size("col")
    chips = devices_along // 2
    bits = count.bit_length() - 1
    row, col = lax.axis_index("row"), lax.axis_index("col")
    chip, core = col // 2, col % 2

    def at(row, chip, core):
        return (row * chips + chip) * 2 + core

    def turned(place, core):
        if core == 0:
            return place
        return sum(((place >> b) & 1) << (bits - 1 - b) for b in range(bits))

    def send(x, pairs):
        return lax.ppermute(x, ("row", "col"), [(at(*s), at(*d)) for s, d in pairs])

    offset = row ^ chip
    reverse = sum(((offset >> b) & 1) << (bits - 1 - b) for b in range(bits))
    place = jnp.where(core == 0, offset, reverse)
    ids = jnp.stack([row, chip, core, row * rows_here - col * cols_here, place]).astype(jnp.int32)

    def needed(chip, core, place, bit):
        rest = range(0, count, 2 ** (bit + 1))
        return any(chip ^ turned(place | r, core) > chip for r in rest)

    everyone = [(k, c) for k in range(chips) for c in range(2)]

    active = [(r, k, c) for r in range(count) for k in range(r + 1) for c in range(2)]

    def spread(place, source):
        bit = place.bit_length() - 1
        before = place - (1 << bit)
        pairs = [
            ((k ^ turned(before, c), k, c), (k ^ turned(place, c), k, c))
            for k, c in everyone
            if needed(k, c, place, bit)
        ]
        return send(source, pairs)

    def collect(bit, message):
        pairs = [
            ((k ^ turned(p, c), k, c), (k ^ turned(p - (1 << bit), c), k, c))
            for k, c in everyone
            for p in range(1 << bit, 2 << bit)
            if needed(k, c, p, bit)
        ]
        return send(message, pairs)

    matrix, diagonal = load(ids, trailing)

    line_of = [(r, k, c) for r in range(count) for k in range(chips) for c in range(2)]

    def step(x, to, wanted):
        return send(x, [((r, k, c), (r, to(k), c)) for r, k, c in line_of if wanted(r, k)])

    def by_distance(block):
        came, places = [block], [lambda chip: (chip, chip >= 0)]
        for by in range(1, chips):
            came.append(step(block, lambda k: (k + by) % chips, lambda r, k: (k + by) % chips <= r))
            places.append(lambda chip, by=by: (lax.rem(chip + chips - by, chips), chip >= 0))
        return came, places

    four = [
        lambda chip: (chip, chip >= 0),
        lambda chip: (chip ^ 2, chip >= 0),
        lambda chip: (jnp.maximum(chip - 1, 0), chip > 0),
        lambda chip: (jnp.minimum(chip + 1, 3), chip < 3),
        lambda chip: (3 - chip, (chip == 0) | (chip == 3)),
    ]

    def two_away(block):
        return step(block, lambda k: k ^ 2, lambda r, k: k >= 2 or k + 2 <= r)

    def next_ones(block):
        up = step(block, lambda k: k + 1, lambda r, k: k + 1 <= r and k < 3)
        return [up, step(block, lambda k: k - 1, lambda r, k: 0 <= k - 1 <= r)]

    def ends(two):
        return step(two, lambda k: 3 * (k - 1), lambda r, k: k == 1 or (k == 2 and r == 3))

    swap = [((r, k, c), (r, k, 1 - c)) for r, k, c in active]

    def widen(panels, after):
        panels[0], panels[1], *_ = lax.optimization_barrier((panels[0], panels[1], *after))
        for place in range(2, count):
            panels.append(spread(place, panels[place - (1 << (place.bit_length() - 1))]))

    def relaying(partial, came, panels, after):
        for bit in reversed(range(bits - 1)):
            partial, message = relay(ids, partial, came, after)
            if panels:
                message, *panels[2:] = lax.optimization_barrier((message, *panels[2:]))
            came = collect(bit, message)
        return partial, came, message

    def deliver(keep, got, partial, came, rounds, after):
        sides = chips // 2
        own, *out = pack(ids, keep, got, partial, came, rounds, sides, after)
        arrays = [own]
        for step, x in enumerate(out):
            pairs = []
            for r, k, c in active:
                at = (k + step) % rounds
                to = (c * sides + at // 2, at % 2) if rounds > sides else (c * sides + at, k // sides)
                if to != (k, c):
                    pairs.append(((r, k, c), (r, *to)))
            arrays.append(send(x, pairs))
        return arrays

    all_swap = [((r, k, c), (r, k, 1 - c)) for r, k, c in line_of]

    if chips == 4:
        two = two_away(panel_vectors)
        came, places = [panel_vectors, two, *next_ones(panel_vectors)], four
        two, matrix = lax.optimization_barrier((two, matrix))
        came.append(ends(two))
    else:
        came, places = by_distance(panel_vectors)
    mine_a, mine_b = line(ids, came, places, [])
    other_a, other_b = send(mine_a, swap), send(mine_b, swap)
    panels_a, panels_b = [half(ids, mine_a, other_a, piece)], [half(ids, mine_b, other_b, piece)]
    panels_a.append(spread(1, panels_a[0]))
    panels_b.append(spread(1, panels_b[0]))
    partial_a, message_a = mirrored_product(ids, matrix, diagonal, mine_a, other_a, piece, [])
    to_a = collect(bits - 1, message_a)
    partial_b, message_b = mirrored_product(ids, matrix, diagonal, mine_b, other_b, piece, [message_a])
    to_b = collect(bits - 1, message_b)
    widen(panels_a, [message_b])
    widen(panels_b, [panels_a[1]])
    partial_a, to_a, relayed = relaying(partial_a, to_a, [], [message_b, panels_b[1]])
    keep_a, *give_a = direct_product(ids, matrix, panels_a, [relayed])
    got_a = [send(x, swap) for x in give_a]
    partial_b, to_b, relayed = relaying(partial_b, to_b, [], [keep_a, to_a, panels_b[2]])
    arrays_a = deliver(keep_a, got_a, partial_a, to_a, chips // 2, [relayed, *panels_b[3:]])
    *give_b, panel_b = give_product(ids, matrix, panels_b, [arrays_a[0]])
    got_b = [send(x, swap) for x in give_b]
    keep_b = keep_product(ids, matrix, panel_b, [to_b])
    arrays_b = deliver(keep_b, got_b, partial_b, to_b, chips, [])
    mine_sum, *gives = add(ids, arrays_a, [arrays_b[1]])
    return finish(ids, mine_sum, [send(x, all_swap) for x in gives], arrays_b)


def solution(mesh):
    in_specs = (P("row", "col"), P(("row", "col"), None))
    out_specs = P(("row", "col"), None)
    return jax.shard_map(shards, mesh=mesh, in_specs=in_specs, out_specs=out_specs, check_vma=False)
```
